128 devices in a mesh: tile: 64 (over y, x, z_lo, core), mem: 2 (over z_hi).
Axes of the slice: x: 4, y: 4, z: 4 (z_hi: 2, z_lo: 2; z = z_hi * 2 + z_lo), core: 2. Of those that a mesh axis runs over, the one named last changes fastest.
Arguments:
- fields: float32 [52, 4, 512, 640], P('mem', None, 'tile'), may hold values from 0 to 150, as said below
- scaling: float32 [52, 4, 512, 640], P('mem', None, 'tile'), may hold values from 0.5 to 2, as said below
- counts: int32 [52], P('mem'), may hold values from 1 to 8
- land_mask: int32 [512, 640], P('tile'), may hold values 0 or 1
Outputs:
- barycenter: float32 [4, 512, 640], P(None, 'tile')
- updated: float32 [52, 4, 512, 640], P('mem', None, 'tile')
The draws below stay inside these ranges and needn't reach their ends.
Inputs may be any that keep to these rules, and one draw needn't show every extreme that they name: `fields`: positive cloud-water amounts. Positive scaling fields.
All inputs are finite; a program needn't handle non-finite values. No bound on the sum of `land_mask` on one device may be relied on, other than what follows from the above.
Results may differ from the reference program's by a relative error of at most 0.0028.
Values sent between devices are 32-bit elements; how exact they have to be, the bound alone decides.
No kernel may reach another device: no remote copies, remote signals or barrier semaphores. Data moves between devices by JAX's collectives and lax.ppermute only.
A program may use at most 128 MiB of HBM per device.

```python
import math
import jax
import jax.numpy as jnp
from jax import lax

MEM_DEV = 26
LEV = 4
LON_DEV = 8
LAT = 640
MEMBERS = 52
LON = 512


def draw_fields(key, part):
    key = jax.random.fold_in(key, 11)
    key_cells, key_rows, key_columns = jax.random.split(key, 3)
    shape = (MEMBERS, LEV, LON, LAT)
    longitude = jnp.arange(LON).astype(jnp.float32)
    rising = 1.0 + 2.0 * longitude / max(LON - 1, 1)
    row_scale = jnp.exp(jax.random.uniform(key_rows, (LAT,), jnp.float32, 0.0, math.log(10.0)))
    column_scale = jnp.exp(jax.random.uniform(key_columns, (LON,), jnp.float32, 0.0, math.log(3.0)))
    baseline = jnp.exp(jax.random.uniform(key_cells, shape, jnp.float32, math.log(0.01), 0.0))
    return baseline * (rising * column_scale)[:, None] * row_scale


def draw_scaling(key, part):
    key = jax.random.fold_in(key, 23)
    key_shift, key_own, key_common, key_bits = jax.random.split(key, 4)
    strips = LON // LON_DEV
    halves = MEMBERS // MEM_DEV
    shift = jax.random.uniform(key_shift, (halves, LEV, strips), jnp.float32, -0.55, 0.55)
    shift_cells = jnp.repeat(jnp.repeat(shift, MEM_DEV, axis=0), LON_DEV, axis=2)[..., None]
    own_noise = jax.random.uniform(key_own, (MEMBERS, LEV, LON, LAT), jnp.float32, -0.55, 0.55)
    common_noise = jax.random.uniform(key_common, (halves, LEV, LON, LAT), jnp.float32, -0.55, 0.55)
    common_noise = jnp.repeat(common_noise, MEM_DEV, axis=0)
    strip_bits = jax.random.randint(key_bits, (strips,), 0, 2)
    shared_cells = (jnp.repeat(strip_bits, LON_DEV) == 1)[:, None]
    noise = jnp.where(shared_cells, common_noise, own_noise)
    return jnp.clip(jnp.exp(shift_cells + noise), 0.5, 2.0)


def set_ends(entries, own_key, least, high):
    extent = entries.shape
    index_at = [jax.random.randint(jax.random.fold_in(own_key, axis), (), 0, extent[axis]) for axis in range(len(extent))]
    entries = entries.at[tuple(index_at)].set(least)
    longest = extent.index(max(extent))
    index_at[longest] = (index_at[longest] + 1) % extent[longest]
    return entries.at[tuple(index_at)].set(high)


def setup_inputs(seed: int = 0) -> dict:
    splits = jax.random.split(jax.random.key(seed), 5)
    return {
        "fields": draw_fields(jax.random.fold_in(splits[4], 71), 0),
        "scaling": draw_scaling(jax.random.fold_in(splits[4], 71), 0),
        "counts": set_ends(jax.random.randint(splits[2], (MEMBERS,), 1, 9), jax.random.fold_in(splits[2], 1), 1, 8).astype(jnp.int32),
        "land_mask": set_ends((jax.random.randint(splits[3], (LON, LAT), 0, 4) < 3).astype(jnp.int32), jax.random.fold_in(splits[3], 1), 0, 1),
    }


BACKGROUND = 0.01


def coefficients(lat_cells):
    row_index = jnp.arange(lat_cells).astype(jnp.int32)
    spacing = math.pi / lat_cells
    latitude = -0.5 * math.pi + (row_index.astype(jnp.float32) + 0.5) * spacing
    cell_area = jnp.cos(latitude)
    zonal_coef = 0.2 * jnp.minimum(2.2, 1.0 / (cell_area * cell_area))
    north_coef = jnp.where(row_index == lat_cells - 1, 0.0, 0.05 * jnp.cos(latitude + 0.5 * spacing) / cell_area)
    south_coef = jnp.where(row_index == 0, 0.0, 0.05 * jnp.cos(latitude - 0.5 * spacing) / cell_area)
    return cell_area, zonal_coef, north_coef, south_coef


def diffuse_step(values, coefs):
    cell_area, zonal_coef, north_coef, south_coef = coefs
    eastern = jnp.roll(values, -1, axis=1)
    western = jnp.roll(values, 1, axis=1)
    zeros_row = jnp.zeros_like(values[..., :1])
    northern = jnp.concatenate([values[..., 1:], zeros_row], axis=-1)
    southern = jnp.concatenate([zeros_row, values[..., :-1]], axis=-1)
    return (values + zonal_coef * (eastern + western - 2.0 * values)
            + north_coef * (northern - values) + south_coef * (southern - values))


def kernel(values, coefs):
    for repeat in range(4):
        values = diffuse_step(values, coefs)
    return values


def reference(fields, scaling, counts, land_mask):
    lat_cells = fields.shape[3]
    cell_count = fields.shape[2] * lat_cells
    coefs = coefficients(lat_cells)
    cell_area = coefs[0]
    weights = counts.astype(jnp.float32)

    def member_return(member_field, member_scaling):
        filled = jnp.where(land_mask[None] == 1, member_field, 0.0) + BACKGROUND
        masses = jnp.sum(filled * cell_area, axis=(1, 2)) / cell_count
        density = filled / masses[:, None, None]
        smoothed = kernel(cell_area * member_scaling, coefs)
        return member_scaling * kernel(cell_area * density / smoothed, coefs)

    def accumulate(carry, inputs):
        member_field, member_scaling, weight = inputs
        returned = member_return(member_field, member_scaling)
        return carry + weight * jnp.log(returned), None

    start = jnp.zeros(fields.shape[1:], jnp.float32)
    log_sum, unused = lax.scan(accumulate, start, (fields, scaling, weights))
    merged = jnp.exp(log_sum / jnp.sum(weights))
    level_mass = jnp.sum(merged * cell_area, axis=(1, 2)) / cell_count
    barycenter = merged / level_mass[:, None, None]

    def member_update(inputs):
        member_field, member_scaling = inputs
        return member_scaling * barycenter / member_return(member_field, member_scaling)

    updated = lax.map(member_update, (fields, scaling))
    return barycenter, updated
```

```python
import math

import jax
import jax.numpy as jnp
import numpy as np
from jax import lax
from jax.experimental import pallas as pl
from jax.experimental.pallas import tpu as pltpu
from jax.sharding import PartitionSpec as P

BACKGROUND = 0.01
REACH = 4
SUB = 8
VMEM = pl.BlockSpec(memory_space=pltpu.VMEM)
HBM = pl.BlockSpec(memory_space=pl.ANY)
AREA, ZONAL, NORTH, SOUTH, CENTER = range(5)


def coefficients(lat_cells):
    spacing = math.pi / lat_cells
    index = np.arange(lat_cells)
    latitude = -0.5 * math.pi + (index + 0.5) * spacing
    cell_area = np.cos(latitude)
    zonal = 0.2 * np.minimum(2.2, 1.0 / cell_area**2)
    north = np.where(index == lat_cells - 1, 0.0, 0.05 * np.cos(latitude + 0.5 * spacing) / cell_area)
    south = np.where(index == 0, 0.0, 0.05 * np.cos(latitude - 0.5 * spacing) / cell_area)
    center = 1.0 - 2.0 * zonal - north - south
    rows = np.stack([cell_area, zonal, north, south, center]).astype(np.float32)
    return np.ascontiguousarray(np.broadcast_to(rows[:, None, :], (5, SUB, lat_cells)))


def params(mib=20):
    return pltpu.CompilerParams(vmem_limit_bytes=mib * 2**20)


def rows_of(group):
    return pl.ds(pl.multiple_of(group * SUB, SUB), SUB)


def block_of(group):
    return pl.ds(pl.multiple_of(group * SUB * SUB, SUB * SUB), SUB * SUB)


def by_longitude(block, lat):
    return jnp.swapaxes(block.reshape(SUB, SUB, lat), 0, 1)


def diffuse(columns, coef_ref):
    lat = columns[0].shape[-1]
    for _ in range(REACH):
        columns = [
            coef_ref[CENTER] * here
            + coef_ref[ZONAL] * (west + east)
            + coef_ref[NORTH] * pltpu.roll(here, lat - 1, 1)
            + coef_ref[SOUTH] * pltpu.roll(here, 1, 1)
            for west, here, east in zip(columns[:-2], columns[1:-1], columns[2:])
        ]
    return columns


def gather_columns(refs, group):
    rows = rows_of(group)
    return [ref[c, rows, :] for ref in refs for c in range(REACH)]


def spread_kernel(scaling_ref, coef_ref, left_ref, right_ref):
    groups = left_ref.shape[1] // SUB
    lat = left_ref.shape[2]

    def step(group, carry):
        columns = by_longitude(scaling_ref[block_of(group), :], lat)
        for c in range(REACH):
            left_ref[c, rows_of(group), :] = columns[c] * coef_ref[AREA]
            right_ref[c, rows_of(group), :] = columns[c + REACH] * coef_ref[AREA]
        return carry

    lax.fori_loop(0, groups, step, 0)


def lane_fold(value):
    lat = value.shape[-1]
    total = value[:, :128]
    for t in range(1, lat // 128):
        total = total + value[:, t * 128 : (t + 1) * 128]
    return total


def smooth_kernel(west_ref, left_ref, right_ref, east_ref, fields_ref, mask_ref, coef_ref, outl_ref, outr_ref, mass_ref):
    groups = left_ref.shape[1] // SUB
    lat = left_ref.shape[2]

    def step(group, carry):
        smoothed = diffuse(gather_columns((west_ref, left_ref, right_ref, east_ref), group), coef_ref)
        fields = by_longitude(fields_ref[block_of(group), :], lat)
        mass = jnp.zeros((SUB, lat), jnp.float32)
        for c in range(2 * REACH):
            valid = jnp.broadcast_to(mask_ref[c : c + 1, :], (SUB, lat)) == 1
            filled = (jnp.where(valid, fields[c], 0.0) + BACKGROUND) * coef_ref[AREA]
            mass = mass + filled
            out_ref = outl_ref if c < REACH else outr_ref
            out_ref[c % REACH, rows_of(group), :] = filled / smoothed[c]
        mass_ref[rows_of(group), :] = lane_fold(mass)
        return carry

    lax.fori_loop(0, groups, step, 0)


def low_half(shape):
    return lax.broadcasted_iota(jnp.int32, shape, 0) < SUB // 2


def return_kernel(west_ref, left_ref, right_ref, east_ref, scaling_ref, weight_ref, coef_ref, result_ref, logs_ref, total_ref):
    groups = left_ref.shape[1] // SUB
    lat = left_ref.shape[2]
    total_ref[...] = jnp.zeros_like(total_ref)

    def step(group, carry):
        result = diffuse(gather_columns((west_ref, left_ref, right_ref, east_ref), group), coef_ref)
        scaling = by_longitude(scaling_ref[block_of(group), :], lat)
        weight = jnp.broadcast_to(weight_ref[rows_of(group), :1], (SUB, lat))
        for c in range(2 * REACH):
            result_ref[c, rows_of(group), :] = result[c]
            total_ref[c] = total_ref[c] + weight * jnp.log(scaling[c] * result[c])
        return carry

    lax.fori_loop(0, groups, step, 0)
    low = low_half((SUB, lat))
    for c in range(REACH):
        first, second = total_ref[c], total_ref[c + REACH]
        first = first + pltpu.roll(first, SUB // 2, 0)
        second = second + pltpu.roll(second, SUB // 2, 0)
        logs_ref[c] = jnp.where(low, first, second)


def merge_kernel(own_ref, other_ref, count_ref, mass_ref, coef_ref, merged_ref, payload_ref):
    members = mass_ref.shape[0]
    lat = own_ref.shape[2]
    scale = 1.0 / count_ref[...]
    scale = jnp.broadcast_to(scale[:, :1], (SUB, lat))
    level = jnp.zeros((SUB, lat), jnp.float32)
    for c in range(REACH):
        merged = jnp.exp((own_ref[c] + other_ref[c]) * scale)
        merged_ref[c] = merged
        level = level + merged * coef_ref[AREA]
    level = lane_fold(level)
    level = level + pltpu.roll(level, SUB // 2, 0)
    spare = jnp.zeros((128 - members - SUB, 128), jnp.float32)
    table = jnp.concatenate([mass_ref[...], level, spare], axis=0)
    row = jnp.sum(table.T, axis=0, keepdims=True)
    payload_ref[...] = jnp.broadcast_to(row[None], payload_ref.shape)


def finish_kernel(cells, got_ref, merged_ref, result_ref, bary_ref, updated_ref, staged_ref, sem):
    members, lat = result_ref.shape[1:]
    groups = members // SUB
    total = jnp.sum(got_ref[...], axis=0)
    table = jnp.broadcast_to(total, (128, 128)).T
    level = table[members : members + SUB, :]
    low = low_half((SUB, lat))
    wide = lambda v: jnp.concatenate([v] * (lat // 128), axis=1)
    merged = [None] * (2 * REACH)
    for c in range(REACH):
        both = merged_ref[c]
        swapped = pltpu.roll(both, SUB // 2, 0)
        merged[c] = jnp.where(low, both, swapped)
        merged[c + REACH] = jnp.where(low, swapped, both)
    inverse = wide(cells / level)
    bary = [m * inverse for m in merged]
    bary_ref[...] = jnp.swapaxes(jnp.stack(bary), 0, 1)[: SUB // 2]
    for group in range(groups):
        rows = slice(group * SUB, (group + 1) * SUB)
        factor = wide(table[rows, :] / cells)
        out = jnp.stack([bary[c] * factor / result_ref[c, rows, :] for c in range(2 * REACH)])
        span = pl.ds(group * SUB * SUB, SUB * SUB)
        staged_ref[span, :] = jnp.swapaxes(out, 0, 1).reshape(SUB * SUB, lat)
        pltpu.make_async_copy(staged_ref.at[span, :], updated_ref.at[span, :], sem.at[group]).start()
    for group in range(groups):
        span = pl.ds(group * SUB * SUB, SUB * SUB)
        pltpu.make_async_copy(staged_ref.at[span, :], updated_ref.at[span, :], sem.at[group]).wait()


def shape(*dims):
    return jax.ShapeDtypeStruct(dims, jnp.float32)


def body(fields, scaling, counts, land_mask):
    members, levels, lon, lat = fields.shape
    tiles = lax.axis_size("tile")
    rows = members * levels
    cells = lon * tiles * lat
    half = shape(REACH, rows, lat)
    coef = jnp.asarray(coefficients(lat))
    eastward = [(i, (i + 1) % tiles) for i in range(tiles)]
    westward = [((i + 1) % tiles, i) for i in range(tiles)]
    scaling = scaling.reshape(rows * lon, lat)
    fields = fields.reshape(rows * lon, lat)
    weights = counts.astype(jnp.float32)
    weight_rows = jnp.broadcast_to(jnp.repeat(weights, levels)[:, None], (rows, 128))
    count = jnp.broadcast_to(jnp.sum(weights), (SUB, 128))
    count = count + lax.ppermute(count, "mem", [(0, 1), (1, 0)])

    left, right = pl.pallas_call(
        spread_kernel, out_shape=(half, half), in_specs=[VMEM] * 2, out_specs=(VMEM,) * 2, compiler_params=params()
    )(scaling, coef)
    west = lax.ppermute(right, "tile", eastward)
    east = lax.ppermute(left, "tile", westward)
    left, right, mass = pl.pallas_call(
        smooth_kernel,
        out_shape=(half, half, shape(rows, 128)),
        in_specs=[VMEM] * 7,
        out_specs=(VMEM,) * 3,
        compiler_params=params(),
    )(west, left, right, east, fields, land_mask, coef)
    west = lax.ppermute(right, "tile", eastward)
    east = lax.ppermute(left, "tile", westward)
    result, logs = pl.pallas_call(
        return_kernel,
        out_shape=(shape(2 * REACH, rows, lat), shape(REACH, SUB, lat)),
        in_specs=[VMEM] * 7,
        out_specs=(VMEM,) * 2,
        scratch_shapes=[pltpu.VMEM((2 * REACH, SUB, lat), jnp.float32)],
        compiler_params=params(),
    )(west, left, right, east, scaling, weight_rows, coef)
    other = lax.ppermute(logs, "mem", [(0, 1), (1, 0)])
    merged, payload = pl.pallas_call(
        merge_kernel,
        out_shape=(shape(REACH, SUB, lat), shape(tiles, 1, 128)),
        in_specs=[VMEM] * 5,
        out_specs=(VMEM,) * 2,
        compiler_params=params(),
    )(logs, other, count, mass, coef)
    got = lax.all_to_all(payload, "tile", split_axis=0, concat_axis=0)
    barycenter, updated = pl.pallas_call(
        lambda *refs: finish_kernel(float(cells), *refs),
        out_shape=(shape(levels, lon, lat), shape(rows * lon, lat)),
        in_specs=[VMEM] * 3,
        out_specs=(VMEM, HBM),
        scratch_shapes=[pltpu.VMEM((rows * lon, lat), jnp.float32), pltpu.SemaphoreType.DMA((rows // SUB,))],
        compiler_params=params(),
    )(got, merged, result)
    return barycenter, updated.reshape(members, levels, lon, lat)


def solution(mesh):
    return jax.shard_map(
        body,
        mesh=mesh,
        in_specs=(
            P("mem", None, "tile", None),
            P("mem", None, "tile", None),
            P("mem"),
            P("tile", None),
        ),
        out_specs=(P(None, "tile", None), P("mem", None, "tile", None)),
        check_vma=False,
    )
```

```python
import math

import jax
import jax.numpy as jnp
import numpy as np
from jax import lax
from jax.experimental import pallas as pl
from jax.experimental.pallas import tpu as pltpu
from jax.sharding import PartitionSpec as P

BACKGROUND = 0.01
REACH = 4
SUB = 8
VMEM = pl.BlockSpec(memory_space=pltpu.VMEM)
HBM = pl.BlockSpec(memory_space=pl.ANY)
AREA, ZONAL, NORTH, SOUTH, CENTER = range(5)


def coefficients(lat_cells):
    spacing = math.pi / lat_cells
    index = np.arange(lat_cells)
    latitude = -0.5 * math.pi + (index + 0.5) * spacing
    cell_area = np.cos(latitude)
    zonal = 0.2 * np.minimum(2.2, 1.0 / cell_area**2)
    north = np.where(index == lat_cells - 1, 0.0, 0.05 * np.cos(latitude + 0.5 * spacing) / cell_area)
    south = np.where(index == 0, 0.0, 0.05 * np.cos(latitude - 0.5 * spacing) / cell_area)
    center = 1.0 - 2.0 * zonal - north - south
    rows = np.stack([cell_area, zonal, north, south, center]).astype(np.float32)
    return np.ascontiguousarray(np.broadcast_to(rows[:, None, :], (5, SUB, lat_cells)))


def params(mib=20):
    return pltpu.CompilerParams(vmem_limit_bytes=mib * 2**20)


def rows_of(group):
    return pl.ds(pl.multiple_of(group * SUB, SUB), SUB)


def block_of(group):
    return pl.ds(pl.multiple_of(group * SUB * SUB, SUB * SUB), SUB * SUB)


def by_longitude(block, lat):
    return jnp.swapaxes(block.reshape(SUB, SUB, lat), 0, 1)


def stack_of(ref, group, order=range(REACH)):
    return [ref[c, rows_of(group), :] for c in order]


def odd_core():
    return lax.rem(lax.axis_index("tile"), 2) == 1


def from_outside(columns, odd):
    last = len(columns) - 1
    return [jnp.where(odd, columns[last - c], columns[c]) for c in range(len(columns))]


def spread_kernel(scaling_ref, coef_ref, outer_ref, inner_ref):
    groups, lat = outer_ref.shape[1] // SUB, outer_ref.shape[2]
    odd = odd_core()

    def step(group, carry):
        columns = from_outside(by_longitude(scaling_ref[block_of(group), :], lat), odd)
        for c in range(REACH):
            outer_ref[c, rows_of(group), :] = columns[c] * coef_ref[AREA]
            inner_ref[c, rows_of(group), :] = columns[c + REACH] * coef_ref[AREA]
        return carry

    lax.fori_loop(0, groups, step, 0)


def lane_fold(value):
    lat = value.shape[-1]
    total = value[:, :128]
    for t in range(1, lat // 128):
        total = total + value[:, t * 128 : (t + 1) * 128]
    return total


def diffuse(columns, coef_ref):
    lat = columns[0].shape[-1]
    return [
        coef_ref[CENTER] * here
        + coef_ref[ZONAL] * (west + east)
        + coef_ref[NORTH] * pltpu.roll(here, lat - 1, 1)
        + coef_ref[SOUTH] * pltpu.roll(here, 1, 1)
        for west, here, east in zip(columns[:-2], columns[1:-1], columns[2:])
    ]


def inner_half(group, halo_ref, outer_ref, inner_ref, coef_ref, edge_ref):
    columns = stack_of(outer_ref, group) + stack_of(inner_ref, group) + stack_of(halo_ref, group, (3, 2, 1, 0))
    for s in range(REACH):
        columns = diffuse(columns, coef_ref)
        if s < REACH - 1:
            edge_ref[2 * s, rows_of(group), :] = columns[0]
            edge_ref[2 * s + 1, rows_of(group), :] = columns[1]
    return columns


def outer_half(group, halo_ref, outer_ref, edge_ref, coef_ref):
    columns = stack_of(halo_ref, group, (3, 2, 1, 0)) + stack_of(outer_ref, group, (0, 1))
    for s in range(REACH):
        columns = diffuse(columns, coef_ref)
        if s < REACH - 1:
            columns = columns + stack_of(edge_ref, group, (2 * s, 2 * s + 1))
    return columns


def smooth_inner_kernel(
    halo_ref, outer_ref, inner_ref, fields_ref, mask_ref, coef_ref, out_ref, edge_ref, filled_ref, mass_ref
):
    groups, lat = outer_ref.shape[1] // SUB, outer_ref.shape[2]
    odd = odd_core()

    def step(group, carry):
        smoothed = inner_half(group, halo_ref, outer_ref, inner_ref, coef_ref, edge_ref)
        fields = by_longitude(fields_ref[block_of(group), :], lat)
        filled = []
        for c in range(2 * REACH):
            valid = jnp.broadcast_to(mask_ref[c : c + 1, :], (SUB, lat)) == 1
            filled.append((jnp.where(valid, fields[c], 0.0) + BACKGROUND) * coef_ref[AREA])
        mass_ref[rows_of(group), :] = lane_fold(sum(filled))
        filled = from_outside(filled, odd)
        for c in range(REACH):
            filled_ref[c, rows_of(group), :] = filled[c]
            out_ref[c, rows_of(group), :] = filled[c + REACH] / smoothed[c]
        return carry

    lax.fori_loop(0, groups, step, 0)


def smooth_outer_kernel(halo_ref, outer_ref, edge_ref, filled_ref, coef_ref, out_ref):
    groups = outer_ref.shape[1] // SUB

    def step(group, carry):
        smoothed = outer_half(group, halo_ref, outer_ref, edge_ref, coef_ref)
        for c in range(REACH):
            out_ref[c, rows_of(group), :] = filled_ref[c, rows_of(group), :] / smoothed[c]
        return carry

    lax.fori_loop(0, groups, step, 0)


def low_half(shape):
    return lax.broadcasted_iota(jnp.int32, shape, 0) < SUB // 2


def add_logs(group, result, scaled_ref, weight_ref, inverse_ref, total_ref):
    lat = scaled_ref.shape[2]
    weight = jnp.broadcast_to(weight_ref[rows_of(group), :1], (SUB, lat))
    for c in range(REACH):
        inverse_ref[c, rows_of(group), :] = 1.0 / result[c]
        total_ref[c] = total_ref[c] + weight * jnp.log(scaled_ref[c, rows_of(group), :] * result[c])


def return_inner_kernel(
    halo_ref, outer_ref, inner_ref, scaled_ref, weight_ref, coef_ref, inverse_ref, edge_ref, total_ref
):
    groups = outer_ref.shape[1] // SUB
    total_ref[...] = jnp.zeros_like(total_ref)

    def step(group, carry):
        result = inner_half(group, halo_ref, outer_ref, inner_ref, coef_ref, edge_ref)
        add_logs(group, result, scaled_ref, weight_ref, inverse_ref, total_ref)
        return carry

    lax.fori_loop(0, groups, step, 0)


def return_outer_kernel(
    halo_ref, outer_ref, edge_ref, scaled_ref, weight_ref, inner_ref, coef_ref, inverse_ref, logs_ref, total_ref
):
    groups, lat = outer_ref.shape[1] // SUB, outer_ref.shape[2]
    total_ref[...] = jnp.zeros_like(total_ref)

    def step(group, carry):
        result = outer_half(group, halo_ref, outer_ref, edge_ref, coef_ref)
        add_logs(group, result, scaled_ref, weight_ref, inverse_ref, total_ref)
        return carry

    lax.fori_loop(0, groups, step, 0)
    low = low_half((SUB, lat))
    for c in range(REACH):
        outer, inner = total_ref[c], inner_ref[c]
        outer = outer + pltpu.roll(outer, SUB // 2, 0)
        inner = inner + pltpu.roll(inner, SUB // 2, 0)
        logs_ref[c] = jnp.where(low, outer, inner)


def merge_kernel(own_ref, other_ref, count_ref, mass_ref, coef_ref, merged_ref, payload_ref):
    members, lat = mass_ref.shape[0], own_ref.shape[2]
    scale = 1.0 / count_ref[...]
    scale = jnp.broadcast_to(scale[:, :1], (SUB, lat))
    level = jnp.zeros((SUB, lat), jnp.float32)
    for c in range(REACH):
        weighted = jnp.exp((own_ref[c] + other_ref[c]) * scale)
        merged_ref[c] = weighted / coef_ref[AREA]
        level = level + weighted
    level = lane_fold(level)
    level = level + pltpu.roll(level, SUB // 2, 0)
    spare = jnp.zeros((128 - members - SUB, 128), jnp.float32)
    table = jnp.concatenate([mass_ref[...], level, spare], axis=0)
    row = jnp.sum(table.T, axis=0, keepdims=True)
    payload_ref[...] = jnp.broadcast_to(row[None], payload_ref.shape)


def finish_kernel(cells, got_ref, merged_ref, outer_ref, inner_ref, bary_ref, updated_ref, staged_ref, sem):
    members, lat = outer_ref.shape[1:]
    groups = members // SUB
    odd = odd_core()
    total = jnp.sum(got_ref[...], axis=0)
    table = jnp.broadcast_to(total, (128, 128)).T
    level = table[members : members + SUB, :]
    low = low_half((SUB, lat))
    wide = lambda v: jnp.concatenate([v] * (lat // 128), axis=1)
    inverse = wide(cells / level)
    outer, inner = [], []
    for c in range(REACH):
        both = merged_ref[c] * inverse
        swapped = pltpu.roll(both, SUB // 2, 0)
        outer.append(jnp.where(low, both, swapped))
        inner.append(jnp.where(low, swapped, both))
    bary = from_outside(outer + inner, odd)
    bary_ref[...] = jnp.swapaxes(jnp.stack(bary), 0, 1)[: SUB // 2]
    for group in range(groups):
        rows = slice(group * SUB, (group + 1) * SUB)
        factor = wide(table[rows, :] / cells)
        quotients = [ref[c, rows, :] for ref in (outer_ref, inner_ref) for c in range(REACH)]
        out = [b * factor * quotient for b, quotient in zip(bary, from_outside(quotients, odd))]
        span = pl.ds(group * SUB * SUB, SUB * SUB)
        staged_ref[span, :] = jnp.swapaxes(jnp.stack(out), 0, 1).reshape(SUB * SUB, lat)
        pltpu.make_async_copy(staged_ref.at[span, :], updated_ref.at[span, :], sem.at[group]).start()
    for group in range(groups):
        span = pl.ds(group * SUB * SUB, SUB * SUB)
        pltpu.make_async_copy(staged_ref.at[span, :], updated_ref.at[span, :], sem.at[group]).wait()


def shape(*dims):
    return jax.ShapeDtypeStruct(dims, jnp.float32)


def call(kernel, outs, *args, scratch=(), out_specs=None):
    return pl.pallas_call(
        kernel,
        out_shape=outs,
        in_specs=[VMEM] * len(args),
        out_specs=out_specs or (VMEM,) * len(outs),
        scratch_shapes=scratch,
        compiler_params=params(),
    )(*args)


def body(fields, scaling, counts, land_mask):
    members, levels, lon, lat = fields.shape
    tiles = lax.axis_size("tile")
    rows = members * levels
    cells = lon * tiles * lat
    half = shape(REACH, rows, lat)
    edge = shape(2 * REACH - 2, rows, lat)
    packed = shape(REACH, SUB, lat)
    coef = jnp.asarray(coefficients(lat))
    with_mate = [(i, i ^ 1) for i in range(tiles)]
    with_neighbour = [(i, (i + (1 if i % 2 else -1)) % tiles) for i in range(tiles)]
    scaling = scaling.reshape(rows * lon, lat)
    fields = fields.reshape(rows * lon, lat)
    weights = counts.astype(jnp.float32)
    weight_rows = jnp.broadcast_to(jnp.repeat(weights, levels)[:, None], (rows, 128))
    count = jnp.broadcast_to(jnp.sum(weights), (SUB, 128))
    count = count + lax.ppermute(count, "mem", [(0, 1), (1, 0)])

    outer, inner = call(spread_kernel, (half, half), scaling, coef)
    inner_halo = lax.ppermute(inner, "tile", with_mate)
    outer_halo = lax.ppermute(outer, "tile", with_neighbour)
    v_inner, edges, filled, mass = call(
        smooth_inner_kernel, (half, edge, half, shape(rows, 128)), inner_halo, outer, inner, fields, land_mask, coef
    )
    v_inner_halo = lax.ppermute(v_inner, "tile", with_mate)
    (v_outer,) = call(smooth_outer_kernel, (half,), outer_halo, outer, edges, filled, coef)
    v_outer_halo = lax.ppermute(v_outer, "tile", with_neighbour)
    inverse_inner, edges, inner_logs = call(
        return_inner_kernel, (half, edge, packed), v_inner_halo, v_outer, v_inner, inner, weight_rows, coef
    )
    inverse_outer, logs = call(
        return_outer_kernel,
        (half, packed),
        v_outer_halo,
        v_outer,
        edges,
        outer,
        weight_rows,
        inner_logs,
        coef,
        scratch=[pltpu.VMEM((REACH, SUB, lat), jnp.float32)],
    )
    other = lax.ppermute(logs, "mem", [(0, 1), (1, 0)])
    merged, payload = call(merge_kernel, (packed, shape(tiles, 1, 128)), logs, other, count, mass, coef)
    got = lax.all_to_all(payload, "tile", split_axis=0, concat_axis=0)
    barycenter, updated = call(
        lambda *refs: finish_kernel(float(cells), *refs),
        (shape(levels, lon, lat), shape(rows * lon, lat)),
        got,
        merged,
        inverse_outer,
        inverse_inner,
        scratch=[pltpu.VMEM((rows * lon, lat), jnp.float32), pltpu.SemaphoreType.DMA((rows // SUB,))],
        out_specs=(VMEM, HBM),
    )
    return barycenter, updated.reshape(members, levels, lon, lat)


def solution(mesh):
    return jax.shard_map(
        body,
        mesh=mesh,
        in_specs=(
            P("mem", None, "tile", None),
            P("mem", None, "tile", None),
            P("mem"),
            P("tile", None),
        ),
        out_specs=(P(None, "tile", None), P("mem", None, "tile", None)),
        check_vma=False,
    )
```

```python
import math

import jax
import jax.numpy as jnp
import numpy as np
from jax import lax
from jax.experimental import pallas as pl
from jax.experimental.pallas import tpu as pltpu
from jax.sharding import PartitionSpec as P

BACKGROUND = 0.01
REACH = 4
SUB = 8
VMEM = pl.BlockSpec(memory_space=pltpu.VMEM)
HBM = pl.BlockSpec(memory_space=pl.ANY)
AREA, ZONAL, NORTH, SOUTH, CENTER = range(5)


def coefficients(lat_cells):
    spacing = math.pi / lat_cells
    index = np.arange(lat_cells)
    latitude = -0.5 * math.pi + (index + 0.5) * spacing
    cell_area = np.cos(latitude)
    zonal = 0.2 * np.minimum(2.2, 1.0 / cell_area**2)
    north = np.where(index == lat_cells - 1, 0.0, 0.05 * np.cos(latitude + 0.5 * spacing) / cell_area)
    south = np.where(index == 0, 0.0, 0.05 * np.cos(latitude - 0.5 * spacing) / cell_area)
    center = 1.0 - 2.0 * zonal - north - south
    rows = np.stack([cell_area, zonal, north, south, center]).astype(np.float32)
    return np.ascontiguousarray(np.broadcast_to(rows[:, None, :], (5, SUB, lat_cells)))


def params(mib=20):
    return pltpu.CompilerParams(vmem_limit_bytes=mib * 2**20)


def rows_of(group):
    return pl.ds(group * SUB, SUB)


def block_of(group):
    return pl.ds(group * SUB * SUB, SUB * SUB)


def batches(groups, size=4):
    return [range(first, min(first + size, groups)) for first in range(0, groups, size)]


def by_longitude(block, lat):
    return jnp.swapaxes(block.reshape(SUB, SUB, lat), 0, 1)


def stack_of(ref, group, order=range(REACH)):
    return [ref[c, rows_of(group), :] for c in order]


def odd_core():
    return lax.rem(lax.axis_index("tile"), 2) == 1


def from_outside(columns, odd):
    last = len(columns) - 1
    return [jnp.where(odd, columns[last - c], columns[c]) for c in range(len(columns))]


def spread_kernel(scaling_ref, coef_ref, outer_ref, inner_ref):
    groups, lat = outer_ref.shape[1] // SUB, outer_ref.shape[2]
    odd = odd_core()
    for group in range(groups):
        columns = from_outside(by_longitude(scaling_ref[block_of(group), :], lat), odd)
        for c in range(REACH):
            outer_ref[c, rows_of(group), :] = columns[c] * coef_ref[AREA]
            inner_ref[c, rows_of(group), :] = columns[c + REACH] * coef_ref[AREA]


def lane_fold(value):
    lat = value.shape[-1]
    total = value[:, :128]
    for t in range(1, lat // 128):
        total = total + value[:, t * 128 : (t + 1) * 128]
    return total


def diffuse(columns, coef_ref):
    lat = columns[0].shape[-1]
    return [
        coef_ref[CENTER] * here
        + coef_ref[ZONAL] * (west + east)
        + coef_ref[NORTH] * pltpu.roll(here, lat - 1, 1)
        + coef_ref[SOUTH] * pltpu.roll(here, 1, 1)
        for west, here, east in zip(columns[:-2], columns[1:-1], columns[2:])
    ]


def inner_half(batch, halo_ref, outer_ref, inner_ref, coef_ref, edge_ref):
    columns = [stack_of(outer_ref, g) + stack_of(inner_ref, g) + stack_of(halo_ref, g, (3, 2, 1, 0)) for g in batch]
    for s in range(REACH):
        columns = [diffuse(own, coef_ref) for own in columns]
        if s < REACH - 1:
            for own, group in zip(columns, batch):
                edge_ref[2 * s, rows_of(group), :] = own[0]
                edge_ref[2 * s + 1, rows_of(group), :] = own[1]
    return zip(batch, columns)


def outer_half(batch, halo_ref, outer_ref, edge_ref, coef_ref):
    columns = [stack_of(halo_ref, g, (3, 2, 1, 0)) + stack_of(outer_ref, g, (0, 1)) for g in batch]
    for s in range(REACH):
        columns = [diffuse(own, coef_ref) for own in columns]
        if s < REACH - 1:
            columns = [own + stack_of(edge_ref, g, (2 * s, 2 * s + 1)) for own, g in zip(columns, batch)]
    return zip(batch, columns)


def smooth_inner_kernel(
    halo_ref, outer_ref, inner_ref, fields_ref, mask_ref, coef_ref, out_ref, edge_ref, filled_ref, mass_ref
):
    groups, lat = outer_ref.shape[1] // SUB, outer_ref.shape[2]
    odd = odd_core()
    for batch in batches(groups):
        for group, smoothed in inner_half(batch, halo_ref, outer_ref, inner_ref, coef_ref, edge_ref):
            fields = by_longitude(fields_ref[block_of(group), :], lat)
            filled = []
            for c in range(2 * REACH):
                valid = jnp.broadcast_to(mask_ref[c : c + 1, :], (SUB, lat)) == 1
                filled.append((jnp.where(valid, fields[c], 0.0) + BACKGROUND) * coef_ref[AREA])
            mass_ref[rows_of(group), :] = lane_fold(sum(filled))
            filled = from_outside(filled, odd)
            for c in range(REACH):
                filled_ref[c, rows_of(group), :] = filled[c]
                out_ref[c, rows_of(group), :] = filled[c + REACH] / smoothed[c]


def smooth_outer_kernel(halo_ref, outer_ref, edge_ref, filled_ref, coef_ref, out_ref):
    groups = outer_ref.shape[1] // SUB
    for batch in batches(groups):
        for group, smoothed in outer_half(batch, halo_ref, outer_ref, edge_ref, coef_ref):
            for c in range(REACH):
                out_ref[c, rows_of(group), :] = filled_ref[c, rows_of(group), :] / smoothed[c]


def low_half(shape):
    return lax.broadcasted_iota(jnp.int32, shape, 0) < SUB // 2


def add_logs(group, result, scaled_ref, weight_ref, inverse_ref, total_ref):
    lat = scaled_ref.shape[2]
    weight = jnp.broadcast_to(weight_ref[rows_of(group), :1], (SUB, lat))
    for c in range(REACH):
        inverse_ref[c, rows_of(group), :] = 1.0 / result[c]
        total_ref[c] = total_ref[c] + weight * jnp.log(scaled_ref[c, rows_of(group), :] * result[c])


def return_inner_kernel(
    halo_ref, outer_ref, inner_ref, scaled_ref, weight_ref, coef_ref, inverse_ref, edge_ref, total_ref
):
    groups = outer_ref.shape[1] // SUB
    total_ref[...] = jnp.zeros_like(total_ref)
    for batch in batches(groups):
        for group, result in inner_half(batch, halo_ref, outer_ref, inner_ref, coef_ref, edge_ref):
            add_logs(group, result, scaled_ref, weight_ref, inverse_ref, total_ref)


def return_outer_kernel(
    halo_ref, outer_ref, edge_ref, scaled_ref, weight_ref, inner_ref, coef_ref, inverse_ref, logs_ref, total_ref
):
    groups, lat = outer_ref.shape[1] // SUB, outer_ref.shape[2]
    total_ref[...] = jnp.zeros_like(total_ref)
    for batch in batches(groups):
        for group, result in outer_half(batch, halo_ref, outer_ref, edge_ref, coef_ref):
            add_logs(group, result, scaled_ref, weight_ref, inverse_ref, total_ref)
    low = low_half((SUB, lat))
    for c in range(REACH):
        outer, inner = total_ref[c], inner_ref[c]
        outer = outer + pltpu.roll(outer, SUB // 2, 0)
        inner = inner + pltpu.roll(inner, SUB // 2, 0)
        logs_ref[c] = jnp.where(low, outer, inner)


def merge_kernel(own_ref, other_ref, count_ref, mass_ref, coef_ref, merged_ref, payload_ref):
    members, lat = mass_ref.shape[0], own_ref.shape[2]
    scale = 1.0 / count_ref[...]
    scale = jnp.broadcast_to(scale[:, :1], (SUB, lat))
    level = jnp.zeros((SUB, lat), jnp.float32)
    for c in range(REACH):
        weighted = jnp.exp((own_ref[c] + other_ref[c]) * scale)
        merged_ref[c] = weighted / coef_ref[AREA]
        level = level + weighted
    level = lane_fold(level)
    level = level + pltpu.roll(level, SUB // 2, 0)
    spare = jnp.zeros((128 - members - SUB, 128), jnp.float32)
    table = jnp.concatenate([mass_ref[...], level, spare], axis=0)
    row = jnp.sum(table.T, axis=0, keepdims=True)
    payload_ref[...] = jnp.broadcast_to(row[None], payload_ref.shape)


def finish_kernel(cells, got_ref, merged_ref, outer_ref, inner_ref, bary_ref, updated_ref, staged_ref, sem):
    members, lat = outer_ref.shape[1:]
    groups = members // SUB
    odd = odd_core()
    total = jnp.sum(got_ref[...], axis=0)
    table = jnp.broadcast_to(total, (128, 128)).T
    level = table[members : members + SUB, :]
    low = low_half((SUB, lat))
    wide = lambda v: jnp.concatenate([v] * (lat // 128), axis=1)
    inverse = wide(cells / level)
    outer, inner = [], []
    for c in range(REACH):
        both = merged_ref[c] * inverse
        swapped = pltpu.roll(both, SUB // 2, 0)
        outer.append(jnp.where(low, both, swapped))
        inner.append(jnp.where(low, swapped, both))
    bary = from_outside(outer + inner, odd)
    bary_ref[...] = jnp.swapaxes(jnp.stack(bary), 0, 1)[: SUB // 2]
    for group in range(groups):
        rows = slice(group * SUB, (group + 1) * SUB)
        factor = wide(table[rows, :] / cells)
        quotients = [ref[c, rows, :] for ref in (outer_ref, inner_ref) for c in range(REACH)]
        out = [b * factor * quotient for b, quotient in zip(bary, from_outside(quotients, odd))]
        span = pl.ds(group * SUB * SUB, SUB * SUB)
        staged_ref[span, :] = jnp.swapaxes(jnp.stack(out), 0, 1).reshape(SUB * SUB, lat)
        pltpu.make_async_copy(staged_ref.at[span, :], updated_ref.at[span, :], sem.at[group]).start()
    for group in range(groups):
        span = pl.ds(group * SUB * SUB, SUB * SUB)
        pltpu.make_async_copy(staged_ref.at[span, :], updated_ref.at[span, :], sem.at[group]).wait()


def shape(*dims):
    return jax.ShapeDtypeStruct(dims, jnp.float32)


def call(kernel, outs, *args, scratch=(), out_specs=None):
    return pl.pallas_call(
        kernel,
        out_shape=outs,
        in_specs=[VMEM] * len(args),
        out_specs=out_specs or (VMEM,) * len(outs),
        scratch_shapes=scratch,
        compiler_params=params(),
    )(*args)


def body(fields, scaling, counts, land_mask):
    members, levels, lon, lat = fields.shape
    tiles = lax.axis_size("tile")
    rows = members * levels
    cells = lon * tiles * lat
    half = shape(REACH, rows, lat)
    edge = shape(2 * REACH - 2, rows, lat)
    packed = shape(REACH, SUB, lat)
    coef = jnp.asarray(coefficients(lat))
    with_mate = [(i, i ^ 1) for i in range(tiles)]
    with_neighbour = [(i, (i + (1 if i % 2 else -1)) % tiles) for i in range(tiles)]
    scaling = scaling.reshape(rows * lon, lat)
    fields = fields.reshape(rows * lon, lat)
    weights = counts.astype(jnp.float32)
    weight_rows = jnp.broadcast_to(jnp.repeat(weights, levels)[:, None], (rows, 128))
    count = jnp.broadcast_to(jnp.sum(weights), (SUB, 128))
    count = count + lax.ppermute(count, "mem", [(0, 1), (1, 0)])

    outer, inner = call(spread_kernel, (half, half), scaling, coef)
    inner_halo = lax.ppermute(inner, "tile", with_mate)
    outer_halo = lax.ppermute(outer, "tile", with_neighbour)
    v_inner, edges, filled, mass = call(
        smooth_inner_kernel, (half, edge, half, shape(rows, 128)), inner_halo, outer, inner, fields, land_mask, coef
    )
    v_inner_halo = lax.ppermute(v_inner, "tile", with_mate)
    (v_outer,) = call(smooth_outer_kernel, (half,), outer_halo, outer, edges, filled, coef)
    v_outer_halo = lax.ppermute(v_outer, "tile", with_neighbour)
    inverse_inner, edges, inner_logs = call(
        return_inner_kernel, (half, edge, packed), v_inner_halo, v_outer, v_inner, inner, weight_rows, coef
    )
    inverse_outer, logs = call(
        return_outer_kernel,
        (half, packed),
        v_outer_halo,
        v_outer,
        edges,
        outer,
        weight_rows,
        inner_logs,
        coef,
        scratch=[pltpu.VMEM((REACH, SUB, lat), jnp.float32)],
    )
    other = lax.ppermute(logs, "mem", [(0, 1), (1, 0)])
    merged, payload = call(merge_kernel, (packed, shape(tiles, 1, 128)), logs, other, count, mass, coef)
    got = lax.all_to_all(payload, "tile", split_axis=0, concat_axis=0)
    barycenter, updated = call(
        lambda *refs: finish_kernel(float(cells), *refs),
        (shape(levels, lon, lat), shape(rows * lon, lat)),
        got,
        merged,
        inverse_outer,
        inverse_inner,
        scratch=[pltpu.VMEM((rows * lon, lat), jnp.float32), pltpu.SemaphoreType.DMA((rows // SUB,))],
        out_specs=(VMEM, HBM),
    )
    return barycenter, updated.reshape(members, levels, lon, lat)


def solution(mesh):
    return jax.shard_map(
        body,
        mesh=mesh,
        in_specs=(
            P("mem", None, "tile", None),
            P("mem", None, "tile", None),
            P("mem"),
            P("tile", None),
        ),
        out_specs=(P(None, "tile", None), P("mem", None, "tile", None)),
        check_vma=False,
    )
```

```python
import math
from functools import partial

import jax
import jax.numpy as jnp
import numpy as np
from jax import lax
from jax.experimental import pallas as pl
from jax.experimental.pallas import tpu as pltpu
from jax.sharding import PartitionSpec as P

BACKGROUND = 0.01
REACH = 4
SUB = 8
VMEM = pl.BlockSpec(memory_space=pltpu.VMEM)
HBM = pl.BlockSpec(memory_space=pl.ANY)
AREA, ZONAL, NORTH, SOUTH, CENTER = range(5)


def coefficients(lat_cells):
    spacing = math.pi / lat_cells
    index = np.arange(lat_cells)
    latitude = -0.5 * math.pi + (index + 0.5) * spacing
    cell_area = np.cos(latitude)
    zonal = 0.2 * np.minimum(2.2, 1.0 / cell_area**2)
    north = np.where(index == lat_cells - 1, 0.0, 0.05 * np.cos(latitude + 0.5 * spacing) / cell_area)
    south = np.where(index == 0, 0.0, 0.05 * np.cos(latitude - 0.5 * spacing) / cell_area)
    center = 1.0 - 2.0 * zonal - north - south
    rows = np.stack([cell_area, zonal, north, south, center]).astype(np.float32)
    return np.ascontiguousarray(np.broadcast_to(rows[:, None, :], (5, SUB, lat_cells)))


def params(mib=20):
    return pltpu.CompilerParams(vmem_limit_bytes=mib * 2**20)


def rows_of(group):
    return pl.ds(group * SUB, SUB)


def block_of(group):
    return pl.ds(group * SUB * SUB, SUB * SUB)


def batches(last, first=0, size=4):
    return [range(start, min(start + size, last)) for start in range(first, last, size)]


def chunk_groups(groups):
    half = (groups + 1) // 2
    return [half, groups - half]


class Chunked:
    def __init__(self, refs):
        self.refs = refs

    def stack(self, group, order=range(REACH)):
        for ref in self.refs:
            held = ref.shape[1] // SUB
            if group < held:
                return stack_of(ref, group, order)
            group -= held

    def put(self, group, values):
        for ref in self.refs:
            held = ref.shape[1] // SUB
            if 0 <= group < held:
                for c, value in enumerate(values):
                    ref[c, rows_of(group), :] = value
            group -= held


def by_longitude(block, lat):
    return jnp.swapaxes(block.reshape(SUB, SUB, lat), 0, 1)


def stack_of(ref, group, order=range(REACH)):
    return [ref[c, rows_of(group), :] for c in order]


def odd_core():
    return lax.rem(lax.axis_index("tile"), 2) == 1


def from_outside(columns, odd):
    last = len(columns) - 1
    return [jnp.where(odd, columns[last - c], columns[c]) for c in range(len(columns))]


def spread_kernel(scaling_ref, coef_ref, inner_ref, *outer_refs):
    groups, lat = inner_ref.shape[1] // SUB, inner_ref.shape[2]
    odd = odd_core()
    outer = Chunked(outer_refs)
    for group in range(groups):
        columns = from_outside(by_longitude(scaling_ref[block_of(group), :], lat), odd)
        columns = [column * coef_ref[AREA] for column in columns]
        outer.put(group, columns[:REACH])
        for c in range(REACH):
            inner_ref[c, rows_of(group), :] = columns[c + REACH]


def lane_fold(value):
    lat = value.shape[-1]
    total = value[:, :128]
    for t in range(1, lat // 128):
        total = total + value[:, t * 128 : (t + 1) * 128]
    return total


def diffuse(columns, coef_ref):
    lat = columns[0].shape[-1]
    return [
        coef_ref[CENTER] * here
        + coef_ref[ZONAL] * (west + east)
        + coef_ref[NORTH] * pltpu.roll(here, lat - 1, 1)
        + coef_ref[SOUTH] * pltpu.roll(here, 1, 1)
        for west, here, east in zip(columns[:-2], columns[1:-1], columns[2:])
    ]


def inner_half(batch, halo_ref, inner_ref, outer_refs, coef_ref, edge_ref):
    outer = Chunked(outer_refs)
    columns = [outer.stack(g) + stack_of(inner_ref, g) + stack_of(halo_ref, g, (3, 2, 1, 0)) for g in batch]
    for s in range(REACH):
        columns = [diffuse(own, coef_ref) for own in columns]
        if s < REACH - 1:
            for own, group in zip(columns, batch):
                edge_ref[2 * s, rows_of(group), :] = own[0]
                edge_ref[2 * s + 1, rows_of(group), :] = own[1]
    return zip(batch, columns)


def outer_half(batch, first, halo_ref, outer_ref, edge_ref, coef_ref):
    columns = [stack_of(halo_ref, g - first, (3, 2, 1, 0)) + stack_of(outer_ref, g - first, (0, 1)) for g in batch]
    for s in range(REACH):
        columns = [diffuse(own, coef_ref) for own in columns]
        if s < REACH - 1:
            columns = [own + stack_of(edge_ref, g, (2 * s, 2 * s + 1)) for own, g in zip(columns, batch)]
    return zip(batch, columns)


def smooth_inner_kernel(
    halo_ref, inner_ref, fields_ref, mask_ref, coef_ref, *refs
):
    *outer_refs, out_ref, edge_ref, filled_ref, mass_ref = refs
    groups, lat = inner_ref.shape[1] // SUB, inner_ref.shape[2]
    odd = odd_core()
    for batch in batches(groups):
        for group, smoothed in inner_half(batch, halo_ref, inner_ref, outer_refs, coef_ref, edge_ref):
            fields = by_longitude(fields_ref[block_of(group), :], lat)
            filled = []
            for c in range(2 * REACH):
                valid = jnp.broadcast_to(mask_ref[c : c + 1, :], (SUB, lat)) == 1
                filled.append((jnp.where(valid, fields[c], 0.0) + BACKGROUND) * coef_ref[AREA])
            mass_ref[rows_of(group), :] = lane_fold(sum(filled))
            filled = from_outside(filled, odd)
            for c in range(REACH):
                filled_ref[c, rows_of(group), :] = filled[c]
                out_ref[c, rows_of(group), :] = filled[c + REACH] / smoothed[c]


def smooth_outer_kernel(first, halo_ref, outer_ref, edge_ref, filled_ref, coef_ref, out_ref):
    last = first + outer_ref.shape[1] // SUB
    for batch in batches(last, first):
        for group, smoothed in outer_half(batch, first, halo_ref, outer_ref, edge_ref, coef_ref):
            for c in range(REACH):
                out_ref[c, rows_of(group - first), :] = filled_ref[c, rows_of(group), :] / smoothed[c]


def low_half(shape):
    return lax.broadcasted_iota(jnp.int32, shape, 0) < SUB // 2


def add_logs(group, held, result, scaled_ref, weight_ref, inverse_ref, total_ref):
    lat = scaled_ref.shape[2]
    weight = jnp.broadcast_to(weight_ref[rows_of(group), :1], (SUB, lat))
    for c in range(REACH):
        inverse_ref[c, rows_of(held), :] = 1.0 / result[c]
        total_ref[c] = total_ref[c] + weight * jnp.log(scaled_ref[c, rows_of(held), :] * result[c])


def return_inner_kernel(halo_ref, inner_ref, scaled_ref, weight_ref, coef_ref, *refs):
    *outer_refs, inverse_ref, edge_ref, total_ref = refs
    groups = inner_ref.shape[1] // SUB
    total_ref[...] = jnp.zeros_like(total_ref)
    for batch in batches(groups):
        for group, result in inner_half(batch, halo_ref, inner_ref, outer_refs, coef_ref, edge_ref):
            add_logs(group, group, result, scaled_ref, weight_ref, inverse_ref, total_ref)


def return_outer_kernel(
    first, halo_ref, outer_ref, edge_ref, scaled_ref, weight_ref, coef_ref, inverse_ref, total_ref
):
    last = first + outer_ref.shape[1] // SUB
    total_ref[...] = jnp.zeros_like(total_ref)
    for batch in batches(last, first):
        for group, result in outer_half(batch, first, halo_ref, outer_ref, edge_ref, coef_ref):
            add_logs(group, group - first, result, scaled_ref, weight_ref, inverse_ref, total_ref)


def last_return_kernel(
    first,
    halo_ref,
    outer_ref,
    edge_ref,
    scaled_ref,
    weight_ref,
    coef_ref,
    inner_ref,
    earlier_ref,
    inverse_ref,
    logs_ref,
    total_ref,
):
    return_outer_kernel(
        first, halo_ref, outer_ref, edge_ref, scaled_ref, weight_ref, coef_ref, inverse_ref, total_ref
    )
    low = low_half(total_ref.shape[1:])
    for c in range(REACH):
        outer, inner = total_ref[c] + earlier_ref[c], inner_ref[c]
        outer = outer + pltpu.roll(outer, SUB // 2, 0)
        inner = inner + pltpu.roll(inner, SUB // 2, 0)
        logs_ref[c] = jnp.where(low, outer, inner)


def merge_kernel(own_ref, other_ref, count_ref, mass_ref, coef_ref, merged_ref, payload_ref):
    members, lat = mass_ref.shape[0], own_ref.shape[2]
    scale = 1.0 / count_ref[...]
    scale = jnp.broadcast_to(scale[:, :1], (SUB, lat))
    level = jnp.zeros((SUB, lat), jnp.float32)
    for c in range(REACH):
        weighted = jnp.exp((own_ref[c] + other_ref[c]) * scale)
        merged_ref[c] = weighted / coef_ref[AREA]
        level = level + weighted
    level = lane_fold(level)
    level = level + pltpu.roll(level, SUB // 2, 0)
    spare = jnp.zeros((128 - members - SUB, 128), jnp.float32)
    table = jnp.concatenate([mass_ref[...], level, spare], axis=0)
    row = jnp.sum(table.T, axis=0, keepdims=True)
    payload_ref[...] = jnp.broadcast_to(row[None], payload_ref.shape)


def finish_kernel(cells, got_ref, merged_ref, inner_ref, *refs):
    *outer_refs, bary_ref, updated_ref, staged_ref, sem = refs
    members, lat = inner_ref.shape[1:]
    groups = members // SUB
    odd = odd_core()
    total = jnp.sum(got_ref[...], axis=0)
    table = jnp.broadcast_to(total, (128, 128)).T
    level = table[members : members + SUB, :]
    low = low_half((SUB, lat))
    wide = lambda v: jnp.concatenate([v] * (lat // 128), axis=1)
    inverse = wide(cells / level)
    outer, inner = [], []
    for c in range(REACH):
        both = merged_ref[c] * inverse
        swapped = pltpu.roll(both, SUB // 2, 0)
        outer.append(jnp.where(low, both, swapped))
        inner.append(jnp.where(low, swapped, both))
    bary = from_outside(outer + inner, odd)
    bary_ref[...] = jnp.swapaxes(jnp.stack(bary), 0, 1)[: SUB // 2]
    for group in range(groups):
        rows = slice(group * SUB, (group + 1) * SUB)
        factor = wide(table[rows, :] / cells)
        quotients = Chunked(outer_refs).stack(group) + stack_of(inner_ref, group)
        out = [b * factor * quotient for b, quotient in zip(bary, from_outside(quotients, odd))]
        span = pl.ds(group * SUB * SUB, SUB * SUB)
        staged_ref[span, :] = jnp.swapaxes(jnp.stack(out), 0, 1).reshape(SUB * SUB, lat)
        pltpu.make_async_copy(staged_ref.at[span, :], updated_ref.at[span, :], sem.at[group]).start()
    for group in range(groups):
        span = pl.ds(group * SUB * SUB, SUB * SUB)
        pltpu.make_async_copy(staged_ref.at[span, :], updated_ref.at[span, :], sem.at[group]).wait()


def shape(*dims):
    return jax.ShapeDtypeStruct(dims, jnp.float32)


def call(kernel, outs, *args, scratch=(), out_specs=None):
    return pl.pallas_call(
        kernel,
        out_shape=outs,
        in_specs=[VMEM] * len(args),
        out_specs=out_specs or (VMEM,) * len(outs),
        scratch_shapes=scratch,
        compiler_params=params(),
    )(*args)


def body(fields, scaling, counts, land_mask):
    members, levels, lon, lat = fields.shape
    tiles = lax.axis_size("tile")
    rows = members * levels
    cells = lon * tiles * lat
    half = shape(REACH, rows, lat)
    edge = shape(2 * REACH - 2, rows, lat)
    packed = shape(REACH, SUB, lat)
    chunks = chunk_groups(rows // SUB)
    firsts = [sum(chunks[:n]) for n in range(len(chunks))]
    parts = [shape(REACH, n * SUB, lat) for n in chunks]
    coef = jnp.asarray(coefficients(lat))
    with_mate = [(i, i ^ 1) for i in range(tiles)]
    with_neighbour = [(i, (i + (1 if i % 2 else -1)) % tiles) for i in range(tiles)]
    scaling = scaling.reshape(rows * lon, lat)
    fields = fields.reshape(rows * lon, lat)
    weights = counts.astype(jnp.float32)
    weight_rows = jnp.broadcast_to(jnp.repeat(weights, levels)[:, None], (rows, 128))
    count = jnp.broadcast_to(jnp.sum(weights), (SUB, 128))
    count = count + lax.ppermute(count, "mem", [(0, 1), (1, 0)])

    inner, *outer = call(spread_kernel, (half, *parts), scaling, coef)
    outer_halo = [lax.ppermute(part, "tile", with_neighbour) for part in outer]
    inner_halo = lax.ppermute(inner, "tile", with_mate)
    inner_halo, count = lax.optimization_barrier((inner_halo, count))
    v_inner, edges, filled, mass = call(
        smooth_inner_kernel, (half, edge, half, shape(rows, 128)), inner_halo, inner, fields, land_mask, coef, *outer
    )
    v_inner_halo = lax.ppermute(v_inner, "tile", with_mate)
    v_outer, v_outer_halo = [], []
    for first, part, halo, own in zip(firsts, parts, outer_halo, outer):
        (value,) = call(partial(smooth_outer_kernel, first), (part,), halo, own, edges, filled, coef)
        v_outer.append(value)
        v_outer_halo.append(lax.ppermute(value, "tile", with_neighbour))
    inverse_inner, edges, inner_logs = call(
        return_inner_kernel, (half, edge, packed), v_inner_halo, v_inner, inner, weight_rows, coef, *v_outer
    )
    inverse_first, first_logs = call(
        partial(return_outer_kernel, firsts[0]),
        (parts[0], packed),
        v_outer_halo[0],
        v_outer[0],
        edges,
        outer[0],
        weight_rows,
        coef,
    )
    inverse_last, logs = call(
        partial(last_return_kernel, firsts[1]),
        (parts[1], packed),
        v_outer_halo[1],
        v_outer[1],
        edges,
        outer[1],
        weight_rows,
        coef,
        inner_logs,
        first_logs,
        scratch=[pltpu.VMEM((REACH, SUB, lat), jnp.float32)],
    )
    other = lax.ppermute(logs, "mem", [(0, 1), (1, 0)])
    merged, payload = call(merge_kernel, (packed, shape(tiles, 1, 128)), logs, other, count, mass, coef)
    got = lax.all_to_all(payload, "tile", split_axis=0, concat_axis=0)
    barycenter, updated = call(
        partial(finish_kernel, float(cells)),
        (shape(levels, lon, lat), shape(rows * lon, lat)),
        got,
        merged,
        inverse_inner,
        inverse_first,
        inverse_last,
        scratch=[pltpu.VMEM((rows * lon, lat), jnp.float32), pltpu.SemaphoreType.DMA((rows // SUB,))],
        out_specs=(VMEM, HBM),
    )
    return barycenter, updated.reshape(members, levels, lon, lat)


def solution(mesh):
    return jax.shard_map(
        body,
        mesh=mesh,
        in_specs=(
            P("mem", None, "tile", None),
            P("mem", None, "tile", None),
            P("mem"),
            P("tile", None),
        ),
        out_specs=(P(None, "tile", None), P("mem", None, "tile", None)),
        check_vma=False,
    )
```

```python
import math
from functools import partial

import jax
import jax.numpy as jnp
import numpy as np
from jax import lax
from jax.experimental import pallas as pl
from jax.experimental.pallas import tpu as pltpu
from jax.sharding import PartitionSpec as P

BACKGROUND = 0.01
REACH = 4
SUB = 8
VMEM = pl.BlockSpec(memory_space=pltpu.VMEM)
HBM = pl.BlockSpec(memory_space=pl.ANY)
AREA, ZONAL, NORTH, SOUTH, CENTER = range(5)


def coefficients(lat_cells):
    spacing = math.pi / lat_cells
    index = np.arange(lat_cells)
    latitude = -0.5 * math.pi + (index + 0.5) * spacing
    cell_area = np.cos(latitude)
    zonal = 0.2 * np.minimum(2.2, 1.0 / cell_area**2)
    north = np.where(index == lat_cells - 1, 0.0, 0.05 * np.cos(latitude + 0.5 * spacing) / cell_area)
    south = np.where(index == 0, 0.0, 0.05 * np.cos(latitude - 0.5 * spacing) / cell_area)
    center = 1.0 - 2.0 * zonal - north - south
    rows = np.stack([cell_area, zonal, north, south, center]).astype(np.float32)
    return np.ascontiguousarray(np.broadcast_to(rows[:, None, :], (5, SUB, lat_cells)))


def params(mib=20):
    return pltpu.CompilerParams(vmem_limit_bytes=mib * 2**20)


def rows_of(group):
    return pl.ds(group * SUB, SUB)


def block_of(group):
    return pl.ds(group * SUB * SUB, SUB * SUB)


def batches(last, first=0, size=4):
    return [range(start, min(start + size, last)) for start in range(first, last, size)]


def chunk_groups(groups):
    half = (groups + 1) // 2
    return [half, groups - half]


class Chunked:
    def __init__(self, refs):
        self.refs = refs

    def stack(self, group, order=range(REACH)):
        for ref in self.refs:
            held = ref.shape[1] // SUB
            if group < held:
                return stack_of(ref, group, order)
            group -= held

    def put(self, group, values):
        for ref in self.refs:
            held = ref.shape[1] // SUB
            if 0 <= group < held:
                for c, value in enumerate(values):
                    ref[c, rows_of(group), :] = value
            group -= held


def by_longitude(block, lat):
    return jnp.swapaxes(block.reshape(SUB, SUB, lat), 0, 1)


def stack_of(ref, group, order=range(REACH)):
    return [ref[c, rows_of(group), :] for c in order]


def odd_core():
    return lax.rem(lax.axis_index("tile"), 2) == 1


def from_outside(columns, odd):
    last = len(columns) - 1
    return [jnp.where(odd, columns[last - c], columns[c]) for c in range(len(columns))]


def spread_kernel(scaling_ref, coef_ref, inner_ref, *outer_refs):
    groups, lat = inner_ref.shape[1] // SUB, inner_ref.shape[2]
    odd = odd_core()
    outer = Chunked(outer_refs)
    for group in range(groups):
        columns = from_outside(by_longitude(scaling_ref[block_of(group), :], lat), odd)
        columns = [column * coef_ref[AREA] for column in columns]
        outer.put(group, columns[:REACH])
        for c in range(REACH):
            inner_ref[c, rows_of(group), :] = columns[c + REACH]


def lane_fold(value):
    lat = value.shape[-1]
    total = value[:, :128]
    for t in range(1, lat // 128):
        total = total + value[:, t * 128 : (t + 1) * 128]
    return total


def diffuse(columns, coef_ref):
    lat = columns[0].shape[-1]
    return [
        coef_ref[CENTER] * here
        + coef_ref[ZONAL] * (west + east)
        + coef_ref[NORTH] * pltpu.roll(here, lat - 1, 1)
        + coef_ref[SOUTH] * pltpu.roll(here, 1, 1)
        for west, here, east in zip(columns[:-2], columns[1:-1], columns[2:])
    ]


def inner_half(batch, halo_ref, inner_ref, outer_refs, coef_ref, edge_ref):
    outer = Chunked(outer_refs)
    columns = [outer.stack(g) + stack_of(inner_ref, g) + stack_of(halo_ref, g, (3, 2, 1, 0)) for g in batch]
    for s in range(REACH):
        columns = [diffuse(own, coef_ref) for own in columns]
        if s < REACH - 1:
            for own, group in zip(columns, batch):
                edge_ref[2 * s, rows_of(group), :] = own[0]
                edge_ref[2 * s + 1, rows_of(group), :] = own[1]
    return zip(batch, columns)


def outer_half(batch, first, halo_ref, outer_ref, edge_ref, coef_ref):
    columns = [stack_of(halo_ref, g - first, (3, 2, 1, 0)) + stack_of(outer_ref, g - first, (0, 1)) for g in batch]
    for s in range(REACH):
        columns = [diffuse(own, coef_ref) for own in columns]
        if s < REACH - 1:
            columns = [own + stack_of(edge_ref, g, (2 * s, 2 * s + 1)) for own, g in zip(columns, batch)]
    return zip(batch, columns)


def smooth_inner_kernel(
    halo_ref, inner_ref, fields_ref, mask_ref, coef_ref, *refs
):
    *outer_refs, out_ref, edge_ref, filled_ref, mass_ref = refs
    groups, lat = inner_ref.shape[1] // SUB, inner_ref.shape[2]
    odd = odd_core()
    for batch in batches(groups):
        for group, smoothed in inner_half(batch, halo_ref, inner_ref, outer_refs, coef_ref, edge_ref):
            fields = by_longitude(fields_ref[block_of(group), :], lat)
            filled = []
            for c in range(2 * REACH):
                valid = jnp.broadcast_to(mask_ref[c : c + 1, :], (SUB, lat)) == 1
                filled.append((jnp.where(valid, fields[c], 0.0) + BACKGROUND) * coef_ref[AREA])
            mass_ref[rows_of(group), :] = lane_fold(sum(filled))
            filled = from_outside(filled, odd)
            for c in range(REACH):
                filled_ref[c, rows_of(group), :] = filled[c]
                out_ref[c, rows_of(group), :] = filled[c + REACH] / smoothed[c]


def smooth_outer_kernel(first, halo_ref, outer_ref, edge_ref, filled_ref, coef_ref, out_ref):
    last = first + outer_ref.shape[1] // SUB
    for batch in batches(last, first):
        for group, smoothed in outer_half(batch, first, halo_ref, outer_ref, edge_ref, coef_ref):
            for c in range(REACH):
                out_ref[c, rows_of(group - first), :] = filled_ref[c, rows_of(group), :] / smoothed[c]


def low_half(shape):
    return lax.broadcasted_iota(jnp.int32, shape, 0) < SUB // 2


def add_logs(group, held, result, scaled_ref, weight_ref, inverse_ref, total_ref):
    lat = scaled_ref.shape[2]
    weight = jnp.broadcast_to(weight_ref[rows_of(group), :1], (SUB, lat))
    for c in range(REACH):
        inverse_ref[c, rows_of(held), :] = 1.0 / result[c]
        total_ref[c] = total_ref[c] + weight * jnp.log(scaled_ref[c, rows_of(held), :] * result[c])


def return_inner_kernel(halo_ref, inner_ref, scaled_ref, weight_ref, coef_ref, *refs):
    *outer_refs, inverse_ref, edge_ref, total_ref = refs
    groups = inner_ref.shape[1] // SUB
    total_ref[...] = jnp.zeros_like(total_ref)
    for batch in batches(groups):
        for group, result in inner_half(batch, halo_ref, inner_ref, outer_refs, coef_ref, edge_ref):
            add_logs(group, group, result, scaled_ref, weight_ref, inverse_ref, total_ref)


def return_outer_kernel(
    first, halo_ref, outer_ref, edge_ref, scaled_ref, weight_ref, coef_ref, inverse_ref, total_ref
):
    last = first + outer_ref.shape[1] // SUB
    total_ref[...] = jnp.zeros_like(total_ref)
    for batch in batches(last, first):
        for group, result in outer_half(batch, first, halo_ref, outer_ref, edge_ref, coef_ref):
            add_logs(group, group - first, result, scaled_ref, weight_ref, inverse_ref, total_ref)


def last_return_kernel(
    first,
    halo_ref,
    outer_ref,
    edge_ref,
    scaled_ref,
    weight_ref,
    coef_ref,
    inner_ref,
    earlier_ref,
    inverse_ref,
    logs_ref,
    total_ref,
):
    return_outer_kernel(
        first, halo_ref, outer_ref, edge_ref, scaled_ref, weight_ref, coef_ref, inverse_ref, total_ref
    )
    low = low_half(total_ref.shape[1:])
    for c in range(REACH):
        outer, inner = total_ref[c] + earlier_ref[c], inner_ref[c]
        outer = outer + pltpu.roll(outer, SUB // 2, 0)
        inner = inner + pltpu.roll(inner, SUB // 2, 0)
        logs_ref[c] = jnp.where(low, outer, inner)


def merge_kernel(own_ref, other_ref, count_ref, mass_ref, coef_ref, merged_ref, payload_ref):
    members, lat = mass_ref.shape[0], own_ref.shape[2]
    scale = 1.0 / count_ref[...]
    scale = jnp.broadcast_to(scale[:, :1], (SUB, lat))
    level = jnp.zeros((SUB, lat), jnp.float32)
    for c in range(REACH):
        weighted = jnp.exp((own_ref[c] + other_ref[c]) * scale)
        merged_ref[c] = weighted / coef_ref[AREA]
        level = level + weighted
    level = lane_fold(level)
    level = level + pltpu.roll(level, SUB // 2, 0)
    spare = jnp.zeros((128 - members - SUB, 128), jnp.float32)
    table = jnp.concatenate([mass_ref[...], level, spare], axis=0)
    row = jnp.sum(table.T, axis=0, keepdims=True)
    payload_ref[...] = jnp.broadcast_to(row[None], payload_ref.shape)


def finish_kernel(cells, got_ref, merged_ref, inner_ref, *refs):
    *outer_refs, bary_ref, updated_ref, staged_ref, sem = refs
    members, lat = inner_ref.shape[1:]
    groups = members // SUB
    odd = odd_core()
    total = jnp.sum(got_ref[...], axis=0)
    table = jnp.broadcast_to(total, (128, 128)).T
    level = table[members : members + SUB, :]
    low = low_half((SUB, lat))
    wide = lambda v: jnp.concatenate([v] * (lat // 128), axis=1)
    inverse = wide(cells / level)
    outer, inner = [], []
    for c in range(REACH):
        both = merged_ref[c] * inverse
        swapped = pltpu.roll(both, SUB // 2, 0)
        outer.append(jnp.where(low, both, swapped))
        inner.append(jnp.where(low, swapped, both))
    bary = from_outside(outer + inner, odd)
    bary_ref[...] = jnp.swapaxes(jnp.stack(bary), 0, 1)[: SUB // 2]
    for group in range(groups):
        rows = slice(group * SUB, (group + 1) * SUB)
        factor = wide(table[rows, :] / cells)
        quotients = Chunked(outer_refs).stack(group) + stack_of(inner_ref, group)
        out = [b * factor * quotient for b, quotient in zip(bary, from_outside(quotients, odd))]
        span = pl.ds(group * SUB * SUB, SUB * SUB)
        staged_ref[span, :] = jnp.swapaxes(jnp.stack(out), 0, 1).reshape(SUB * SUB, lat)
        pltpu.make_async_copy(staged_ref.at[span, :], updated_ref.at[span, :], sem.at[group]).start()
    for group in range(groups):
        span = pl.ds(group * SUB * SUB, SUB * SUB)
        pltpu.make_async_copy(staged_ref.at[span, :], updated_ref.at[span, :], sem.at[group]).wait()


def shape(*dims):
    return jax.ShapeDtypeStruct(dims, jnp.float32)


def call(kernel, outs, *args, scratch=(), out_specs=None):
    return pl.pallas_call(
        kernel,
        out_shape=outs,
        in_specs=[VMEM] * len(args),
        out_specs=out_specs or (VMEM,) * len(outs),
        scratch_shapes=scratch,
        compiler_params=params(),
    )(*args)


def body(fields, scaling, counts, land_mask):
    members, levels, lon, lat = fields.shape
    tiles = lax.axis_size("tile")
    rows = members * levels
    cells = lon * tiles * lat
    half = shape(REACH, rows, lat)
    edge = shape(2 * REACH - 2, rows, lat)
    packed = shape(REACH, SUB, lat)
    chunks = chunk_groups(rows // SUB)
    firsts = [sum(chunks[:n]) for n in range(len(chunks))]
    parts = [shape(REACH, n * SUB, lat) for n in chunks]
    coef = jnp.asarray(coefficients(lat))
    with_mate = [(i, i ^ 1) for i in range(tiles)]
    with_neighbour = [(i, (i + (1 if i % 2 else -1)) % tiles) for i in range(tiles)]
    scaling = scaling.reshape(rows * lon, lat)
    fields = fields.reshape(rows * lon, lat)
    weights = counts.astype(jnp.float32)
    weight_rows = jnp.broadcast_to(jnp.repeat(weights, levels)[:, None], (rows, 128))
    count = jnp.broadcast_to(jnp.sum(weights), (SUB, 128))
    count = count + lax.ppermute(count, "mem", [(0, 1), (1, 0)])

    inner, *outer = call(spread_kernel, (half, *parts), scaling, coef)
    outer_halo = [lax.ppermute(part, "tile", with_neighbour) for part in outer]
    inner_halo = lax.ppermute(inner, "tile", with_mate)
    outer_halo[0], count = lax.optimization_barrier((outer_halo[0], count))
    v_inner, edges, filled, mass = call(
        smooth_inner_kernel, (half, edge, half, shape(rows, 128)), inner_halo, inner, fields, land_mask, coef, *outer
    )
    v_inner_halo = lax.ppermute(v_inner, "tile", with_mate)
    v_outer, v_outer_halo = [], []
    for first, part, halo, own in zip(firsts, parts, outer_halo, outer):
        (value,) = call(partial(smooth_outer_kernel, first), (part,), halo, own, edges, filled, coef)
        v_outer.append(value)
        v_outer_halo.append(lax.ppermute(value, "tile", with_neighbour))
    inverse_inner, edges, inner_logs = call(
        return_inner_kernel, (half, edge, packed), v_inner_halo, v_inner, inner, weight_rows, coef, *v_outer
    )
    inverse_first, first_logs = call(
        partial(return_outer_kernel, firsts[0]),
        (parts[0], packed),
        v_outer_halo[0],
        v_outer[0],
        edges,
        outer[0],
        weight_rows,
        coef,
    )
    inverse_last, logs = call(
        partial(last_return_kernel, firsts[1]),
        (parts[1], packed),
        v_outer_halo[1],
        v_outer[1],
        edges,
        outer[1],
        weight_rows,
        coef,
        inner_logs,
        first_logs,
        scratch=[pltpu.VMEM((REACH, SUB, lat), jnp.float32)],
    )
    other = lax.ppermute(logs, "mem", [(0, 1), (1, 0)])
    merged, payload = call(merge_kernel, (packed, shape(tiles, 1, 128)), logs, other, count, mass, coef)
    got = lax.all_to_all(payload, "tile", split_axis=0, concat_axis=0)
    barycenter, updated = call(
        partial(finish_kernel, float(cells)),
        (shape(levels, lon, lat), shape(rows * lon, lat)),
        got,
        merged,
        inverse_inner,
        inverse_first,
        inverse_last,
        scratch=[pltpu.VMEM((rows * lon, lat), jnp.float32), pltpu.SemaphoreType.DMA((rows // SUB,))],
        out_specs=(VMEM, HBM),
    )
    return barycenter, updated.reshape(members, levels, lon, lat)


def solution(mesh):
    return jax.shard_map(
        body,
        mesh=mesh,
        in_specs=(
            P("mem", None, "tile", None),
            P("mem", None, "tile", None),
            P("mem"),
            P("tile", None),
        ),
        out_specs=(P(None, "tile", None), P("mem", None, "tile", None)),
        check_vma=False,
    )
```

```python
import math
from functools import partial

import jax
import jax.numpy as jnp
import numpy as np
from jax import lax
from jax.experimental import pallas as pl
from jax.experimental.pallas import tpu as pltpu
from jax.sharding import PartitionSpec as P

BACKGROUND = 0.01
REACH = 4
SUB = 8
VMEM = pl.BlockSpec(memory_space=pltpu.VMEM)
HBM = pl.BlockSpec(memory_space=pl.ANY)
AREA, ZONAL, NORTH, SOUTH, CENTER = range(5)


def coefficients(lat_cells):
    spacing = math.pi / lat_cells
    index = np.arange(lat_cells)
    latitude = -0.5 * math.pi + (index + 0.5) * spacing
    cell_area = np.cos(latitude)
    zonal = 0.2 * np.minimum(2.2, 1.0 / cell_area**2)
    north = np.where(index == lat_cells - 1, 0.0, 0.05 * np.cos(latitude + 0.5 * spacing) / cell_area)
    south = np.where(index == 0, 0.0, 0.05 * np.cos(latitude - 0.5 * spacing) / cell_area)
    center = 1.0 - 2.0 * zonal - north - south
    rows = np.stack([cell_area, zonal, north, south, center]).astype(np.float32)
    return np.ascontiguousarray(np.broadcast_to(rows[:, None, :], (5, SUB, lat_cells)))


def params(mib=20):
    return pltpu.CompilerParams(vmem_limit_bytes=mib * 2**20)


def rows_of(group):
    return pl.ds(group * SUB, SUB)


def block_of(group):
    return pl.ds(group * SUB * SUB, SUB * SUB)


def batches(last, first=0, size=4):
    return [range(start, min(start + size, last)) for start in range(first, last, size)]


def chunk_groups(groups):
    half = (groups + 1) // 2
    return [half, groups - half]


class Chunked:
    def __init__(self, refs):
        self.refs = refs

    def stack(self, group, order=range(REACH)):
        for ref in self.refs:
            held = ref.shape[1] // SUB
            if group < held:
                return stack_of(ref, group, order)
            group -= held

    def put(self, group, values):
        for ref in self.refs:
            held = ref.shape[1] // SUB
            if 0 <= group < held:
                for c, value in enumerate(values):
                    ref[c, rows_of(group), :] = value
            group -= held


def by_longitude(block, lat):
    return jnp.swapaxes(block.reshape(SUB, SUB, lat), 0, 1)


def stack_of(ref, group, order=range(REACH)):
    return [ref[c, rows_of(group), :] for c in order]


def odd_core():
    return lax.rem(lax.axis_index("tile"), 2) == 1


def from_outside(columns, odd):
    last = len(columns) - 1
    return [jnp.where(odd, columns[last - c], columns[c]) for c in range(len(columns))]


def spread_kernel(scaling_ref, coef_ref, inner_ref, *outer_refs):
    groups, lat = inner_ref.shape[1] // SUB, inner_ref.shape[2]
    odd = odd_core()
    outer = Chunked(outer_refs)
    for group in range(groups):
        columns = from_outside(by_longitude(scaling_ref[block_of(group), :], lat), odd)
        columns = [column * coef_ref[AREA] for column in columns]
        outer.put(group, columns[:REACH])
        for c in range(REACH):
            inner_ref[c, rows_of(group), :] = columns[c + REACH]


def lane_fold(value):
    lat = value.shape[-1]
    total = value[:, :128]
    for t in range(1, lat // 128):
        total = total + value[:, t * 128 : (t + 1) * 128]
    return total


def diffuse(columns, coef_ref):
    lat = columns[0].shape[-1]
    return [
        coef_ref[CENTER] * here
        + coef_ref[ZONAL] * (west + east)
        + coef_ref[NORTH] * pltpu.roll(here, lat - 1, 1)
        + coef_ref[SOUTH] * pltpu.roll(here, 1, 1)
        for west, here, east in zip(columns[:-2], columns[1:-1], columns[2:])
    ]


def inner_half(batch, halo_ref, inner_ref, outer_refs, coef_ref, edge_ref):
    outer = Chunked(outer_refs)
    columns = [outer.stack(g) + stack_of(inner_ref, g) + stack_of(halo_ref, g, (3, 2, 1, 0)) for g in batch]
    for s in range(REACH):
        columns = [diffuse(own, coef_ref) for own in columns]
        if s < REACH - 1:
            for own, group in zip(columns, batch):
                edge_ref[2 * s, rows_of(group), :] = own[0]
                edge_ref[2 * s + 1, rows_of(group), :] = own[1]
    return zip(batch, columns)


def outer_half(batch, first, halo_ref, outer_ref, edge_ref, coef_ref):
    columns = [stack_of(halo_ref, g - first, (3, 2, 1, 0)) + stack_of(outer_ref, g - first, (0, 1)) for g in batch]
    for s in range(REACH):
        columns = [diffuse(own, coef_ref) for own in columns]
        if s < REACH - 1:
            columns = [own + stack_of(edge_ref, g, (2 * s, 2 * s + 1)) for own, g in zip(columns, batch)]
    return zip(batch, columns)


def smooth_inner_kernel(
    halo_ref, inner_ref, fields_ref, mask_ref, coef_ref, *refs
):
    *outer_refs, out_ref, edge_ref, filled_ref, mass_ref = refs
    groups, lat = inner_ref.shape[1] // SUB, inner_ref.shape[2]
    odd = odd_core()
    for batch in batches(groups):
        for group, smoothed in inner_half(batch, halo_ref, inner_ref, outer_refs, coef_ref, edge_ref):
            fields = by_longitude(fields_ref[block_of(group), :], lat)
            filled = []
            for c in range(2 * REACH):
                valid = jnp.broadcast_to(mask_ref[c : c + 1, :], (SUB, lat)) == 1
                filled.append((jnp.where(valid, fields[c], 0.0) + BACKGROUND) * coef_ref[AREA])
            mass_ref[rows_of(group), :] = lane_fold(sum(filled))
            filled = from_outside(filled, odd)
            for c in range(REACH):
                filled_ref[c, rows_of(group), :] = filled[c]
                out_ref[c, rows_of(group), :] = filled[c + REACH] / smoothed[c]


def smooth_outer_kernel(first, halo_ref, outer_ref, edge_ref, filled_ref, coef_ref, out_ref):
    last = first + outer_ref.shape[1] // SUB
    for batch in batches(last, first):
        for group, smoothed in outer_half(batch, first, halo_ref, outer_ref, edge_ref, coef_ref):
            for c in range(REACH):
                out_ref[c, rows_of(group - first), :] = filled_ref[c, rows_of(group), :] / smoothed[c]


def low_half(shape):
    return lax.broadcasted_iota(jnp.int32, shape, 0) < SUB // 2


def add_logs(group, held, result, scaled_ref, weight_ref, inverse_ref, total_ref):
    lat = scaled_ref.shape[2]
    weight = jnp.broadcast_to(weight_ref[rows_of(group), :1], (SUB, lat))
    for c in range(REACH):
        inverse_ref[c, rows_of(held), :] = 1.0 / result[c]
        total_ref[c] = total_ref[c] + weight * jnp.log(scaled_ref[c, rows_of(held), :] * result[c])


def return_inner_kernel(halo_ref, inner_ref, scaled_ref, weight_ref, coef_ref, *refs):
    *outer_refs, inverse_ref, edge_ref, total_ref = refs
    groups = inner_ref.shape[1] // SUB
    total_ref[...] = jnp.zeros_like(total_ref)
    for batch in batches(groups):
        for group, result in inner_half(batch, halo_ref, inner_ref, outer_refs, coef_ref, edge_ref):
            add_logs(group, group, result, scaled_ref, weight_ref, inverse_ref, total_ref)


def return_outer_kernel(
    first, halo_ref, outer_ref, edge_ref, scaled_ref, weight_ref, coef_ref, inverse_ref, total_ref
):
    last = first + outer_ref.shape[1] // SUB
    total_ref[...] = jnp.zeros_like(total_ref)
    for batch in batches(last, first):
        for group, result in outer_half(batch, first, halo_ref, outer_ref, edge_ref, coef_ref):
            add_logs(group, group - first, result, scaled_ref, weight_ref, inverse_ref, total_ref)


def last_return_kernel(
    first,
    halo_ref,
    outer_ref,
    edge_ref,
    scaled_ref,
    weight_ref,
    coef_ref,
    inner_ref,
    earlier_ref,
    inverse_ref,
    logs_ref,
    total_ref,
):
    return_outer_kernel(
        first, halo_ref, outer_ref, edge_ref, scaled_ref, weight_ref, coef_ref, inverse_ref, total_ref
    )
    low = low_half(total_ref.shape[1:])
    tiles = total_ref.shape[2] // 128
    for c in range(REACH):
        outer, inner = total_ref[c] + earlier_ref[c], inner_ref[c]
        outer = outer + pltpu.roll(outer, SUB // 2, 0)
        inner = inner + pltpu.roll(inner, SUB // 2, 0)
        both = jnp.where(low, outer, inner)
        for t in range(tiles):
            logs_ref[rows_of(c * tiles + t), :] = both[:, t * 128 : (t + 1) * 128]
    count = jnp.sum(weight_ref[...], axis=0, keepdims=True) * (1.0 / (SUB // 2))
    logs_ref[rows_of(REACH * tiles), :] = jnp.broadcast_to(count, (SUB, 128))


def merge_kernel(own_ref, other_ref, mass_ref, coef_ref, merged_ref, payload_ref):
    members, tiles = mass_ref.shape[0], merged_ref.shape[2] // 128
    both = lambda n: own_ref[rows_of(n), :] + other_ref[rows_of(n), :]
    scale = 1.0 / both(REACH * tiles)
    level = jnp.zeros((SUB, 128), jnp.float32)
    for c in range(REACH):
        for t in range(tiles):
            span = slice(t * 128, (t + 1) * 128)
            weighted = jnp.exp(both(c * tiles + t) * scale)
            merged_ref[c, :, span] = weighted / coef_ref[AREA, :, span]
            level = level + weighted
    level = level + pltpu.roll(level, SUB // 2, 0)
    spare = jnp.zeros((128 - members - SUB, 128), jnp.float32)
    table = jnp.concatenate([mass_ref[...], level, spare], axis=0)
    row = jnp.sum(table.T, axis=0, keepdims=True)
    payload_ref[...] = jnp.broadcast_to(row[None], payload_ref.shape)


def finish_kernel(cells, got_ref, merged_ref, inner_ref, *refs):
    *outer_refs, bary_ref, updated_ref, staged_ref, sem = refs
    members, lat = inner_ref.shape[1:]
    groups = members // SUB
    odd = odd_core()
    total = jnp.sum(got_ref[...], axis=0)
    table = jnp.broadcast_to(total, (128, 128)).T
    level = table[members : members + SUB, :]
    low = low_half((SUB, lat))
    wide = lambda v: jnp.concatenate([v] * (lat // 128), axis=1)
    inverse = wide(cells / level)
    outer, inner = [], []
    for c in range(REACH):
        both = merged_ref[c] * inverse
        swapped = pltpu.roll(both, SUB // 2, 0)
        outer.append(jnp.where(low, both, swapped))
        inner.append(jnp.where(low, swapped, both))
    bary = from_outside(outer + inner, odd)
    bary_ref[...] = jnp.swapaxes(jnp.stack(bary), 0, 1)[: SUB // 2]
    for group in range(groups):
        rows = slice(group * SUB, (group + 1) * SUB)
        factor = wide(table[rows, :] / cells)
        quotients = Chunked(outer_refs).stack(group) + stack_of(inner_ref, group)
        out = [b * factor * quotient for b, quotient in zip(bary, from_outside(quotients, odd))]
        span = pl.ds(group * SUB * SUB, SUB * SUB)
        staged_ref[span, :] = jnp.swapaxes(jnp.stack(out), 0, 1).reshape(SUB * SUB, lat)
        pltpu.make_async_copy(staged_ref.at[span, :], updated_ref.at[span, :], sem.at[group]).start()
    for group in range(groups):
        span = pl.ds(group * SUB * SUB, SUB * SUB)
        pltpu.make_async_copy(staged_ref.at[span, :], updated_ref.at[span, :], sem.at[group]).wait()


def shape(*dims):
    return jax.ShapeDtypeStruct(dims, jnp.float32)


def call(kernel, outs, *args, scratch=(), out_specs=None):
    return pl.pallas_call(
        kernel,
        out_shape=outs,
        in_specs=[VMEM] * len(args),
        out_specs=out_specs or (VMEM,) * len(outs),
        scratch_shapes=scratch,
        compiler_params=params(),
    )(*args)


def body(fields, scaling, counts, land_mask):
    members, levels, lon, lat = fields.shape
    tiles = lax.axis_size("tile")
    rows = members * levels
    cells = lon * tiles * lat
    half = shape(REACH, rows, lat)
    edge = shape(2 * REACH - 2, rows, lat)
    packed = shape(REACH, SUB, lat)
    chunks = chunk_groups(rows // SUB)
    firsts = [sum(chunks[:n]) for n in range(len(chunks))]
    parts = [shape(REACH, n * SUB, lat) for n in chunks]
    coef = jnp.asarray(coefficients(lat))
    with_mate = [(i, i ^ 1) for i in range(tiles)]
    with_neighbour = [(i, (i + (1 if i % 2 else -1)) % tiles) for i in range(tiles)]
    scaling = scaling.reshape(rows * lon, lat)
    fields = fields.reshape(rows * lon, lat)
    weights = counts.astype(jnp.float32)
    weight_rows = jnp.broadcast_to(jnp.repeat(weights, levels)[:, None], (rows, 128))

    inner, *outer = call(spread_kernel, (half, *parts), scaling, coef)
    outer_halo = [lax.ppermute(part, "tile", with_neighbour) for part in outer]
    inner_halo = lax.ppermute(inner, "tile", with_mate)
    v_inner, edges, filled, mass = call(
        smooth_inner_kernel, (half, edge, half, shape(rows, 128)), inner_halo, inner, fields, land_mask, coef, *outer
    )
    v_inner_halo = lax.ppermute(v_inner, "tile", with_mate)
    v_outer, v_outer_halo = [], []
    for first, part, halo, own in zip(firsts, parts, outer_halo, outer):
        (value,) = call(partial(smooth_outer_kernel, first), (part,), halo, own, edges, filled, coef)
        v_outer.append(value)
        v_outer_halo.append(lax.ppermute(value, "tile", with_neighbour))
    inverse_inner, edges, inner_logs = call(
        return_inner_kernel, (half, edge, packed), v_inner_halo, v_inner, inner, weight_rows, coef, *v_outer
    )
    inverse_first, first_logs = call(
        partial(return_outer_kernel, firsts[0]),
        (parts[0], packed),
        v_outer_halo[0],
        v_outer[0],
        edges,
        outer[0],
        weight_rows,
        coef,
    )
    inverse_last, logs = call(
        partial(last_return_kernel, firsts[1]),
        (parts[1], shape((REACH * lat // 128 + 1) * SUB, 128)),
        v_outer_halo[1],
        v_outer[1],
        edges,
        outer[1],
        weight_rows,
        coef,
        inner_logs,
        first_logs,
        scratch=[pltpu.VMEM((REACH, SUB, lat), jnp.float32)],
    )
    other = lax.ppermute(logs, "mem", [(0, 1), (1, 0)])
    merged, payload = call(merge_kernel, (packed, shape(tiles, 1, 128)), logs, other, mass, coef)
    got = lax.all_to_all(payload, "tile", split_axis=0, concat_axis=0)
    barycenter, updated = call(
        partial(finish_kernel, float(cells)),
        (shape(levels, lon, lat), shape(rows * lon, lat)),
        got,
        merged,
        inverse_inner,
        inverse_first,
        inverse_last,
        scratch=[pltpu.VMEM((rows * lon, lat), jnp.float32), pltpu.SemaphoreType.DMA((rows // SUB,))],
        out_specs=(VMEM, HBM),
    )
    return barycenter, updated.reshape(members, levels, lon, lat)


def solution(mesh):
    return jax.shard_map(
        body,
        mesh=mesh,
        in_specs=(
            P("mem", None, "tile", None),
            P("mem", None, "tile", None),
            P("mem"),
            P("tile", None),
        ),
        out_specs=(P(None, "tile", None), P("mem", None, "tile", None)),
        check_vma=False,
    )
```

```python
import math
from functools import partial

import jax
import jax.numpy as jnp
import numpy as np
from jax import lax
from jax.experimental import pallas as pl
from jax.experimental.pallas import tpu as pltpu
from jax.sharding import PartitionSpec as P

BACKGROUND = 0.01
REACH = 4
SUB = 8
VMEM = pl.BlockSpec(memory_space=pltpu.VMEM)
HBM = pl.BlockSpec(memory_space=pl.ANY)
AREA, ZONAL, NORTH, SOUTH, CENTER = range(5)


def coefficients(lat_cells):
    spacing = math.pi / lat_cells
    index = np.arange(lat_cells)
    latitude = -0.5 * math.pi + (index + 0.5) * spacing
    cell_area = np.cos(latitude)
    zonal = 0.2 * np.minimum(2.2, 1.0 / cell_area**2)
    north = np.where(index == lat_cells - 1, 0.0, 0.05 * np.cos(latitude + 0.5 * spacing) / cell_area)
    south = np.where(index == 0, 0.0, 0.05 * np.cos(latitude - 0.5 * spacing) / cell_area)
    center = 1.0 - 2.0 * zonal - north - south
    rows = np.stack([cell_area, zonal, north, south, center]).astype(np.float32)
    return np.ascontiguousarray(np.broadcast_to(rows[:, None, :], (5, SUB, lat_cells)))


def params(mib=20):
    return pltpu.CompilerParams(vmem_limit_bytes=mib * 2**20)


def rows_of(group):
    return pl.ds(group * SUB, SUB)


def block_of(group):
    return pl.ds(group * SUB * SUB, SUB * SUB)


def batches(last, first=0, size=4):
    return [range(start, min(start + size, last)) for start in range(first, last, size)]


def chunk_groups(groups):
    last = max(1, groups // 6)
    second = (groups - last) // 2
    return [groups - last - second, second, last]


class Chunked:
    def __init__(self, refs):
        self.refs = refs

    def stack(self, group, order=range(REACH)):
        for ref in self.refs:
            held = ref.shape[1] // SUB
            if group < held:
                return stack_of(ref, group, order)
            group -= held

    def put(self, group, values):
        for ref in self.refs:
            held = ref.shape[1] // SUB
            if 0 <= group < held:
                for c, value in enumerate(values):
                    ref[c, rows_of(group), :] = value
            group -= held


def by_longitude(block, lat):
    return jnp.swapaxes(block.reshape(SUB, SUB, lat), 0, 1)


def stack_of(ref, group, order=range(REACH)):
    return [ref[c, rows_of(group), :] for c in order]


def odd_core():
    return lax.rem(lax.axis_index("tile"), 2) == 1


def from_outside(columns, odd):
    last = len(columns) - 1
    return [jnp.where(odd, columns[last - c], columns[c]) for c in range(len(columns))]


def spread_kernel(scaling_ref, coef_ref, inner_ref, *outer_refs):
    groups, lat = inner_ref.shape[1] // SUB, inner_ref.shape[2]
    odd = odd_core()
    outer = Chunked(outer_refs)
    for group in range(groups):
        columns = from_outside(by_longitude(scaling_ref[block_of(group), :], lat), odd)
        columns = [column * coef_ref[AREA] for column in columns]
        outer.put(group, columns[:REACH])
        for c in range(REACH):
            inner_ref[c, rows_of(group), :] = columns[c + REACH]


def lane_fold(value):
    lat = value.shape[-1]
    total = value[:, :128]
    for t in range(1, lat // 128):
        total = total + value[:, t * 128 : (t + 1) * 128]
    return total


def diffuse(columns, coef_ref):
    lat = columns[0].shape[-1]
    return [
        coef_ref[CENTER] * here
        + coef_ref[ZONAL] * (west + east)
        + coef_ref[NORTH] * pltpu.roll(here, lat - 1, 1)
        + coef_ref[SOUTH] * pltpu.roll(here, 1, 1)
        for west, here, east in zip(columns[:-2], columns[1:-1], columns[2:])
    ]


def inner_half(batch, halo_ref, inner_ref, outer_refs, coef_ref, edge_ref):
    outer = Chunked(outer_refs)
    columns = [outer.stack(g) + stack_of(inner_ref, g) + stack_of(halo_ref, g, (3, 2, 1, 0)) for g in batch]
    for s in range(REACH):
        columns = [diffuse(own, coef_ref) for own in columns]
        if s < REACH - 1:
            for own, group in zip(columns, batch):
                edge_ref[2 * s, rows_of(group), :] = own[0]
                edge_ref[2 * s + 1, rows_of(group), :] = own[1]
    return zip(batch, columns)


def outer_half(batch, first, halo_ref, outer_ref, edge_ref, coef_ref):
    columns = [stack_of(halo_ref, g - first, (3, 2, 1, 0)) + stack_of(outer_ref, g - first, (0, 1)) for g in batch]
    for s in range(REACH):
        columns = [diffuse(own, coef_ref) for own in columns]
        if s < REACH - 1:
            columns = [own + stack_of(edge_ref, g, (2 * s, 2 * s + 1)) for own, g in zip(columns, batch)]
    return zip(batch, columns)


def smooth_inner_kernel(
    halo_ref, inner_ref, fields_ref, mask_ref, coef_ref, *refs
):
    *outer_refs, out_ref, edge_ref, filled_ref, mass_ref = refs
    groups, lat = inner_ref.shape[1] // SUB, inner_ref.shape[2]
    odd = odd_core()
    for batch in batches(groups):
        for group, smoothed in inner_half(batch, halo_ref, inner_ref, outer_refs, coef_ref, edge_ref):
            fields = by_longitude(fields_ref[block_of(group), :], lat)
            filled = []
            for c in range(2 * REACH):
                valid = jnp.broadcast_to(mask_ref[c : c + 1, :], (SUB, lat)) == 1
                filled.append((jnp.where(valid, fields[c], 0.0) + BACKGROUND) * coef_ref[AREA])
            mass_ref[rows_of(group), :] = lane_fold(sum(filled))
            filled = from_outside(filled, odd)
            for c in range(REACH):
                filled_ref[c, rows_of(group), :] = filled[c]
                out_ref[c, rows_of(group), :] = filled[c + REACH] / smoothed[c]


def smooth_outer_kernel(first, halo_ref, outer_ref, edge_ref, filled_ref, coef_ref, out_ref):
    last = first + outer_ref.shape[1] // SUB
    for batch in batches(last, first):
        for group, smoothed in outer_half(batch, first, halo_ref, outer_ref, edge_ref, coef_ref):
            for c in range(REACH):
                out_ref[c, rows_of(group - first), :] = filled_ref[c, rows_of(group), :] / smoothed[c]


def low_half(shape):
    return lax.broadcasted_iota(jnp.int32, shape, 0) < SUB // 2


def add_logs(group, held, result, scaled_ref, weight_ref, inverse_ref, total_ref):
    lat = scaled_ref.shape[2]
    weight = jnp.broadcast_to(weight_ref[rows_of(group), :1], (SUB, lat))
    for c in range(REACH):
        inverse_ref[c, rows_of(held), :] = 1.0 / result[c]
        total_ref[c] = total_ref[c] + weight * jnp.log(scaled_ref[c, rows_of(held), :] * result[c])


def return_inner_kernel(halo_ref, inner_ref, scaled_ref, weight_ref, coef_ref, *refs):
    *outer_refs, inverse_ref, edge_ref, total_ref = refs
    groups = inner_ref.shape[1] // SUB
    total_ref[...] = jnp.zeros_like(total_ref)
    for batch in batches(groups):
        for group, result in inner_half(batch, halo_ref, inner_ref, outer_refs, coef_ref, edge_ref):
            add_logs(group, group, result, scaled_ref, weight_ref, inverse_ref, total_ref)


def return_outer_kernel(
    first, halo_ref, outer_ref, edge_ref, scaled_ref, weight_ref, coef_ref, inverse_ref, total_ref
):
    last = first + outer_ref.shape[1] // SUB
    total_ref[...] = jnp.zeros_like(total_ref)
    for batch in batches(last, first):
        for group, result in outer_half(batch, first, halo_ref, outer_ref, edge_ref, coef_ref):
            add_logs(group, group - first, result, scaled_ref, weight_ref, inverse_ref, total_ref)


def last_return_kernel(
    first,
    halo_ref,
    outer_ref,
    edge_ref,
    scaled_ref,
    weight_ref,
    coef_ref,
    inner_ref,
    *refs,
):
    *earlier_refs, inverse_ref, logs_ref, total_ref = refs
    return_outer_kernel(
        first, halo_ref, outer_ref, edge_ref, scaled_ref, weight_ref, coef_ref, inverse_ref, total_ref
    )
    low = low_half(total_ref.shape[1:])
    tiles = total_ref.shape[2] // 128
    for c in range(REACH):
        outer, inner = sum((ref[c] for ref in earlier_refs), total_ref[c]), inner_ref[c]
        outer = outer + pltpu.roll(outer, SUB // 2, 0)
        inner = inner + pltpu.roll(inner, SUB // 2, 0)
        both = jnp.where(low, outer, inner)
        for t in range(tiles):
            logs_ref[rows_of(c * tiles + t), :] = both[:, t * 128 : (t + 1) * 128]
    count = jnp.sum(weight_ref[...], axis=0, keepdims=True) * (1.0 / (SUB // 2))
    logs_ref[rows_of(REACH * tiles), :] = jnp.broadcast_to(count, (SUB, 128))


def merge_kernel(own_ref, other_ref, mass_ref, coef_ref, merged_ref, payload_ref):
    members, tiles = mass_ref.shape[0], merged_ref.shape[2] // 128
    both = lambda n: own_ref[rows_of(n), :] + other_ref[rows_of(n), :]
    scale = 1.0 / both(REACH * tiles)
    level = jnp.zeros((SUB, 128), jnp.float32)
    for c in range(REACH):
        for t in range(tiles):
            span = slice(t * 128, (t + 1) * 128)
            weighted = jnp.exp(both(c * tiles + t) * scale)
            merged_ref[c, :, span] = weighted / coef_ref[AREA, :, span]
            level = level + weighted
    level = level + pltpu.roll(level, SUB // 2, 0)
    spare = jnp.zeros((128 - members - SUB, 128), jnp.float32)
    table = jnp.concatenate([mass_ref[...], level, spare], axis=0)
    row = jnp.sum(table.T, axis=0, keepdims=True)
    payload_ref[...] = jnp.broadcast_to(row[None], payload_ref.shape)


def finish_kernel(cells, got_ref, merged_ref, inner_ref, *refs):
    *outer_refs, bary_ref, updated_ref, staged_ref, sem = refs
    members, lat = inner_ref.shape[1:]
    groups = members // SUB
    odd = odd_core()
    total = jnp.sum(got_ref[...], axis=0)
    table = jnp.broadcast_to(total, (128, 128)).T
    level = table[members : members + SUB, :]
    low = low_half((SUB, lat))
    wide = lambda v: jnp.concatenate([v] * (lat // 128), axis=1)
    inverse = wide(cells / level)
    outer, inner = [], []
    for c in range(REACH):
        both = merged_ref[c] * inverse
        swapped = pltpu.roll(both, SUB // 2, 0)
        outer.append(jnp.where(low, both, swapped))
        inner.append(jnp.where(low, swapped, both))
    bary = from_outside(outer + inner, odd)
    bary_ref[...] = jnp.swapaxes(jnp.stack(bary), 0, 1)[: SUB // 2]
    for group in range(groups):
        rows = slice(group * SUB, (group + 1) * SUB)
        factor = wide(table[rows, :] / cells)
        quotients = Chunked(outer_refs).stack(group) + stack_of(inner_ref, group)
        out = [b * factor * quotient for b, quotient in zip(bary, from_outside(quotients, odd))]
        span = pl.ds(group * SUB * SUB, SUB * SUB)
        staged_ref[span, :] = jnp.swapaxes(jnp.stack(out), 0, 1).reshape(SUB * SUB, lat)
        pltpu.make_async_copy(staged_ref.at[span, :], updated_ref.at[span, :], sem.at[group]).start()
    for group in range(groups):
        span = pl.ds(group * SUB * SUB, SUB * SUB)
        pltpu.make_async_copy(staged_ref.at[span, :], updated_ref.at[span, :], sem.at[group]).wait()


def shape(*dims):
    return jax.ShapeDtypeStruct(dims, jnp.float32)


def call(kernel, outs, *args, scratch=(), out_specs=None):
    return pl.pallas_call(
        kernel,
        out_shape=outs,
        in_specs=[VMEM] * len(args),
        out_specs=out_specs or (VMEM,) * len(outs),
        scratch_shapes=scratch,
        compiler_params=params(),
    )(*args)


def body(fields, scaling, counts, land_mask):
    members, levels, lon, lat = fields.shape
    tiles = lax.axis_size("tile")
    rows = members * levels
    cells = lon * tiles * lat
    half = shape(REACH, rows, lat)
    edge = shape(2 * REACH - 2, rows, lat)
    packed = shape(REACH, SUB, lat)
    chunks = chunk_groups(rows // SUB)
    firsts = [sum(chunks[:n]) for n in range(len(chunks))]
    parts = [shape(REACH, n * SUB, lat) for n in chunks]
    coef = jnp.asarray(coefficients(lat))
    with_mate = [(i, i ^ 1) for i in range(tiles)]
    with_neighbour = [(i, (i + (1 if i % 2 else -1)) % tiles) for i in range(tiles)]
    scaling = scaling.reshape(rows * lon, lat)
    fields = fields.reshape(rows * lon, lat)
    weights = counts.astype(jnp.float32)
    weight_rows = jnp.broadcast_to(jnp.repeat(weights, levels)[:, None], (rows, 128))

    inner, *outer = call(spread_kernel, (half, *parts), scaling, coef)
    outer_halo = [lax.ppermute(part, "tile", with_neighbour) for part in outer]
    inner_halo = lax.ppermute(inner, "tile", with_mate)
    v_inner, edges, filled, mass = call(
        smooth_inner_kernel, (half, edge, half, shape(rows, 128)), inner_halo, inner, fields, land_mask, coef, *outer
    )
    v_inner_halo = lax.ppermute(v_inner, "tile", with_mate)
    v_outer, v_outer_halo = [], []
    for first, part, halo, own in zip(firsts, parts, outer_halo, outer):
        (value,) = call(partial(smooth_outer_kernel, first), (part,), halo, own, edges, filled, coef)
        v_outer.append(value)
        v_outer_halo.append(lax.ppermute(value, "tile", with_neighbour))
    inverse_inner, edges, inner_logs = call(
        return_inner_kernel, (half, edge, packed), v_inner_halo, v_inner, inner, weight_rows, coef, *v_outer
    )
    inverses, earlier = [inverse_inner], []
    for n, first in enumerate(firsts[:-1]):
        operands = v_outer_halo[n], v_outer[n], edges, outer[n], weight_rows, coef
        inverse, partial_logs = call(partial(return_outer_kernel, first), (parts[n], packed), *operands)
        inverses.append(inverse)
        earlier.append(partial_logs)
    inverse, logs = call(
        partial(last_return_kernel, firsts[-1]),
        (parts[-1], shape((REACH * lat // 128 + 1) * SUB, 128)),
        v_outer_halo[-1],
        v_outer[-1],
        edges,
        outer[-1],
        weight_rows,
        coef,
        inner_logs,
        *earlier,
        scratch=[pltpu.VMEM((REACH, SUB, lat), jnp.float32)],
    )
    inverses.append(inverse)
    other = lax.ppermute(logs, "mem", [(0, 1), (1, 0)])
    merged, payload = call(merge_kernel, (packed, shape(tiles, 1, 128)), logs, other, mass, coef)
    got = lax.all_to_all(payload, "tile", split_axis=0, concat_axis=0)
    barycenter, updated = call(
        partial(finish_kernel, float(cells)),
        (shape(levels, lon, lat), shape(rows * lon, lat)),
        got,
        merged,
        *inverses,
        scratch=[pltpu.VMEM((rows * lon, lat), jnp.float32), pltpu.SemaphoreType.DMA((rows // SUB,))],
        out_specs=(VMEM, HBM),
    )
    return barycenter, updated.reshape(members, levels, lon, lat)


def solution(mesh):
    return jax.shard_map(
        body,
        mesh=mesh,
        in_specs=(
            P("mem", None, "tile", None),
            P("mem", None, "tile", None),
            P("mem"),
            P("tile", None),
        ),
        out_specs=(P(None, "tile", None), P("mem", None, "tile", None)),
        check_vma=False,
    )
```

```python
import math
from functools import partial

import jax
import jax.numpy as jnp
import numpy as np
from jax import lax
from jax.experimental import pallas as pl
from jax.experimental.pallas import tpu as pltpu
from jax.sharding import PartitionSpec as P

BACKGROUND = 0.01
REACH = 4
SUB = 8
VMEM = pl.BlockSpec(memory_space=pltpu.VMEM)
HBM = pl.BlockSpec(memory_space=pl.ANY)
AREA, ZONAL, NORTH, SOUTH, CENTER = range(5)


def coefficients(lat_cells):
    spacing = math.pi / lat_cells
    index = np.arange(lat_cells)
    latitude = -0.5 * math.pi + (index + 0.5) * spacing
    cell_area = np.cos(latitude)
    zonal = 0.2 * np.minimum(2.2, 1.0 / cell_area**2)
    north = np.where(index == lat_cells - 1, 0.0, 0.05 * np.cos(latitude + 0.5 * spacing) / cell_area)
    south = np.where(index == 0, 0.0, 0.05 * np.cos(latitude - 0.5 * spacing) / cell_area)
    center = 1.0 - 2.0 * zonal - north - south
    rows = np.stack([cell_area, zonal, north, south, center]).astype(np.float32)
    return np.ascontiguousarray(np.broadcast_to(rows[:, None, :], (5, SUB, lat_cells)))


def params(mib=20):
    return pltpu.CompilerParams(vmem_limit_bytes=mib * 2**20)


def rows_of(group):
    return pl.ds(group * SUB, SUB)


def block_of(group):
    return pl.ds(group * SUB * SUB, SUB * SUB)


def batches(last, first=0, size=4):
    return [range(start, min(start + size, last)) for start in range(first, last, size)]


def chunk_groups(groups):
    half = (groups + 1) // 2
    last = max(1, (groups - half) // 3)
    return [[half], [groups - half - last, last]]


class Chunked:
    def __init__(self, refs):
        self.refs = refs

    def stack(self, group, order=range(REACH)):
        for ref in self.refs:
            held = ref.shape[1] // SUB
            if group < held:
                return stack_of(ref, group, order)
            group -= held

    def put(self, group, values):
        for ref in self.refs:
            held = ref.shape[1] // SUB
            if 0 <= group < held:
                for c, value in enumerate(values):
                    ref[c, rows_of(group), :] = value
            group -= held


def by_longitude(block, lat):
    return jnp.swapaxes(block.reshape(SUB, SUB, lat), 0, 1)


def stack_of(ref, group, order=range(REACH)):
    return [ref[c, rows_of(group), :] for c in order]


def odd_core():
    return lax.rem(lax.axis_index("tile"), 2) == 1


def from_outside(columns, odd):
    last = len(columns) - 1
    return [jnp.where(odd, columns[last - c], columns[c]) for c in range(len(columns))]


def spread_kernel(scaling_ref, coef_ref, inner_ref, *outer_refs):
    groups, lat = inner_ref.shape[1] // SUB, inner_ref.shape[2]
    odd = odd_core()
    outer = Chunked(outer_refs)
    for group in range(groups):
        columns = from_outside(by_longitude(scaling_ref[block_of(group), :], lat), odd)
        columns = [column * coef_ref[AREA] for column in columns]
        outer.put(group, columns[:REACH])
        for c in range(REACH):
            inner_ref[c, rows_of(group), :] = columns[c + REACH]


def lane_fold(value):
    lat = value.shape[-1]
    total = value[:, :128]
    for t in range(1, lat // 128):
        total = total + value[:, t * 128 : (t + 1) * 128]
    return total


def diffuse(columns, coef_ref):
    lat = columns[0].shape[-1]
    return [
        coef_ref[CENTER] * here
        + coef_ref[ZONAL] * (west + east)
        + coef_ref[NORTH] * pltpu.roll(here, lat - 1, 1)
        + coef_ref[SOUTH] * pltpu.roll(here, 1, 1)
        for west, here, east in zip(columns[:-2], columns[1:-1], columns[2:])
    ]


def inner_half(batch, halo_ref, inner_ref, outer_refs, coef_ref, edge_ref):
    outer = Chunked(outer_refs)
    columns = [outer.stack(g) + stack_of(inner_ref, g) + stack_of(halo_ref, g, (3, 2, 1, 0)) for g in batch]
    for s in range(REACH):
        columns = [diffuse(own, coef_ref) for own in columns]
        if s < REACH - 1:
            for own, group in zip(columns, batch):
                edge_ref[2 * s, rows_of(group), :] = own[0]
                edge_ref[2 * s + 1, rows_of(group), :] = own[1]
    return zip(batch, columns)


def outer_half(batch, first, halo_ref, outer_ref, edge_ref, coef_ref):
    columns = [stack_of(halo_ref, g - first, (3, 2, 1, 0)) + stack_of(outer_ref, g - first, (0, 1)) for g in batch]
    for s in range(REACH):
        columns = [diffuse(own, coef_ref) for own in columns]
        if s < REACH - 1:
            columns = [own + stack_of(edge_ref, g, (2 * s, 2 * s + 1)) for own, g in zip(columns, batch)]
    return zip(batch, columns)


def smooth_inner_kernel(
    halo_ref, inner_ref, fields_ref, mask_ref, coef_ref, *refs
):
    *outer_refs, out_ref, edge_ref, filled_ref, mass_ref = refs
    groups, lat = inner_ref.shape[1] // SUB, inner_ref.shape[2]
    odd = odd_core()
    for batch in batches(groups):
        for group, smoothed in inner_half(batch, halo_ref, inner_ref, outer_refs, coef_ref, edge_ref):
            fields = by_longitude(fields_ref[block_of(group), :], lat)
            filled = []
            for c in range(2 * REACH):
                valid = jnp.broadcast_to(mask_ref[c : c + 1, :], (SUB, lat)) == 1
                filled.append((jnp.where(valid, fields[c], 0.0) + BACKGROUND) * coef_ref[AREA])
            mass_ref[rows_of(group), :] = lane_fold(sum(filled))
            filled = from_outside(filled, odd)
            for c in range(REACH):
                filled_ref[c, rows_of(group), :] = filled[c]
                out_ref[c, rows_of(group), :] = filled[c + REACH] / smoothed[c]


def smooth_outer_kernel(first, halo_ref, outer_ref, edge_ref, filled_ref, coef_ref, *out_refs):
    last = first + outer_ref.shape[1] // SUB
    out = Chunked(out_refs)
    for batch in batches(last, first):
        for group, smoothed in outer_half(batch, first, halo_ref, outer_ref, edge_ref, coef_ref):
            filled = stack_of(filled_ref, group)
            out.put(group - first, [top / bottom for top, bottom in zip(filled, smoothed)])


def low_half(shape):
    return lax.broadcasted_iota(jnp.int32, shape, 0) < SUB // 2


def add_logs(group, held, result, scaled, weight_ref, inverse_ref, total_ref):
    lat = total_ref.shape[2]
    weight = jnp.broadcast_to(weight_ref[rows_of(group), :1], (SUB, lat))
    for c in range(REACH):
        inverse_ref[c, rows_of(held), :] = 1.0 / result[c]
        total_ref[c] = total_ref[c] + weight * jnp.log(scaled[c] * result[c])


def return_inner_kernel(halo_ref, inner_ref, scaled_ref, weight_ref, coef_ref, *refs):
    *outer_refs, inverse_ref, edge_ref, total_ref = refs
    groups = inner_ref.shape[1] // SUB
    total_ref[...] = jnp.zeros_like(total_ref)
    for batch in batches(groups):
        for group, result in inner_half(batch, halo_ref, inner_ref, outer_refs, coef_ref, edge_ref):
            add_logs(group, group, result, stack_of(scaled_ref, group), weight_ref, inverse_ref, total_ref)


def return_outer_kernel(
    base, first, halo_ref, outer_ref, edge_ref, scaled_ref, weight_ref, coef_ref, inverse_ref, total_ref
):
    last = first + outer_ref.shape[1] // SUB
    total_ref[...] = jnp.zeros_like(total_ref)
    for batch in batches(last, first):
        for group, result in outer_half(batch, first, halo_ref, outer_ref, edge_ref, coef_ref):
            scaled = stack_of(scaled_ref, group - base)
            add_logs(group, group - first, result, scaled, weight_ref, inverse_ref, total_ref)


def last_return_kernel(
    base,
    first,
    halo_ref,
    outer_ref,
    edge_ref,
    scaled_ref,
    weight_ref,
    coef_ref,
    inner_ref,
    *refs,
):
    *earlier_refs, inverse_ref, logs_ref, total_ref = refs
    return_outer_kernel(
        base, first, halo_ref, outer_ref, edge_ref, scaled_ref, weight_ref, coef_ref, inverse_ref, total_ref
    )
    low = low_half(total_ref.shape[1:])
    tiles = total_ref.shape[2] // 128
    for c in range(REACH):
        outer, inner = sum((ref[c] for ref in earlier_refs), total_ref[c]), inner_ref[c]
        outer = outer + pltpu.roll(outer, SUB // 2, 0)
        inner = inner + pltpu.roll(inner, SUB // 2, 0)
        both = jnp.where(low, outer, inner)
        for t in range(tiles):
            logs_ref[rows_of(c * tiles + t), :] = both[:, t * 128 : (t + 1) * 128]
    count = jnp.sum(weight_ref[...], axis=0, keepdims=True) * (1.0 / (SUB // 2))
    logs_ref[rows_of(REACH * tiles), :] = jnp.broadcast_to(count, (SUB, 128))


def merge_kernel(own_ref, other_ref, mass_ref, coef_ref, merged_ref, payload_ref):
    members, tiles = mass_ref.shape[0], merged_ref.shape[2] // 128
    both = lambda n: own_ref[rows_of(n), :] + other_ref[rows_of(n), :]
    scale = 1.0 / both(REACH * tiles)
    level = jnp.zeros((SUB, 128), jnp.float32)
    for c in range(REACH):
        for t in range(tiles):
            span = slice(t * 128, (t + 1) * 128)
            weighted = jnp.exp(both(c * tiles + t) * scale)
            merged_ref[c, :, span] = weighted / coef_ref[AREA, :, span]
            level = level + weighted
    level = level + pltpu.roll(level, SUB // 2, 0)
    spare = jnp.zeros((128 - members - SUB, 128), jnp.float32)
    table = jnp.concatenate([mass_ref[...], level, spare], axis=0)
    row = jnp.sum(table.T, axis=0, keepdims=True)
    payload_ref[...] = jnp.broadcast_to(row[None], payload_ref.shape)


def finish_kernel(cells, got_ref, merged_ref, inner_ref, *refs):
    *outer_refs, bary_ref, updated_ref, staged_ref, sem = refs
    members, lat = inner_ref.shape[1:]
    groups = members // SUB
    odd = odd_core()
    total = jnp.sum(got_ref[...], axis=0)
    table = jnp.broadcast_to(total, (128, 128)).T
    level = table[members : members + SUB, :]
    low = low_half((SUB, lat))
    wide = lambda v: jnp.concatenate([v] * (lat // 128), axis=1)
    inverse = wide(cells / level)
    outer, inner = [], []
    for c in range(REACH):
        both = merged_ref[c] * inverse
        swapped = pltpu.roll(both, SUB // 2, 0)
        outer.append(jnp.where(low, both, swapped))
        inner.append(jnp.where(low, swapped, both))
    bary = from_outside(outer + inner, odd)
    bary_ref[...] = jnp.swapaxes(jnp.stack(bary), 0, 1)[: SUB // 2]
    for group in range(groups):
        rows = slice(group * SUB, (group + 1) * SUB)
        factor = wide(table[rows, :] / cells)
        quotients = Chunked(outer_refs).stack(group) + stack_of(inner_ref, group)
        out = [b * factor * quotient for b, quotient in zip(bary, from_outside(quotients, odd))]
        span = pl.ds(group * SUB * SUB, SUB * SUB)
        staged_ref[span, :] = jnp.swapaxes(jnp.stack(out), 0, 1).reshape(SUB * SUB, lat)
        pltpu.make_async_copy(staged_ref.at[span, :], updated_ref.at[span, :], sem.at[group]).start()
    for group in range(groups):
        span = pl.ds(group * SUB * SUB, SUB * SUB)
        pltpu.make_async_copy(staged_ref.at[span, :], updated_ref.at[span, :], sem.at[group]).wait()


def shape(*dims):
    return jax.ShapeDtypeStruct(dims, jnp.float32)


def call(kernel, outs, *args, scratch=(), out_specs=None):
    return pl.pallas_call(
        kernel,
        out_shape=outs,
        in_specs=[VMEM] * len(args),
        out_specs=out_specs or (VMEM,) * len(outs),
        scratch_shapes=scratch,
        compiler_params=params(),
    )(*args)


def body(fields, scaling, counts, land_mask):
    members, levels, lon, lat = fields.shape
    tiles = lax.axis_size("tile")
    rows = members * levels
    cells = lon * tiles * lat
    half = shape(REACH, rows, lat)
    edge = shape(2 * REACH - 2, rows, lat)
    packed = shape(REACH, SUB, lat)
    chunks = chunk_groups(rows // SUB)
    bases = [sum(map(sum, chunks[:n])) for n in range(len(chunks))]
    parts = [shape(REACH, sum(own) * SUB, lat) for own in chunks]
    coef = jnp.asarray(coefficients(lat))
    with_mate = [(i, i ^ 1) for i in range(tiles)]
    with_neighbour = [(i, (i + (1 if i % 2 else -1)) % tiles) for i in range(tiles)]
    scaling = scaling.reshape(rows * lon, lat)
    fields = fields.reshape(rows * lon, lat)
    weights = counts.astype(jnp.float32)
    weight_rows = jnp.broadcast_to(jnp.repeat(weights, levels)[:, None], (rows, 128))

    inner, *outer = call(spread_kernel, (half, *parts), scaling, coef)
    outer_halo = [lax.ppermute(part, "tile", with_neighbour) for part in outer]
    inner_halo = lax.ppermute(inner, "tile", with_mate)
    v_inner, edges, filled, mass = call(
        smooth_inner_kernel, (half, edge, half, shape(rows, 128)), inner_halo, inner, fields, land_mask, coef, *outer
    )
    v_inner_halo = lax.ppermute(v_inner, "tile", with_mate)
    v_outer, v_outer_halo, places = [], [], []
    for base, sizes, halo, own in zip(bases, chunks, outer_halo, outer):
        outs = tuple(shape(REACH, size * SUB, lat) for size in sizes)
        values = call(partial(smooth_outer_kernel, base), outs, halo, own, edges, filled, coef)
        v_outer += values
        v_outer_halo += [lax.ppermute(value, "tile", with_neighbour) for value in values]
        places += [(base, base + sum(sizes[:n]), own) for n in range(len(sizes))]
    inverse_inner, edges, inner_logs = call(
        return_inner_kernel, (half, edge, packed), v_inner_halo, v_inner, inner, weight_rows, coef, *v_outer
    )
    inverses, earlier = [inverse_inner], []
    for n, (base, first, own) in enumerate(places):
        operands = v_outer_halo[n], v_outer[n], edges, own, weight_rows, coef
        part = shape(*v_outer[n].shape)
        if n < len(places) - 1:
            inverse, logs = call(partial(return_outer_kernel, base, first), (part, packed), *operands)
            earlier.append(logs)
        else:
            inverse, logs = call(
                partial(last_return_kernel, base, first),
                (part, shape((REACH * lat // 128 + 1) * SUB, 128)),
                *operands,
                inner_logs,
                *earlier,
                scratch=[pltpu.VMEM((REACH, SUB, lat), jnp.float32)],
            )
        inverses.append(inverse)
    other = lax.ppermute(logs, "mem", [(0, 1), (1, 0)])
    merged, payload = call(merge_kernel, (packed, shape(tiles, 1, 128)), logs, other, mass, coef)
    got = lax.all_to_all(payload, "tile", split_axis=0, concat_axis=0)
    barycenter, updated = call(
        partial(finish_kernel, float(cells)),
        (shape(levels, lon, lat), shape(rows * lon, lat)),
        got,
        merged,
        *inverses,
        scratch=[pltpu.VMEM((rows * lon, lat), jnp.float32), pltpu.SemaphoreType.DMA((rows // SUB,))],
        out_specs=(VMEM, HBM),
    )
    return barycenter, updated.reshape(members, levels, lon, lat)


def solution(mesh):
    return jax.shard_map(
        body,
        mesh=mesh,
        in_specs=(
            P("mem", None, "tile", None),
            P("mem", None, "tile", None),
            P("mem"),
            P("tile", None),
        ),
        out_specs=(P(None, "tile", None), P("mem", None, "tile", None)),
        check_vma=False,
    )
```

```python
import math
from functools import partial

import jax
import jax.numpy as jnp
import numpy as np
from jax import lax
from jax.experimental import pallas as pl
from jax.experimental.pallas import tpu as pltpu
from jax.sharding import PartitionSpec as P

BACKGROUND = 0.01
REACH = 4
SUB = 8
VMEM = pl.BlockSpec(memory_space=pltpu.VMEM)
HBM = pl.BlockSpec(memory_space=pl.ANY)
AREA, ZONAL, NORTH, SOUTH, CENTER = range(5)


def coefficients(lat_cells):
    spacing = math.pi / lat_cells
    index = np.arange(lat_cells)
    latitude = -0.5 * math.pi + (index + 0.5) * spacing
    cell_area = np.cos(latitude)
    zonal = 0.2 * np.minimum(2.2, 1.0 / cell_area**2)
    north = np.where(index == lat_cells - 1, 0.0, 0.05 * np.cos(latitude + 0.5 * spacing) / cell_area)
    south = np.where(index == 0, 0.0, 0.05 * np.cos(latitude - 0.5 * spacing) / cell_area)
    center = 1.0 - 2.0 * zonal - north - south
    rows = np.stack([cell_area, zonal, north, south, center]).astype(np.float32)
    return np.ascontiguousarray(np.broadcast_to(rows[:, None, :], (5, SUB, lat_cells)))


def params(mib=20):
    return pltpu.CompilerParams(vmem_limit_bytes=mib * 2**20)


def rows_of(group):
    return pl.ds(group * SUB, SUB)


def block_of(group):
    return pl.ds(group * SUB * SUB, SUB * SUB)


def batches(last, first=0, size=4):
    return [range(start, min(start + size, last)) for start in range(first, last, size)]


def chunk_groups(groups):
    half = (groups + 1) // 2
    last = max(1, (groups - half) // 3)
    return [[half], [groups - half - last, last]]


class Chunked:
    def __init__(self, refs):
        self.refs = refs

    def stack(self, group, order=range(REACH)):
        for ref in self.refs:
            held = ref.shape[1] // SUB
            if group < held:
                return stack_of(ref, group, order)
            group -= held

    def put(self, group, values):
        for ref in self.refs:
            held = ref.shape[1] // SUB
            if 0 <= group < held:
                for c, value in enumerate(values):
                    ref[c, rows_of(group), :] = value
            group -= held


def by_longitude(block, lat):
    return jnp.swapaxes(block.reshape(SUB, SUB, lat), 0, 1)


def stack_of(ref, group, order=range(REACH)):
    return [ref[c, rows_of(group), :] for c in order]


def odd_core():
    return lax.rem(lax.axis_index("tile"), 2) == 1


def from_outside(columns, odd):
    last = len(columns) - 1
    return [jnp.where(odd, columns[last - c], columns[c]) for c in range(len(columns))]


def spread_kernel(scaling_ref, coef_ref, inner_ref, *outer_refs):
    groups, lat = inner_ref.shape[1] // SUB, inner_ref.shape[2]
    odd = odd_core()
    outer = Chunked(outer_refs)
    for group in range(groups):
        columns = from_outside(by_longitude(scaling_ref[block_of(group), :], lat), odd)
        columns = [column * coef_ref[AREA] for column in columns]
        outer.put(group, columns[:REACH])
        for c in range(REACH):
            inner_ref[c, rows_of(group), :] = columns[c + REACH]


def lane_fold(value):
    lat = value.shape[-1]
    total = value[:, :128]
    for t in range(1, lat // 128):
        total = total + value[:, t * 128 : (t + 1) * 128]
    return total


def diffuse(columns, coef_ref):
    lat = columns[0].shape[-1]
    return [
        coef_ref[CENTER] * here
        + coef_ref[ZONAL] * (west + east)
        + coef_ref[NORTH] * pltpu.roll(here, lat - 1, 1)
        + coef_ref[SOUTH] * pltpu.roll(here, 1, 1)
        for west, here, east in zip(columns[:-2], columns[1:-1], columns[2:])
    ]


def inner_half(batch, halo_ref, inner_ref, outer_refs, coef_ref, edge_ref):
    outer = Chunked(outer_refs)
    columns = [outer.stack(g) + stack_of(inner_ref, g) + stack_of(halo_ref, g, (3, 2, 1, 0)) for g in batch]
    for s in range(REACH):
        columns = [diffuse(own, coef_ref) for own in columns]
        if s < REACH - 1:
            for own, group in zip(columns, batch):
                edge_ref[2 * s, rows_of(group), :] = own[0]
                edge_ref[2 * s + 1, rows_of(group), :] = own[1]
    return zip(batch, columns)


def outer_half(batch, first, halo_ref, outer_ref, edge_ref, coef_ref):
    columns = [stack_of(halo_ref, g - first, (3, 2, 1, 0)) + stack_of(outer_ref, g - first, (0, 1)) for g in batch]
    for s in range(REACH):
        columns = [diffuse(own, coef_ref) for own in columns]
        if s < REACH - 1:
            columns = [own + stack_of(edge_ref, g, (2 * s, 2 * s + 1)) for own, g in zip(columns, batch)]
    return zip(batch, columns)


def smooth_inner_kernel(
    halo_ref, inner_ref, fields_ref, mask_ref, coef_ref, *refs
):
    *outer_refs, out_ref, edge_ref, filled_ref, mass_ref = refs
    groups, lat = inner_ref.shape[1] // SUB, inner_ref.shape[2]
    odd = odd_core()
    for batch in batches(groups):
        for group, smoothed in inner_half(batch, halo_ref, inner_ref, outer_refs, coef_ref, edge_ref):
            fields = by_longitude(fields_ref[block_of(group), :], lat)
            filled = []
            for c in range(2 * REACH):
                valid = jnp.broadcast_to(mask_ref[c : c + 1, :], (SUB, lat)) == 1
                filled.append((jnp.where(valid, fields[c], 0.0) + BACKGROUND) * coef_ref[AREA])
            mass_ref[rows_of(group), :] = lane_fold(sum(filled))
            filled = from_outside(filled, odd)
            for c in range(REACH):
                filled_ref[c, rows_of(group), :] = filled[c]
                out_ref[c, rows_of(group), :] = filled[c + REACH] / smoothed[c]


def smooth_outer_kernel(first, halo_ref, outer_ref, edge_ref, filled_ref, coef_ref, *out_refs):
    last = first + outer_ref.shape[1] // SUB
    out = Chunked(out_refs)
    for batch in batches(last, first):
        for group, smoothed in outer_half(batch, first, halo_ref, outer_ref, edge_ref, coef_ref):
            filled = stack_of(filled_ref, group)
            out.put(group - first, [top / bottom for top, bottom in zip(filled, smoothed)])


def low_half(shape):
    return lax.broadcasted_iota(jnp.int32, shape, 0) < SUB // 2


def add_logs(group, held, result, scaled, weight_ref, inverse_ref, total_ref):
    lat = total_ref.shape[2]
    weight = jnp.broadcast_to(weight_ref[rows_of(group), :1], (SUB, lat))
    for c in range(REACH):
        inverse_ref[c, rows_of(held), :] = 1.0 / result[c]
        total_ref[c] = total_ref[c] + weight * jnp.log(scaled[c] * result[c])


def return_inner_kernel(halo_ref, inner_ref, scaled_ref, weight_ref, coef_ref, *refs):
    *outer_refs, inverse_ref, edge_ref, total_ref = refs
    groups = inner_ref.shape[1] // SUB
    total_ref[...] = jnp.zeros_like(total_ref)
    for batch in batches(groups):
        for group, result in inner_half(batch, halo_ref, inner_ref, outer_refs, coef_ref, edge_ref):
            add_logs(group, group, result, stack_of(scaled_ref, group), weight_ref, inverse_ref, total_ref)


def return_outer_kernel(
    base, first, halo_ref, outer_ref, edge_ref, scaled_ref, weight_ref, coef_ref, inverse_ref, total_ref
):
    last = first + outer_ref.shape[1] // SUB
    total_ref[...] = jnp.zeros_like(total_ref)
    for batch in batches(last, first):
        for group, result in outer_half(batch, first, halo_ref, outer_ref, edge_ref, coef_ref):
            scaled = stack_of(scaled_ref, group - base)
            add_logs(group, group - first, result, scaled, weight_ref, inverse_ref, total_ref)


def last_return_kernel(
    base,
    first,
    halo_ref,
    outer_ref,
    edge_ref,
    scaled_ref,
    weight_ref,
    coef_ref,
    inner_ref,
    *refs,
):
    *earlier_refs, inverse_ref, logs_ref, total_ref = refs
    return_outer_kernel(
        base, first, halo_ref, outer_ref, edge_ref, scaled_ref, weight_ref, coef_ref, inverse_ref, total_ref
    )
    low = low_half(total_ref.shape[1:])
    tiles = total_ref.shape[2] // 128
    for c in range(REACH):
        outer, inner = sum((ref[c] for ref in earlier_refs), total_ref[c]), inner_ref[c]
        outer = outer + pltpu.roll(outer, SUB // 2, 0)
        inner = inner + pltpu.roll(inner, SUB // 2, 0)
        both = jnp.where(low, outer, inner)
        for t in range(tiles):
            logs_ref[rows_of(c * tiles + t), :] = both[:, t * 128 : (t + 1) * 128]
    count = jnp.sum(weight_ref[...], axis=0, keepdims=True) * (1.0 / (SUB // 2))
    logs_ref[rows_of(REACH * tiles), :] = jnp.broadcast_to(count, (SUB, 128))


def merge_kernel(own_ref, other_ref, mass_ref, coef_ref, merged_ref, payload_ref):
    members, tiles = mass_ref.shape[0], merged_ref.shape[2] // 128
    both = lambda n: own_ref[rows_of(n), :] + other_ref[rows_of(n), :]
    scale = 1.0 / both(REACH * tiles)
    level = jnp.zeros((SUB, 128), jnp.float32)
    for c in range(REACH):
        for t in range(tiles):
            span = slice(t * 128, (t + 1) * 128)
            weighted = jnp.exp(both(c * tiles + t) * scale)
            merged_ref[c, :, span] = weighted / coef_ref[AREA, :, span]
            level = level + weighted
    level = level + pltpu.roll(level, SUB // 2, 0)
    spare = jnp.zeros((128 - members - SUB, 128), jnp.float32)
    table = jnp.concatenate([mass_ref[...], level, spare], axis=0)
    row = jnp.sum(table.T, axis=0, keepdims=True)
    payload_ref[...] = jnp.broadcast_to(row[None], payload_ref.shape)


def finish_kernel(cells, got_ref, merged_ref, inner_ref, *refs):
    *outer_refs, bary_ref, updated_ref, staged_ref, sem = refs
    members, lat = inner_ref.shape[1:]
    groups = members // SUB
    odd = odd_core()
    total = jnp.sum(got_ref[...], axis=0)
    table = jnp.broadcast_to(total, (128, 128)).T
    level = table[members : members + SUB, :]
    low = low_half((SUB, lat))
    wide = lambda v: jnp.concatenate([v] * (lat // 128), axis=1)
    inverse = wide(cells / level)
    outer, inner = [], []
    for c in range(REACH):
        both = merged_ref[c] * inverse
        swapped = pltpu.roll(both, SUB // 2, 0)
        outer.append(jnp.where(low, both, swapped))
        inner.append(jnp.where(low, swapped, both))
    bary = from_outside(outer + inner, odd)
    bary_ref[...] = jnp.swapaxes(jnp.stack(bary), 0, 1)[: SUB // 2]
    for group in range(groups):
        rows = slice(group * SUB, (group + 1) * SUB)
        factor = wide(table[rows, :] / cells)
        quotients = Chunked(outer_refs).stack(group) + stack_of(inner_ref, group)
        out = [b * factor * quotient for b, quotient in zip(bary, from_outside(quotients, odd))]
        span = pl.ds(group * SUB * SUB, SUB * SUB)
        staged_ref[span, :] = jnp.swapaxes(jnp.stack(out), 0, 1).reshape(SUB * SUB, lat)
        pltpu.make_async_copy(staged_ref.at[span, :], updated_ref.at[span, :], sem.at[group]).start()
    for group in range(groups):
        span = pl.ds(group * SUB * SUB, SUB * SUB)
        pltpu.make_async_copy(staged_ref.at[span, :], updated_ref.at[span, :], sem.at[group]).wait()


def shape(*dims):
    return jax.ShapeDtypeStruct(dims, jnp.float32)


def call(kernel, outs, *args, scratch=(), out_specs=None):
    return pl.pallas_call(
        kernel,
        out_shape=outs,
        in_specs=[VMEM] * len(args),
        out_specs=out_specs or (VMEM,) * len(outs),
        scratch_shapes=scratch,
        compiler_params=params(),
    )(*args)


def body(fields, scaling, counts, land_mask):
    members, levels, lon, lat = fields.shape
    tiles = lax.axis_size("tile")
    rows = members * levels
    cells = lon * tiles * lat
    half = shape(REACH, rows, lat)
    edge = shape(2 * REACH - 2, rows, lat)
    packed = shape(REACH, SUB, lat)
    chunks = chunk_groups(rows // SUB)
    bases = [sum(map(sum, chunks[:n])) for n in range(len(chunks))]
    parts = [shape(REACH, sum(own) * SUB, lat) for own in chunks]
    coef = jnp.asarray(coefficients(lat))
    with_mate = [(i, i ^ 1) for i in range(tiles)]
    with_neighbour = [(i, (i + (1 if i % 2 else -1)) % tiles) for i in range(tiles)]
    scaling = scaling.reshape(rows * lon, lat)
    fields = fields.reshape(rows * lon, lat)
    weights = counts.astype(jnp.float32)
    weight_rows = jnp.broadcast_to(jnp.repeat(weights, levels)[:, None], (rows, 128))

    inner, *outer = call(spread_kernel, (half, *parts), scaling, coef)
    outer_halo = [lax.ppermute(part, "tile", with_neighbour) for part in outer]
    inner_halo = lax.ppermute(inner, "tile", with_mate)
    v_inner, edges, filled, mass = call(
        smooth_inner_kernel, (half, edge, half, shape(rows, 128)), inner_halo, inner, fields, land_mask, coef, *outer
    )
    v_outer, v_outer_halo, places = [], [], []
    for base, sizes, halo, own in zip(bases, chunks, outer_halo, outer):
        outs = tuple(shape(REACH, size * SUB, lat) for size in sizes)
        values = call(partial(smooth_outer_kernel, base), outs, halo, own, edges, filled, coef)
        if not v_outer:
            v_inner, *values = lax.optimization_barrier((v_inner, *values))
            v_inner_halo = lax.ppermute(v_inner, "tile", with_mate)
            v_inner_halo, *values = lax.optimization_barrier((v_inner_halo, *values))
        v_outer += values
        v_outer_halo += [lax.ppermute(value, "tile", with_neighbour) for value in values]
        places += [(base, base + sum(sizes[:n]), own) for n in range(len(sizes))]
    inverse_inner, edges, inner_logs = call(
        return_inner_kernel, (half, edge, packed), v_inner_halo, v_inner, inner, weight_rows, coef, *v_outer
    )
    inverses, earlier = [inverse_inner], []
    for n, (base, first, own) in enumerate(places):
        if earlier:
            v_outer_halo[n], earlier[-1] = lax.optimization_barrier((v_outer_halo[n], earlier[-1]))
        operands = v_outer_halo[n], v_outer[n], edges, own, weight_rows, coef
        part = shape(*v_outer[n].shape)
        if n < len(places) - 1:
            inverse, logs = call(partial(return_outer_kernel, base, first), (part, packed), *operands)
            earlier.append(logs)
        else:
            inverse, logs = call(
                partial(last_return_kernel, base, first),
                (part, shape((REACH * lat // 128 + 1) * SUB, 128)),
                *operands,
                inner_logs,
                *earlier,
                scratch=[pltpu.VMEM((REACH, SUB, lat), jnp.float32)],
            )
        inverses.append(inverse)
    other = lax.ppermute(logs, "mem", [(0, 1), (1, 0)])
    merged, payload = call(merge_kernel, (packed, shape(tiles, 1, 128)), logs, other, mass, coef)
    got = lax.all_to_all(payload, "tile", split_axis=0, concat_axis=0)
    barycenter, updated = call(
        partial(finish_kernel, float(cells)),
        (shape(levels, lon, lat), shape(rows * lon, lat)),
        got,
        merged,
        *inverses,
        scratch=[pltpu.VMEM((rows * lon, lat), jnp.float32), pltpu.SemaphoreType.DMA((rows // SUB,))],
        out_specs=(VMEM, HBM),
    )
    return barycenter, updated.reshape(members, levels, lon, lat)


def solution(mesh):
    return jax.shard_map(
        body,
        mesh=mesh,
        in_specs=(
            P("mem", None, "tile", None),
            P("mem", None, "tile", None),
            P("mem"),
            P("tile", None),
        ),
        out_specs=(P(None, "tile", None), P("mem", None, "tile", None)),
        check_vma=False,
    )
```

```python
import math
from functools import partial

import jax
import jax.numpy as jnp
import numpy as np
from jax import lax
from jax.experimental import pallas as pl
from jax.experimental.pallas import tpu as pltpu
from jax.sharding import PartitionSpec as P

BACKGROUND = 0.01
REACH = 4
SUB = 8
VMEM = pl.BlockSpec(memory_space=pltpu.VMEM)
HBM = pl.BlockSpec(memory_space=pl.ANY)
AREA, ZONAL, NORTH, SOUTH, CENTER = range(5)


def coefficients(lat_cells):
    spacing = math.pi / lat_cells
    index = np.arange(lat_cells)
    latitude = -0.5 * math.pi + (index + 0.5) * spacing
    cell_area = np.cos(latitude)
    zonal = 0.2 * np.minimum(2.2, 1.0 / cell_area**2)
    north = np.where(index == lat_cells - 1, 0.0, 0.05 * np.cos(latitude + 0.5 * spacing) / cell_area)
    south = np.where(index == 0, 0.0, 0.05 * np.cos(latitude - 0.5 * spacing) / cell_area)
    center = 1.0 - 2.0 * zonal - north - south
    rows = np.stack([cell_area, zonal, north, south, center]).astype(np.float32)
    return np.ascontiguousarray(np.broadcast_to(rows[:, None, :], (5, SUB, lat_cells)))


def params(mib=20):
    return pltpu.CompilerParams(vmem_limit_bytes=mib * 2**20)


def rows_of(group):
    return pl.ds(group * SUB, SUB)


def block_of(group):
    return pl.ds(group * SUB * SUB, SUB * SUB)


def batches(last, first=0, size=4):
    return [range(start, min(start + size, last)) for start in range(first, last, size)]


def chunk_groups(groups):
    half = (groups + 1) // 2
    last = max(1, (groups - half) // 3)
    return [[half], [groups - half - last, last]]


class Chunked:
    def __init__(self, refs):
        self.refs = refs

    def stack(self, group, order=range(REACH)):
        for ref in self.refs:
            held = ref.shape[1] // SUB
            if group < held:
                return stack_of(ref, group, order)
            group -= held

    def put(self, group, values):
        for ref in self.refs:
            held = ref.shape[1] // SUB
            if 0 <= group < held:
                for c, value in enumerate(values):
                    ref[c, rows_of(group), :] = value
            group -= held


def by_longitude(block, lat):
    return jnp.swapaxes(block.reshape(SUB, SUB, lat), 0, 1)


def stack_of(ref, group, order=range(REACH)):
    return [ref[c, rows_of(group), :] for c in order]


def odd_core():
    return lax.rem(lax.axis_index("tile"), 2) == 1


def from_outside(columns, odd):
    last = len(columns) - 1
    return [jnp.where(odd, columns[last - c], columns[c]) for c in range(len(columns))]


def spread_kernel(scaling_ref, coef_ref, inner_ref, *outer_refs):
    groups, lat = inner_ref.shape[1] // SUB, inner_ref.shape[2]
    odd = odd_core()
    outer = Chunked(outer_refs)
    for group in range(groups):
        columns = from_outside(by_longitude(scaling_ref[block_of(group), :], lat), odd)
        columns = [column * coef_ref[AREA] for column in columns]
        outer.put(group, columns[:REACH])
        for c in range(REACH):
            inner_ref[c, rows_of(group), :] = columns[c + REACH]


def lane_fold(value):
    lat = value.shape[-1]
    total = value[:, :128]
    for t in range(1, lat // 128):
        total = total + value[:, t * 128 : (t + 1) * 128]
    return total


def diffuse(columns, coef_ref):
    lat = columns[0].shape[-1]
    return [
        coef_ref[CENTER] * here
        + coef_ref[ZONAL] * (west + east)
        + coef_ref[NORTH] * pltpu.roll(here, lat - 1, 1)
        + coef_ref[SOUTH] * pltpu.roll(here, 1, 1)
        for west, here, east in zip(columns[:-2], columns[1:-1], columns[2:])
    ]


def inner_half(batch, halo_ref, inner_ref, outer_refs, coef_ref, edge_ref):
    outer = Chunked(outer_refs)
    columns = [outer.stack(g) + stack_of(inner_ref, g) + stack_of(halo_ref, g, (3, 2, 1, 0)) for g in batch]
    for s in range(REACH):
        columns = [diffuse(own, coef_ref) for own in columns]
        if s < REACH - 1:
            for own, group in zip(columns, batch):
                edge_ref[2 * s, rows_of(group), :] = own[0]
                edge_ref[2 * s + 1, rows_of(group), :] = own[1]
    return zip(batch, columns)


def outer_half(batch, first, halo_ref, outer_ref, edge_ref, coef_ref):
    columns = [stack_of(halo_ref, g - first, (3, 2, 1, 0)) + stack_of(outer_ref, g - first, (0, 1)) for g in batch]
    for s in range(REACH):
        columns = [diffuse(own, coef_ref) for own in columns]
        if s < REACH - 1:
            columns = [own + stack_of(edge_ref, g, (2 * s, 2 * s + 1)) for own, g in zip(columns, batch)]
    return zip(batch, columns)


def smooth_inner_kernel(
    halo_ref, inner_ref, fields_ref, mask_ref, coef_ref, *refs
):
    *outer_refs, out_ref, edge_ref, filled_ref, mass_ref = refs
    groups, lat = inner_ref.shape[1] // SUB, inner_ref.shape[2]
    odd = odd_core()
    for batch in batches(groups):
        for group, smoothed in inner_half(batch, halo_ref, inner_ref, outer_refs, coef_ref, edge_ref):
            fields = by_longitude(fields_ref[block_of(group), :], lat)
            filled = []
            for c in range(2 * REACH):
                valid = jnp.broadcast_to(mask_ref[c : c + 1, :], (SUB, lat)) == 1
                filled.append((jnp.where(valid, fields[c], 0.0) + BACKGROUND) * coef_ref[AREA])
            mass_ref[rows_of(group), :] = lane_fold(sum(filled))
            filled = from_outside(filled, odd)
            for c in range(REACH):
                filled_ref[c, rows_of(group), :] = filled[c]
                out_ref[c, rows_of(group), :] = filled[c + REACH] / smoothed[c]


def smooth_outer_kernel(first, halo_ref, outer_ref, edge_ref, filled_ref, coef_ref, *out_refs):
    last = first + outer_ref.shape[1] // SUB
    out = Chunked(out_refs)
    for batch in batches(last, first):
        for group, smoothed in outer_half(batch, first, halo_ref, outer_ref, edge_ref, coef_ref):
            filled = stack_of(filled_ref, group)
            out.put(group - first, [top / bottom for top, bottom in zip(filled, smoothed)])


def low_half(shape):
    return lax.broadcasted_iota(jnp.int32, shape, 0) < SUB // 2


def add_logs(group, held, result, scaled, weight_ref, inverse_ref, total_ref):
    lat = total_ref.shape[2]
    weight = jnp.broadcast_to(weight_ref[rows_of(group), :1], (SUB, lat))
    for c in range(REACH):
        inverse_ref[c, rows_of(held), :] = 1.0 / result[c]
        total_ref[c] = total_ref[c] + weight * jnp.log(scaled[c] * result[c])


def return_inner_kernel(halo_ref, inner_ref, scaled_ref, weight_ref, coef_ref, *refs):
    *outer_refs, inverse_ref, edge_ref, total_ref = refs
    groups = inner_ref.shape[1] // SUB
    total_ref[...] = jnp.zeros_like(total_ref)
    for batch in batches(groups):
        for group, result in inner_half(batch, halo_ref, inner_ref, outer_refs, coef_ref, edge_ref):
            add_logs(group, group, result, stack_of(scaled_ref, group), weight_ref, inverse_ref, total_ref)


def return_outer_kernel(
    base, first, halo_ref, outer_ref, edge_ref, scaled_ref, weight_ref, coef_ref, inverse_ref, total_ref
):
    last = first + outer_ref.shape[1] // SUB
    total_ref[...] = jnp.zeros_like(total_ref)
    for batch in batches(last, first):
        for group, result in outer_half(batch, first, halo_ref, outer_ref, edge_ref, coef_ref):
            scaled = stack_of(scaled_ref, group - base)
            add_logs(group, group - first, result, scaled, weight_ref, inverse_ref, total_ref)


def last_return_kernel(
    base,
    first,
    halo_ref,
    outer_ref,
    edge_ref,
    scaled_ref,
    weight_ref,
    coef_ref,
    inner_ref,
    *refs,
):
    *earlier_refs, inverse_ref, logs_ref, total_ref = refs
    return_outer_kernel(
        base, first, halo_ref, outer_ref, edge_ref, scaled_ref, weight_ref, coef_ref, inverse_ref, total_ref
    )
    low = low_half(total_ref.shape[1:])
    tiles = total_ref.shape[2] // 128
    for c in range(REACH):
        outer, inner = sum((ref[c] for ref in earlier_refs), total_ref[c]), inner_ref[c]
        outer = outer + pltpu.roll(outer, SUB // 2, 0)
        inner = inner + pltpu.roll(inner, SUB // 2, 0)
        both = jnp.where(low, outer, inner)
        for t in range(tiles):
            logs_ref[rows_of(c * tiles + t), :] = both[:, t * 128 : (t + 1) * 128]
    count = jnp.sum(weight_ref[...], axis=0, keepdims=True) * (1.0 / (SUB // 2))
    logs_ref[rows_of(REACH * tiles), :] = jnp.broadcast_to(count, (SUB, 128))


def merge_kernel(own_ref, other_ref, mass_ref, coef_ref, merged_ref, payload_ref):
    members, tiles = mass_ref.shape[0], merged_ref.shape[2] // 128
    both = lambda n: own_ref[rows_of(n), :] + other_ref[rows_of(n), :]
    scale = 1.0 / both(REACH * tiles)
    level = jnp.zeros((SUB, 128), jnp.float32)
    for c in range(REACH):
        for t in range(tiles):
            span = slice(t * 128, (t + 1) * 128)
            weighted = jnp.exp(both(c * tiles + t) * scale)
            merged_ref[c, :, span] = weighted / coef_ref[AREA, :, span]
            level = level + weighted
    level = level + pltpu.roll(level, SUB // 2, 0)
    spare = jnp.zeros((128 - members - SUB, 128), jnp.float32)
    table = jnp.concatenate([mass_ref[...], level, spare], axis=0)
    row = jnp.sum(table.T, axis=0, keepdims=True)
    payload_ref[...] = jnp.broadcast_to(row[None], payload_ref.shape)


def finish_kernel(cells, got_ref, merged_ref, inner_ref, *refs):
    *outer_refs, bary_ref, updated_ref, staged_ref, sem = refs
    members, lat = inner_ref.shape[1:]
    groups = members // SUB
    odd = odd_core()
    total = jnp.sum(got_ref[...], axis=0)
    table = jnp.broadcast_to(total, (128, 128)).T
    level = table[members : members + SUB, :]
    low = low_half((SUB, lat))
    wide = lambda v: jnp.concatenate([v] * (lat // 128), axis=1)
    inverse = wide(cells / level)
    outer, inner = [], []
    for c in range(REACH):
        both = merged_ref[c] * inverse
        swapped = pltpu.roll(both, SUB // 2, 0)
        outer.append(jnp.where(low, both, swapped))
        inner.append(jnp.where(low, swapped, both))
    bary = from_outside(outer + inner, odd)
    bary_ref[...] = jnp.swapaxes(jnp.stack(bary), 0, 1)[: SUB // 2]
    for group in range(groups):
        rows = slice(group * SUB, (group + 1) * SUB)
        factor = wide(table[rows, :] / cells)
        quotients = Chunked(outer_refs).stack(group) + stack_of(inner_ref, group)
        out = [b * factor * quotient for b, quotient in zip(bary, from_outside(quotients, odd))]
        span = pl.ds(group * SUB * SUB, SUB * SUB)
        staged_ref[span, :] = jnp.swapaxes(jnp.stack(out), 0, 1).reshape(SUB * SUB, lat)
        pltpu.make_async_copy(staged_ref.at[span, :], updated_ref.at[span, :], sem.at[group]).start()
    for group in range(groups):
        span = pl.ds(group * SUB * SUB, SUB * SUB)
        pltpu.make_async_copy(staged_ref.at[span, :], updated_ref.at[span, :], sem.at[group]).wait()


def shape(*dims):
    return jax.ShapeDtypeStruct(dims, jnp.float32)


def call(kernel, outs, *args, scratch=(), out_specs=None):
    return pl.pallas_call(
        kernel,
        out_shape=outs,
        in_specs=[VMEM] * len(args),
        out_specs=out_specs or (VMEM,) * len(outs),
        scratch_shapes=scratch,
        compiler_params=params(),
    )(*args)


def body(fields, scaling, counts, land_mask):
    members, levels, lon, lat = fields.shape
    tiles = lax.axis_size("tile")
    rows = members * levels
    cells = lon * tiles * lat
    half = shape(REACH, rows, lat)
    edge = shape(2 * REACH - 2, rows, lat)
    packed = shape(REACH, SUB, lat)
    chunks = chunk_groups(rows // SUB)
    bases = [sum(map(sum, chunks[:n])) for n in range(len(chunks))]
    parts = [shape(REACH, sum(own) * SUB, lat) for own in chunks]
    coef = jnp.asarray(coefficients(lat))
    with_mate = [(i, i ^ 1) for i in range(tiles)]
    with_neighbour = [(i, (i + (1 if i % 2 else -1)) % tiles) for i in range(tiles)]
    scaling = scaling.reshape(rows * lon, lat)
    fields = fields.reshape(rows * lon, lat)
    weights = counts.astype(jnp.float32)
    weight_rows = jnp.broadcast_to(jnp.repeat(weights, levels)[:, None], (rows, 128))

    inner, *outer = call(spread_kernel, (half, *parts), scaling, coef)
    outer_halo = [lax.ppermute(part, "tile", with_neighbour) for part in outer]
    inner_halo = lax.ppermute(inner, "tile", with_mate)
    v_inner, edges, filled, mass = call(
        smooth_inner_kernel, (half, edge, half, shape(rows, 128)), inner_halo, inner, fields, land_mask, coef, *outer
    )
    v_inner_halo = lax.ppermute(v_inner, "tile", with_mate)
    weight_rows, outer_halo[-1] = lax.optimization_barrier((weight_rows, outer_halo[-1]))
    weight_rows = lax.ppermute(weight_rows, "tile", with_mate)
    v_outer, v_outer_halo, places = [], [], []
    for base, sizes, halo, own in zip(bases, chunks, outer_halo, outer):
        outs = tuple(shape(REACH, size * SUB, lat) for size in sizes)
        values = call(partial(smooth_outer_kernel, base), outs, halo, own, edges, filled, coef)
        if not v_outer:
            weight_rows, *values = lax.optimization_barrier((weight_rows, *values))
        v_outer += values
        v_outer_halo += [lax.ppermute(value, "tile", with_neighbour) for value in values]
        places += [(base, base + sum(sizes[:n]), own) for n in range(len(sizes))]
    inverse_inner, edges, inner_logs = call(
        return_inner_kernel, (half, edge, packed), v_inner_halo, v_inner, inner, weight_rows, coef, *v_outer
    )
    inverses, earlier = [inverse_inner], []
    for n, (base, first, own) in enumerate(places):
        if earlier:
            v_outer_halo[n], earlier[-1] = lax.optimization_barrier((v_outer_halo[n], earlier[-1]))
        operands = v_outer_halo[n], v_outer[n], edges, own, weight_rows, coef
        part = shape(*v_outer[n].shape)
        if n < len(places) - 1:
            inverse, logs = call(partial(return_outer_kernel, base, first), (part, packed), *operands)
            earlier.append(logs)
        else:
            inverse, logs = call(
                partial(last_return_kernel, base, first),
                (part, shape((REACH * lat // 128 + 1) * SUB, 128)),
                *operands,
                inner_logs,
                *earlier,
                scratch=[pltpu.VMEM((REACH, SUB, lat), jnp.float32)],
            )
        inverses.append(inverse)
    other = lax.ppermute(logs, "mem", [(0, 1), (1, 0)])
    merged, payload = call(merge_kernel, (packed, shape(tiles, 1, 128)), logs, other, mass, coef)
    got = lax.all_to_all(payload, "tile", split_axis=0, concat_axis=0)
    barycenter, updated = call(
        partial(finish_kernel, float(cells)),
        (shape(levels, lon, lat), shape(rows * lon, lat)),
        got,
        merged,
        *inverses,
        scratch=[pltpu.VMEM((rows * lon, lat), jnp.float32), pltpu.SemaphoreType.DMA((rows // SUB,))],
        out_specs=(VMEM, HBM),
    )
    return barycenter, updated.reshape(members, levels, lon, lat)


def solution(mesh):
    return jax.shard_map(
        body,
        mesh=mesh,
        in_specs=(
            P("mem", None, "tile", None),
            P("mem", None, "tile", None),
            P("mem"),
            P("tile", None),
        ),
        out_specs=(P(None, "tile", None), P("mem", None, "tile", None)),
        check_vma=False,
    )
```

```python
import math
from functools import partial

import jax
import jax.numpy as jnp
import numpy as np
from jax import lax
from jax.experimental import pallas as pl
from jax.experimental.pallas import tpu as pltpu
from jax.sharding import PartitionSpec as P

BACKGROUND = 0.01
REACH = 4
SUB = 8
VMEM = pl.BlockSpec(memory_space=pltpu.VMEM)
HBM = pl.BlockSpec(memory_space=pl.ANY)
AREA, ZONAL, NORTH, SOUTH, CENTER = range(5)


def coefficients(lat_cells):
    spacing = math.pi / lat_cells
    index = np.arange(lat_cells)
    latitude = -0.5 * math.pi + (index + 0.5) * spacing
    cell_area = np.cos(latitude)
    zonal = 0.2 * np.minimum(2.2, 1.0 / cell_area**2)
    north = np.where(index == lat_cells - 1, 0.0, 0.05 * np.cos(latitude + 0.5 * spacing) / cell_area)
    south = np.where(index == 0, 0.0, 0.05 * np.cos(latitude - 0.5 * spacing) / cell_area)
    center = 1.0 - 2.0 * zonal - north - south
    rows = np.stack([cell_area, zonal, north, south, center]).astype(np.float32)
    return np.ascontiguousarray(np.broadcast_to(rows[:, None, :], (5, SUB, lat_cells)))


def params(mib=12):
    return pltpu.CompilerParams(vmem_limit_bytes=mib * 2**20)


def rows_of(group):
    return pl.ds(group * SUB, SUB)


def block_of(group):
    return pl.ds(group * SUB * SUB, SUB * SUB)


def batches(last, first=0, size=4):
    return [range(start, min(start + size, last)) for start in range(first, last, size)]


def chunk_groups(groups):
    half = (groups + 1) // 2
    last = max(1, (groups - half) // 3)
    return [[half], [groups - half - last, last]]


class Chunked:
    def __init__(self, refs):
        self.refs = refs

    def stack(self, group, order=range(REACH)):
        for ref in self.refs:
            held = ref.shape[1] // SUB
            if group < held:
                return stack_of(ref, group, order)
            group -= held

    def put(self, group, values):
        for ref in self.refs:
            held = ref.shape[1] // SUB
            if 0 <= group < held:
                for c, value in enumerate(values):
                    ref[c, rows_of(group), :] = value
            group -= held


def by_longitude(block, lat):
    return jnp.swapaxes(block.reshape(SUB, SUB, lat), 0, 1)


def stack_of(ref, group, order=range(REACH)):
    return [ref[c, rows_of(group), :] for c in order]


def odd_core():
    return lax.rem(lax.axis_index("tile"), 2) == 1


def from_outside(columns, odd):
    last = len(columns) - 1
    return [jnp.where(odd, columns[last - c], columns[c]) for c in range(len(columns))]


def spread_kernel(scaling_ref, coef_ref, inner_ref, *outer_refs):
    groups, lat = inner_ref.shape[1] // SUB, inner_ref.shape[2]
    odd = odd_core()
    outer = Chunked(outer_refs)
    for group in range(groups):
        columns = from_outside(by_longitude(scaling_ref[block_of(group), :], lat), odd)
        columns = [column * coef_ref[AREA] for column in columns]
        outer.put(group, columns[:REACH])
        for c in range(REACH):
            inner_ref[c, rows_of(group), :] = columns[c + REACH]


def lane_fold(value):
    lat = value.shape[-1]
    total = value[:, :128]
    for t in range(1, lat // 128):
        total = total + value[:, t * 128 : (t + 1) * 128]
    return total


def diffuse(columns, coef_ref):
    lat = columns[0].shape[-1]
    return [
        coef_ref[CENTER] * here
        + coef_ref[ZONAL] * (west + east)
        + coef_ref[NORTH] * pltpu.roll(here, lat - 1, 1)
        + coef_ref[SOUTH] * pltpu.roll(here, 1, 1)
        for west, here, east in zip(columns[:-2], columns[1:-1], columns[2:])
    ]


def inner_half(batch, halo_ref, inner_ref, outer_refs, coef_ref, edge_ref):
    outer = Chunked(outer_refs)
    columns = [outer.stack(g) + stack_of(inner_ref, g) + stack_of(halo_ref, g, (3, 2, 1, 0)) for g in batch]
    for s in range(REACH):
        columns = [diffuse(own, coef_ref) for own in columns]
        if s < REACH - 1:
            for own, group in zip(columns, batch):
                edge_ref[2 * s, rows_of(group), :] = own[0]
                edge_ref[2 * s + 1, rows_of(group), :] = own[1]
    return zip(batch, columns)


def outer_half(batch, first, halo_ref, outer_ref, edge_ref, coef_ref):
    columns = [stack_of(halo_ref, g - first, (3, 2, 1, 0)) + stack_of(outer_ref, g - first, (0, 1)) for g in batch]
    for s in range(REACH):
        columns = [diffuse(own, coef_ref) for own in columns]
        if s < REACH - 1:
            columns = [own + stack_of(edge_ref, g, (2 * s, 2 * s + 1)) for own, g in zip(columns, batch)]
    return zip(batch, columns)


def smooth_inner_kernel(
    halo_ref, inner_ref, fields_ref, mask_ref, coef_ref, *refs
):
    *outer_refs, out_ref, edge_ref, filled_ref, mass_ref = refs
    groups, lat = inner_ref.shape[1] // SUB, inner_ref.shape[2]
    odd = odd_core()
    for batch in batches(groups):
        for group, smoothed in inner_half(batch, halo_ref, inner_ref, outer_refs, coef_ref, edge_ref):
            fields = by_longitude(fields_ref[block_of(group), :], lat)
            filled = []
            for c in range(2 * REACH):
                valid = jnp.broadcast_to(mask_ref[c : c + 1, :], (SUB, lat)) == 1
                filled.append((jnp.where(valid, fields[c], 0.0) + BACKGROUND) * coef_ref[AREA])
            mass_ref[rows_of(group), :] = lane_fold(sum(filled))
            filled = from_outside(filled, odd)
            for c in range(REACH):
                filled_ref[c, rows_of(group), :] = filled[c]
                out_ref[c, rows_of(group), :] = filled[c + REACH] / smoothed[c]


def smooth_outer_kernel(first, halo_ref, outer_ref, edge_ref, filled_ref, coef_ref, *out_refs):
    last = first + outer_ref.shape[1] // SUB
    out = Chunked(out_refs)
    for batch in batches(last, first):
        for group, smoothed in outer_half(batch, first, halo_ref, outer_ref, edge_ref, coef_ref):
            filled = stack_of(filled_ref, group)
            out.put(group - first, [top / bottom for top, bottom in zip(filled, smoothed)])


def low_half(shape):
    return lax.broadcasted_iota(jnp.int32, shape, 0) < SUB // 2


def add_logs(group, held, result, scaled, weight_ref, inverse_ref, total_ref):
    lat = total_ref.shape[2]
    weight = jnp.broadcast_to(weight_ref[rows_of(group), :1], (SUB, lat))
    for c in range(REACH):
        inverse_ref[c, rows_of(held), :] = 1.0 / result[c]
        total_ref[c] = total_ref[c] + weight * jnp.log(scaled[c] * result[c])


def return_inner_kernel(halo_ref, inner_ref, scaled_ref, weight_ref, coef_ref, *refs):
    *outer_refs, inverse_ref, edge_ref, total_ref = refs
    groups = inner_ref.shape[1] // SUB
    total_ref[...] = jnp.zeros_like(total_ref)
    for batch in batches(groups):
        for group, result in inner_half(batch, halo_ref, inner_ref, outer_refs, coef_ref, edge_ref):
            add_logs(group, group, result, stack_of(scaled_ref, group), weight_ref, inverse_ref, total_ref)


def return_outer_kernel(
    base, first, halo_ref, outer_ref, edge_ref, scaled_ref, weight_ref, coef_ref, inverse_ref, total_ref
):
    last = first + outer_ref.shape[1] // SUB
    total_ref[...] = jnp.zeros_like(total_ref)
    for batch in batches(last, first):
        for group, result in outer_half(batch, first, halo_ref, outer_ref, edge_ref, coef_ref):
            scaled = stack_of(scaled_ref, group - base)
            add_logs(group, group - first, result, scaled, weight_ref, inverse_ref, total_ref)


def last_return_kernel(
    base,
    first,
    halo_ref,
    outer_ref,
    edge_ref,
    scaled_ref,
    weight_ref,
    coef_ref,
    inner_ref,
    *refs,
):
    *earlier_refs, inverse_ref, logs_ref, total_ref = refs
    return_outer_kernel(
        base, first, halo_ref, outer_ref, edge_ref, scaled_ref, weight_ref, coef_ref, inverse_ref, total_ref
    )
    low = low_half(total_ref.shape[1:])
    tiles = total_ref.shape[2] // 128
    for c in range(REACH):
        outer, inner = sum((ref[c] for ref in earlier_refs), total_ref[c]), inner_ref[c]
        outer = outer + pltpu.roll(outer, SUB // 2, 0)
        inner = inner + pltpu.roll(inner, SUB // 2, 0)
        both = jnp.where(low, outer, inner)
        for t in range(tiles):
            logs_ref[rows_of(c * tiles + t), :] = both[:, t * 128 : (t + 1) * 128]
    count = jnp.sum(weight_ref[...], axis=0, keepdims=True) * (1.0 / (SUB // 2))
    logs_ref[rows_of(REACH * tiles), :] = jnp.broadcast_to(count, (SUB, 128))


def merge_kernel(own_ref, other_ref, mass_ref, coef_ref, merged_ref, payload_ref):
    members, tiles = mass_ref.shape[0], merged_ref.shape[2] // 128
    both = lambda n: own_ref[rows_of(n), :] + other_ref[rows_of(n), :]
    scale = 1.0 / both(REACH * tiles)
    level = jnp.zeros((SUB, 128), jnp.float32)
    for c in range(REACH):
        for t in range(tiles):
            span = slice(t * 128, (t + 1) * 128)
            weighted = jnp.exp(both(c * tiles + t) * scale)
            merged_ref[c, :, span] = weighted / coef_ref[AREA, :, span]
            level = level + weighted
    level = level + pltpu.roll(level, SUB // 2, 0)
    spare = jnp.zeros((128 - members - SUB, 128), jnp.float32)
    table = jnp.concatenate([mass_ref[...], level, spare], axis=0)
    row = jnp.sum(table.T, axis=0, keepdims=True)
    payload_ref[...] = jnp.broadcast_to(row[None], payload_ref.shape)


def finish_kernel(cells, got_ref, merged_ref, inner_ref, *refs):
    *outer_refs, bary_ref, updated_ref, staged_ref, sem = refs
    members, lat = inner_ref.shape[1:]
    groups = members // SUB
    odd = odd_core()
    total = jnp.sum(got_ref[...], axis=0)
    table = jnp.broadcast_to(total, (128, 128)).T
    level = table[members : members + SUB, :]
    low = low_half((SUB, lat))
    wide = lambda v: jnp.concatenate([v] * (lat // 128), axis=1)
    inverse = wide(cells / level)
    outer, inner = [], []
    for c in range(REACH):
        both = merged_ref[c] * inverse
        swapped = pltpu.roll(both, SUB // 2, 0)
        outer.append(jnp.where(low, both, swapped))
        inner.append(jnp.where(low, swapped, both))
    bary = from_outside(outer + inner, odd)
    bary_ref[...] = jnp.swapaxes(jnp.stack(bary), 0, 1)[: SUB // 2]
    for group in range(groups):
        rows = slice(group * SUB, (group + 1) * SUB)
        factor = wide(table[rows, :] / cells)
        quotients = Chunked(outer_refs).stack(group) + stack_of(inner_ref, group)
        out = [b * factor * quotient for b, quotient in zip(bary, from_outside(quotients, odd))]
        span = pl.ds(group * SUB * SUB, SUB * SUB)
        staged_ref[span, :] = jnp.swapaxes(jnp.stack(out), 0, 1).reshape(SUB * SUB, lat)
        pltpu.make_async_copy(staged_ref.at[span, :], updated_ref.at[span, :], sem.at[group]).start()
    for group in range(groups):
        span = pl.ds(group * SUB * SUB, SUB * SUB)
        pltpu.make_async_copy(staged_ref.at[span, :], updated_ref.at[span, :], sem.at[group]).wait()


def shape(*dims):
    return jax.ShapeDtypeStruct(dims, jnp.float32)


def call(kernel, outs, *args, scratch=(), out_specs=None):
    return pl.pallas_call(
        kernel,
        out_shape=outs,
        in_specs=[VMEM] * len(args),
        out_specs=out_specs or (VMEM,) * len(outs),
        scratch_shapes=scratch,
        compiler_params=params(),
    )(*args)


def body(fields, scaling, counts, land_mask):
    members, levels, lon, lat = fields.shape
    tiles = lax.axis_size("tile")
    rows = members * levels
    cells = lon * tiles * lat
    half = shape(REACH, rows, lat)
    edge = shape(2 * REACH - 2, rows, lat)
    packed = shape(REACH, SUB, lat)
    chunks = chunk_groups(rows // SUB)
    bases = [sum(map(sum, chunks[:n])) for n in range(len(chunks))]
    parts = [shape(REACH, sum(own) * SUB, lat) for own in chunks]
    coef = jnp.asarray(coefficients(lat))
    with_mate = [(i, i ^ 1) for i in range(tiles)]
    with_neighbour = [(i, (i + (1 if i % 2 else -1)) % tiles) for i in range(tiles)]
    scaling = scaling.reshape(rows * lon, lat)
    fields = fields.reshape(rows * lon, lat)
    weights = counts.astype(jnp.float32)
    weight_rows = jnp.broadcast_to(jnp.repeat(weights, levels)[:, None], (rows, 128))

    inner, *outer = call(spread_kernel, (half, *parts), scaling, coef)
    outer_halo = [lax.ppermute(part, "tile", with_neighbour) for part in outer]
    inner_halo = lax.ppermute(inner, "tile", with_mate)
    v_inner, edges, filled, mass = call(
        smooth_inner_kernel, (half, edge, half, shape(rows, 128)), inner_halo, inner, fields, land_mask, coef, *outer
    )
    v_inner_halo = lax.ppermute(v_inner, "tile", with_mate)
    v_outer, v_outer_halo, places = [], [], []
    for base, sizes, halo, own in zip(bases, chunks, outer_halo, outer):
        outs = tuple(shape(REACH, size * SUB, lat) for size in sizes)
        values = call(partial(smooth_outer_kernel, base), outs, halo, own, edges, filled, coef)
        v_outer += values
        v_outer_halo += [lax.ppermute(value, "tile", with_neighbour) for value in values]
        places += [(base, base + sum(sizes[:n]), own) for n in range(len(sizes))]
    inverse_inner, edges, inner_logs = call(
        return_inner_kernel, (half, edge, packed), v_inner_halo, v_inner, inner, weight_rows, coef, *v_outer
    )
    inverses, earlier = [inverse_inner], []
    for n, (base, first, own) in enumerate(places):
        if earlier:
            v_outer_halo[n], earlier[-1] = lax.optimization_barrier((v_outer_halo[n], earlier[-1]))
        operands = v_outer_halo[n], v_outer[n], edges, own, weight_rows, coef
        part = shape(*v_outer[n].shape)
        if n < len(places) - 1:
            inverse, logs = call(partial(return_outer_kernel, base, first), (part, packed), *operands)
            earlier.append(logs)
        else:
            inverse, logs = call(
                partial(last_return_kernel, base, first),
                (part, shape((REACH * lat // 128 + 1) * SUB, 128)),
                *operands,
                inner_logs,
                *earlier,
                scratch=[pltpu.VMEM((REACH, SUB, lat), jnp.float32)],
            )
        inverses.append(inverse)
    other = lax.ppermute(logs, "mem", [(0, 1), (1, 0)])
    merged, payload = call(merge_kernel, (packed, shape(tiles, 1, 128)), logs, other, mass, coef)
    got = lax.all_to_all(payload, "tile", split_axis=0, concat_axis=0)
    barycenter, updated = call(
        partial(finish_kernel, float(cells)),
        (shape(levels, lon, lat), shape(rows * lon, lat)),
        got,
        merged,
        *inverses,
        scratch=[pltpu.VMEM((rows * lon, lat), jnp.float32), pltpu.SemaphoreType.DMA((rows // SUB,))],
        out_specs=(VMEM, HBM),
    )
    return barycenter, updated.reshape(members, levels, lon, lat)


def solution(mesh):
    return jax.shard_map(
        body,
        mesh=mesh,
        in_specs=(
            P("mem", None, "tile", None),
            P("mem", None, "tile", None),
            P("mem"),
            P("tile", None),
        ),
        out_specs=(P(None, "tile", None), P("mem", None, "tile", None)),
        check_vma=False,
    )
```

```python
import math
from functools import partial

import jax
import jax.numpy as jnp
import numpy as np
from jax import lax
from jax.experimental import pallas as pl
from jax.experimental.pallas import tpu as pltpu
from jax.sharding import PartitionSpec as P

BACKGROUND = 0.01
REACH = 4
SUB = 8
VMEM = pl.BlockSpec(memory_space=pltpu.VMEM)
SMEM = pl.BlockSpec(memory_space=pltpu.SMEM)
HBM = pl.BlockSpec(memory_space=pl.ANY)
AREA, ZONAL, NORTH, SOUTH, CENTER = range(5)


def coefficients(lat_cells):
    spacing = math.pi / lat_cells
    index = np.arange(lat_cells)
    latitude = -0.5 * math.pi + (index + 0.5) * spacing
    cell_area = np.cos(latitude)
    zonal = 0.2 * np.minimum(2.2, 1.0 / cell_area**2)
    north = np.where(index == lat_cells - 1, 0.0, 0.05 * np.cos(latitude + 0.5 * spacing) / cell_area)
    south = np.where(index == 0, 0.0, 0.05 * np.cos(latitude - 0.5 * spacing) / cell_area)
    center = 1.0 - 2.0 * zonal - north - south
    rows = np.stack([cell_area, zonal, north, south, center]).astype(np.float32)
    return np.ascontiguousarray(np.broadcast_to(rows[:, None, :], (5, SUB, lat_cells)))


def params(mib=12):
    return pltpu.CompilerParams(vmem_limit_bytes=mib * 2**20)


def rows_of(group):
    return pl.ds(group * SUB, SUB)


def block_of(group):
    return pl.ds(group * SUB * SUB, SUB * SUB)


def batches(last, first=0, size=4):
    return [range(start, min(start + size, last)) for start in range(first, last, size)]


def chunk_groups(groups):
    half = (groups + 1) // 2
    last = max(1, (groups - half) // 3)
    return [[half], [groups - half - last, last]]


class Chunked:
    def __init__(self, refs):
        self.refs = refs

    def stack(self, group, order=range(REACH)):
        for ref in self.refs:
            held = ref.shape[1] // SUB
            if group < held:
                return stack_of(ref, group, order)
            group -= held

    def put(self, group, values):
        for ref in self.refs:
            held = ref.shape[1] // SUB
            if 0 <= group < held:
                for c, value in enumerate(values):
                    ref[c, rows_of(group), :] = value
            group -= held


def by_longitude(block, lat):
    return jnp.swapaxes(block.reshape(SUB, SUB, lat), 0, 1)


def stack_of(ref, group, order=range(REACH)):
    return [ref[c, rows_of(group), :] for c in order]


def odd_core():
    return lax.rem(lax.axis_index("tile"), 2) == 1


def from_outside(columns, odd):
    last = len(columns) - 1
    return [jnp.where(odd, columns[last - c], columns[c]) for c in range(len(columns))]


def spread_kernel(scaling_ref, coef_ref, inner_ref, *outer_refs):
    groups, lat = inner_ref.shape[1] // SUB, inner_ref.shape[2]
    odd = odd_core()
    outer = Chunked(outer_refs)
    for group in range(groups):
        columns = from_outside(by_longitude(scaling_ref[block_of(group), :], lat), odd)
        columns = [column * coef_ref[AREA] for column in columns]
        outer.put(group, columns[:REACH])
        for c in range(REACH):
            inner_ref[c, rows_of(group), :] = columns[c + REACH]


def lane_fold(value):
    lat = value.shape[-1]
    total = value[:, :128]
    for t in range(1, lat // 128):
        total = total + value[:, t * 128 : (t + 1) * 128]
    return total


def diffuse(columns, coef_ref):
    lat = columns[0].shape[-1]
    return [
        coef_ref[CENTER] * here
        + coef_ref[ZONAL] * (west + east)
        + coef_ref[NORTH] * pltpu.roll(here, lat - 1, 1)
        + coef_ref[SOUTH] * pltpu.roll(here, 1, 1)
        for west, here, east in zip(columns[:-2], columns[1:-1], columns[2:])
    ]


def inner_half(batch, halo_ref, inner_ref, outer_refs, coef_ref, edge_ref):
    outer = Chunked(outer_refs)
    columns = [outer.stack(g) + stack_of(inner_ref, g) + stack_of(halo_ref, g, (3, 2, 1, 0)) for g in batch]
    for s in range(REACH):
        columns = [diffuse(own, coef_ref) for own in columns]
        if s < REACH - 1:
            for own, group in zip(columns, batch):
                edge_ref[2 * s, rows_of(group), :] = own[0]
                edge_ref[2 * s + 1, rows_of(group), :] = own[1]
    return zip(batch, columns)


def outer_half(batch, first, halo_ref, outer_ref, edge_ref, coef_ref):
    columns = [stack_of(halo_ref, g - first, (3, 2, 1, 0)) + stack_of(outer_ref, g - first, (0, 1)) for g in batch]
    for s in range(REACH):
        columns = [diffuse(own, coef_ref) for own in columns]
        if s < REACH - 1:
            columns = [own + stack_of(edge_ref, g, (2 * s, 2 * s + 1)) for own, g in zip(columns, batch)]
    return zip(batch, columns)


def smooth_inner_kernel(
    halo_ref, inner_ref, fields_ref, mask_ref, coef_ref, *refs
):
    *outer_refs, out_ref, edge_ref, filled_ref, mass_ref = refs
    groups, lat = inner_ref.shape[1] // SUB, inner_ref.shape[2]
    odd = odd_core()
    for batch in batches(groups):
        for group, smoothed in inner_half(batch, halo_ref, inner_ref, outer_refs, coef_ref, edge_ref):
            fields = by_longitude(fields_ref[block_of(group), :], lat)
            filled = []
            for c in range(2 * REACH):
                valid = jnp.broadcast_to(mask_ref[c : c + 1, :], (SUB, lat)) == 1
                filled.append((jnp.where(valid, fields[c], 0.0) + BACKGROUND) * coef_ref[AREA])
            mass_ref[rows_of(group), :] = lane_fold(sum(filled))
            filled = from_outside(filled, odd)
            for c in range(REACH):
                filled_ref[c, rows_of(group), :] = filled[c]
                out_ref[c, rows_of(group), :] = filled[c + REACH] / smoothed[c]


def smooth_outer_kernel(first, halo_ref, outer_ref, edge_ref, filled_ref, coef_ref, *out_refs):
    last = first + outer_ref.shape[1] // SUB
    out = Chunked(out_refs)
    for batch in batches(last, first):
        for group, smoothed in outer_half(batch, first, halo_ref, outer_ref, edge_ref, coef_ref):
            filled = stack_of(filled_ref, group)
            out.put(group - first, [top / bottom for top, bottom in zip(filled, smoothed)])


def low_half(shape):
    return lax.broadcasted_iota(jnp.int32, shape, 0) < SUB // 2


def add_logs(group, held, result, scaled, weight_ref, inverse_ref, total_ref):
    lat = total_ref.shape[2]
    first, second = (weight_ref[2 * group + n].astype(jnp.float32) for n in range(2))
    weight = jnp.where(low_half((SUB, lat)), first, second)
    for c in range(REACH):
        inverse_ref[c, rows_of(held), :] = 1.0 / result[c]
        total_ref[c] = total_ref[c] + weight * jnp.log(scaled[c] * result[c])


def return_inner_kernel(halo_ref, inner_ref, scaled_ref, weight_ref, coef_ref, *refs):
    *outer_refs, inverse_ref, edge_ref, total_ref = refs
    groups = inner_ref.shape[1] // SUB
    total_ref[...] = jnp.zeros_like(total_ref)
    for batch in batches(groups):
        for group, result in inner_half(batch, halo_ref, inner_ref, outer_refs, coef_ref, edge_ref):
            add_logs(group, group, result, stack_of(scaled_ref, group), weight_ref, inverse_ref, total_ref)


def return_outer_kernel(
    base, first, halo_ref, outer_ref, edge_ref, scaled_ref, weight_ref, coef_ref, inverse_ref, total_ref
):
    last = first + outer_ref.shape[1] // SUB
    total_ref[...] = jnp.zeros_like(total_ref)
    for batch in batches(last, first):
        for group, result in outer_half(batch, first, halo_ref, outer_ref, edge_ref, coef_ref):
            scaled = stack_of(scaled_ref, group - base)
            add_logs(group, group - first, result, scaled, weight_ref, inverse_ref, total_ref)


def last_return_kernel(
    base,
    first,
    halo_ref,
    outer_ref,
    edge_ref,
    scaled_ref,
    weight_ref,
    coef_ref,
    inner_ref,
    *refs,
):
    *earlier_refs, inverse_ref, logs_ref, total_ref = refs
    return_outer_kernel(
        base, first, halo_ref, outer_ref, edge_ref, scaled_ref, weight_ref, coef_ref, inverse_ref, total_ref
    )
    low = low_half(total_ref.shape[1:])
    tiles = total_ref.shape[2] // 128
    for c in range(REACH):
        outer, inner = sum((ref[c] for ref in earlier_refs), total_ref[c]), inner_ref[c]
        outer = outer + pltpu.roll(outer, SUB // 2, 0)
        inner = inner + pltpu.roll(inner, SUB // 2, 0)
        both = jnp.where(low, outer, inner)
        for t in range(tiles):
            logs_ref[rows_of(c * tiles + t), :] = both[:, t * 128 : (t + 1) * 128]
    count = sum(weight_ref[m] for m in range(weight_ref.shape[0])).astype(jnp.float32)
    logs_ref[rows_of(REACH * tiles), :] = jnp.full((SUB, 128), count)


def merge_kernel(own_ref, other_ref, mass_ref, coef_ref, merged_ref, payload_ref):
    members, tiles = mass_ref.shape[0], merged_ref.shape[2] // 128
    both = lambda n: own_ref[rows_of(n), :] + other_ref[rows_of(n), :]
    scale = 1.0 / both(REACH * tiles)
    level = jnp.zeros((SUB, 128), jnp.float32)
    for c in range(REACH):
        for t in range(tiles):
            span = slice(t * 128, (t + 1) * 128)
            weighted = jnp.exp(both(c * tiles + t) * scale)
            merged_ref[c, :, span] = weighted / coef_ref[AREA, :, span]
            level = level + weighted
    level = level + pltpu.roll(level, SUB // 2, 0)
    spare = jnp.zeros((128 - members - SUB, 128), jnp.float32)
    table = jnp.concatenate([mass_ref[...], level, spare], axis=0)
    row = jnp.sum(table.T, axis=0, keepdims=True)
    payload_ref[...] = jnp.broadcast_to(row[None], payload_ref.shape)


def finish_kernel(cells, got_ref, merged_ref, inner_ref, *refs):
    *outer_refs, bary_ref, updated_ref, staged_ref, sem = refs
    members, lat = inner_ref.shape[1:]
    groups = members // SUB
    odd = odd_core()
    total = jnp.sum(got_ref[...], axis=0)
    table = jnp.broadcast_to(total, (128, 128)).T
    level = table[members : members + SUB, :]
    low = low_half((SUB, lat))
    wide = lambda v: jnp.concatenate([v] * (lat // 128), axis=1)
    inverse = wide(cells / level)
    outer, inner = [], []
    for c in range(REACH):
        both = merged_ref[c] * inverse
        swapped = pltpu.roll(both, SUB // 2, 0)
        outer.append(jnp.where(low, both, swapped))
        inner.append(jnp.where(low, swapped, both))
    bary = from_outside(outer + inner, odd)
    bary_ref[...] = jnp.swapaxes(jnp.stack(bary), 0, 1)[: SUB // 2]
    for group in range(groups):
        rows = slice(group * SUB, (group + 1) * SUB)
        factor = wide(table[rows, :] / cells)
        quotients = Chunked(outer_refs).stack(group) + stack_of(inner_ref, group)
        out = [b * factor * quotient for b, quotient in zip(bary, from_outside(quotients, odd))]
        span = pl.ds(group * SUB * SUB, SUB * SUB)
        staged_ref[span, :] = jnp.swapaxes(jnp.stack(out), 0, 1).reshape(SUB * SUB, lat)
        pltpu.make_async_copy(staged_ref.at[span, :], updated_ref.at[span, :], sem.at[group]).start()
    for group in range(groups):
        span = pl.ds(group * SUB * SUB, SUB * SUB)
        pltpu.make_async_copy(staged_ref.at[span, :], updated_ref.at[span, :], sem.at[group]).wait()


def shape(*dims):
    return jax.ShapeDtypeStruct(dims, jnp.float32)


def call(kernel, outs, *args, scratch=(), out_specs=None):
    return pl.pallas_call(
        kernel,
        out_shape=outs,
        in_specs=[SMEM if arg.ndim == 1 else VMEM for arg in args],
        out_specs=out_specs or (VMEM,) * len(outs),
        scratch_shapes=scratch,
        compiler_params=params(),
    )(*args)


def body(fields, scaling, counts, land_mask):
    members, levels, lon, lat = fields.shape
    tiles = lax.axis_size("tile")
    rows = members * levels
    cells = lon * tiles * lat
    half = shape(REACH, rows, lat)
    edge = shape(2 * REACH - 2, rows, lat)
    packed = shape(REACH, SUB, lat)
    chunks = chunk_groups(rows // SUB)
    bases = [sum(map(sum, chunks[:n])) for n in range(len(chunks))]
    parts = [shape(REACH, sum(own) * SUB, lat) for own in chunks]
    coef = jnp.asarray(coefficients(lat))
    with_mate = [(i, i ^ 1) for i in range(tiles)]
    with_neighbour = [(i, (i + (1 if i % 2 else -1)) % tiles) for i in range(tiles)]
    scaling = scaling.reshape(rows * lon, lat)
    fields = fields.reshape(rows * lon, lat)

    inner, *outer = call(spread_kernel, (half, *parts), scaling, coef)
    outer_halo = [lax.ppermute(part, "tile", with_neighbour) for part in outer]
    inner_halo = lax.ppermute(inner, "tile", with_mate)
    v_inner, edges, filled, mass = call(
        smooth_inner_kernel, (half, edge, half, shape(rows, 128)), inner_halo, inner, fields, land_mask, coef, *outer
    )
    v_inner_halo = lax.ppermute(v_inner, "tile", with_mate)
    v_outer, v_outer_halo, places = [], [], []
    for base, sizes, halo, own in zip(bases, chunks, outer_halo, outer):
        outs = tuple(shape(REACH, size * SUB, lat) for size in sizes)
        values = call(partial(smooth_outer_kernel, base), outs, halo, own, edges, filled, coef)
        v_outer += values
        v_outer_halo += [lax.ppermute(value, "tile", with_neighbour) for value in values]
        places += [(base, base + sum(sizes[:n]), own) for n in range(len(sizes))]
    inverse_inner, edges, inner_logs = call(
        return_inner_kernel, (half, edge, packed), v_inner_halo, v_inner, inner, counts, coef, *v_outer
    )
    inverses, earlier = [inverse_inner], []
    for n, (base, first, own) in enumerate(places):
        if earlier:
            v_outer_halo[n], earlier[-1] = lax.optimization_barrier((v_outer_halo[n], earlier[-1]))
        operands = v_outer_halo[n], v_outer[n], edges, own, counts, coef
        part = shape(*v_outer[n].shape)
        if n < len(places) - 1:
            inverse, logs = call(partial(return_outer_kernel, base, first), (part, packed), *operands)
            earlier.append(logs)
        else:
            inverse, logs = call(
                partial(last_return_kernel, base, first),
                (part, shape((REACH * lat // 128 + 1) * SUB, 128)),
                *operands,
                inner_logs,
                *earlier,
                scratch=[pltpu.VMEM((REACH, SUB, lat), jnp.float32)],
            )
        inverses.append(inverse)
    other = lax.ppermute(logs, "mem", [(0, 1), (1, 0)])
    merged, payload = call(merge_kernel, (packed, shape(tiles, 1, 128)), logs, other, mass, coef)
    got = lax.all_to_all(payload, "tile", split_axis=0, concat_axis=0)
    barycenter, updated = call(
        partial(finish_kernel, float(cells)),
        (shape(levels, lon, lat), shape(rows * lon, lat)),
        got,
        merged,
        *inverses,
        scratch=[pltpu.VMEM((rows * lon, lat), jnp.float32), pltpu.SemaphoreType.DMA((rows // SUB,))],
        out_specs=(VMEM, HBM),
    )
    return barycenter, updated.reshape(members, levels, lon, lat)


def solution(mesh):
    return jax.shard_map(
        body,
        mesh=mesh,
        in_specs=(
            P("mem", None, "tile", None),
            P("mem", None, "tile", None),
            P("mem"),
            P("tile", None),
        ),
        out_specs=(P(None, "tile", None), P("mem", None, "tile", None)),
        check_vma=False,
    )
```

```python
import math
from functools import partial

import jax
import jax.numpy as jnp
import numpy as np
from jax import lax
from jax.experimental import pallas as pl
from jax.experimental.pallas import tpu as pltpu
from jax.sharding import PartitionSpec as P

BACKGROUND = 0.01
REACH = 4
SUB = 8
VMEM = pl.BlockSpec(memory_space=pltpu.VMEM)
SMEM = pl.BlockSpec(memory_space=pltpu.SMEM)
HBM = pl.BlockSpec(memory_space=pl.ANY)
AREA, ZONAL, NORTH, SOUTH, CENTER = range(5)


def coefficients(lat_cells):
    spacing = math.pi / lat_cells
    index = np.arange(lat_cells)
    latitude = -0.5 * math.pi + (index + 0.5) * spacing
    cell_area = np.cos(latitude)
    zonal = 0.2 * np.minimum(2.2, 1.0 / cell_area**2)
    north = np.where(index == lat_cells - 1, 0.0, 0.05 * np.cos(latitude + 0.5 * spacing) / cell_area)
    south = np.where(index == 0, 0.0, 0.05 * np.cos(latitude - 0.5 * spacing) / cell_area)
    center = 1.0 - 2.0 * zonal - north - south
    rows = np.stack([cell_area, zonal, north, south, center]).astype(np.float32)
    return np.ascontiguousarray(np.broadcast_to(rows[:, None, :], (5, SUB, lat_cells)))


def params(mib=12):
    return pltpu.CompilerParams(vmem_limit_bytes=mib * 2**20)


def rows_of(group):
    return pl.ds(group * SUB, SUB)


def block_of(group):
    return pl.ds(group * SUB * SUB, SUB * SUB)


def batches(last, first=0, size=4):
    return [range(start, min(start + size, last)) for start in range(first, last, size)]


def chunk_groups(groups):
    half = (groups + 1) // 2
    last = max(1, (groups - half) // 3)
    return [[half], [groups - half - last, last]]


class Chunked:
    def __init__(self, refs):
        self.refs = refs

    def stack(self, group, order=range(REACH)):
        for ref in self.refs:
            held = ref.shape[1] // SUB
            if group < held:
                return stack_of(ref, group, order)
            group -= held

    def put(self, group, values):
        for ref in self.refs:
            held = ref.shape[1] // SUB
            if 0 <= group < held:
                for c, value in enumerate(values):
                    ref[c, rows_of(group), :] = value
            group -= held


def by_longitude(block, lat):
    return jnp.swapaxes(block.reshape(SUB, SUB, lat), 0, 1)


def stack_of(ref, group, order=range(REACH)):
    return [ref[c, rows_of(group), :] for c in order]


def odd_core():
    return lax.rem(lax.axis_index("tile"), 2) == 1


def from_outside(columns, odd):
    last = len(columns) - 1
    return [jnp.where(odd, columns[last - c], columns[c]) for c in range(len(columns))]


def low_half(shape):
    return lax.broadcasted_iota(jnp.int32, shape, 0) < SUB // 2


def spread_kernel(scaling_ref, coef_ref, inner_ref, *outer_refs):
    groups, lat = inner_ref.shape[1] // SUB, inner_ref.shape[2]
    odd = odd_core()
    outer = Chunked(outer_refs)
    for group in range(groups):
        columns = from_outside(by_longitude(scaling_ref[block_of(group), :], lat), odd)
        columns = [column * coef_ref[AREA] for column in columns]
        outer.put(group, columns[:REACH])
        for c in range(REACH):
            inner_ref[c, rows_of(group), :] = columns[c + REACH]


def lane_fold(value):
    lat = value.shape[-1]
    total = value[:, :128]
    for t in range(1, lat // 128):
        total = total + value[:, t * 128 : (t + 1) * 128]
    return total


def diffuse(columns, coef_ref):
    lat = columns[0].shape[-1]
    return [
        coef_ref[CENTER] * here
        + coef_ref[ZONAL] * (west + east)
        + coef_ref[NORTH] * pltpu.roll(here, lat - 1, 1)
        + coef_ref[SOUTH] * pltpu.roll(here, 1, 1)
        for west, here, east in zip(columns[:-2], columns[1:-1], columns[2:])
    ]


def inner_half(batch, halo_ref, inner_ref, outer_refs, coef_ref, edge_ref):
    outer = Chunked(outer_refs)
    columns = [outer.stack(g) + stack_of(inner_ref, g) + stack_of(halo_ref, g, (3, 2, 1, 0)) for g in batch]
    for s in range(REACH):
        columns = [diffuse(own, coef_ref) for own in columns]
        if s < REACH - 1:
            for own, group in zip(columns, batch):
                edge_ref[2 * s, rows_of(group), :] = own[0]
                edge_ref[2 * s + 1, rows_of(group), :] = own[1]
    return zip(batch, columns)


def outer_half(batch, first, halo_ref, outer_ref, edge_ref, coef_ref):
    columns = [stack_of(halo_ref, g - first, (3, 2, 1, 0)) + stack_of(outer_ref, g - first, (0, 1)) for g in batch]
    for s in range(REACH):
        columns = [diffuse(own, coef_ref) for own in columns]
        if s < REACH - 1:
            columns = [own + stack_of(edge_ref, g, (2 * s, 2 * s + 1)) for own, g in zip(columns, batch)]
    return zip(batch, columns)


def smooth_inner_kernel(
    halo_ref, inner_ref, fields_ref, mask_ref, count_ref, coef_ref, *refs
):
    *outer_refs, out_ref, edge_ref, filled_ref, mass_ref, weight_ref = refs
    groups, lat = inner_ref.shape[1] // SUB, inner_ref.shape[2]
    odd = odd_core()
    low = low_half((SUB, 128))
    for group in range(groups):
        first, second = (count_ref[2 * group + n].astype(jnp.float32) for n in range(2))
        weight_ref[rows_of(group), :] = jnp.where(low, first, second)
    count = sum(count_ref[m] for m in range(2 * groups)).astype(jnp.float32)
    weight_ref[rows_of(groups), :] = jnp.full((SUB, 128), count)
    for batch in batches(groups):
        for group, smoothed in inner_half(batch, halo_ref, inner_ref, outer_refs, coef_ref, edge_ref):
            fields = by_longitude(fields_ref[block_of(group), :], lat)
            filled = []
            for c in range(2 * REACH):
                valid = jnp.broadcast_to(mask_ref[c : c + 1, :], (SUB, lat)) == 1
                filled.append((jnp.where(valid, fields[c], 0.0) + BACKGROUND) * coef_ref[AREA])
            mass_ref[rows_of(group), :] = lane_fold(sum(filled))
            filled = from_outside(filled, odd)
            for c in range(REACH):
                filled_ref[c, rows_of(group), :] = filled[c]
                out_ref[c, rows_of(group), :] = filled[c + REACH] / smoothed[c]


def smooth_outer_kernel(first, halo_ref, outer_ref, edge_ref, filled_ref, coef_ref, *out_refs):
    last = first + outer_ref.shape[1] // SUB
    out = Chunked(out_refs)
    for batch in batches(last, first):
        for group, smoothed in outer_half(batch, first, halo_ref, outer_ref, edge_ref, coef_ref):
            filled = stack_of(filled_ref, group)
            out.put(group - first, [top / bottom for top, bottom in zip(filled, smoothed)])


def add_logs(group, held, result, scaled, weight_ref, inverse_ref, total_ref):
    lat = total_ref.shape[2]
    weight = jnp.concatenate([weight_ref[rows_of(group), :]] * (lat // 128), axis=1)
    for c in range(REACH):
        inverse_ref[c, rows_of(held), :] = 1.0 / result[c]
        total_ref[c] = total_ref[c] + weight * jnp.log(scaled[c] * result[c])


def return_inner_kernel(halo_ref, inner_ref, scaled_ref, weight_ref, coef_ref, *refs):
    *outer_refs, inverse_ref, edge_ref, total_ref = refs
    groups = inner_ref.shape[1] // SUB
    total_ref[...] = jnp.zeros_like(total_ref)
    for batch in batches(groups):
        for group, result in inner_half(batch, halo_ref, inner_ref, outer_refs, coef_ref, edge_ref):
            add_logs(group, group, result, stack_of(scaled_ref, group), weight_ref, inverse_ref, total_ref)


def return_outer_kernel(
    base, first, halo_ref, outer_ref, edge_ref, scaled_ref, weight_ref, coef_ref, inverse_ref, total_ref
):
    last = first + outer_ref.shape[1] // SUB
    total_ref[...] = jnp.zeros_like(total_ref)
    for batch in batches(last, first):
        for group, result in outer_half(batch, first, halo_ref, outer_ref, edge_ref, coef_ref):
            scaled = stack_of(scaled_ref, group - base)
            add_logs(group, group - first, result, scaled, weight_ref, inverse_ref, total_ref)


def last_return_kernel(
    base,
    first,
    halo_ref,
    outer_ref,
    edge_ref,
    scaled_ref,
    weight_ref,
    coef_ref,
    inner_ref,
    *refs,
):
    *earlier_refs, inverse_ref, logs_ref, total_ref = refs
    return_outer_kernel(
        base, first, halo_ref, outer_ref, edge_ref, scaled_ref, weight_ref, coef_ref, inverse_ref, total_ref
    )
    low = low_half(total_ref.shape[1:])
    tiles = total_ref.shape[2] // 128
    for c in range(REACH):
        outer, inner = sum((ref[c] for ref in earlier_refs), total_ref[c]), inner_ref[c]
        outer = outer + pltpu.roll(outer, SUB // 2, 0)
        inner = inner + pltpu.roll(inner, SUB // 2, 0)
        both = jnp.where(low, outer, inner)
        for t in range(tiles):
            logs_ref[rows_of(c * tiles + t), :] = both[:, t * 128 : (t + 1) * 128]
    logs_ref[rows_of(REACH * tiles), :] = weight_ref[rows_of(weight_ref.shape[0] // SUB - 1), :]


def merge_kernel(own_ref, other_ref, mass_ref, coef_ref, merged_ref, payload_ref):
    members, tiles = mass_ref.shape[0], merged_ref.shape[2] // 128
    both = lambda n: own_ref[rows_of(n), :] + other_ref[rows_of(n), :]
    scale = 1.0 / both(REACH * tiles)
    level = jnp.zeros((SUB, 128), jnp.float32)
    for c in range(REACH):
        for t in range(tiles):
            span = slice(t * 128, (t + 1) * 128)
            weighted = jnp.exp(both(c * tiles + t) * scale)
            merged_ref[c, :, span] = weighted / coef_ref[AREA, :, span]
            level = level + weighted
    level = level + pltpu.roll(level, SUB // 2, 0)
    spare = jnp.zeros((128 - members - SUB, 128), jnp.float32)
    table = jnp.concatenate([mass_ref[...], level, spare], axis=0)
    row = jnp.sum(table.T, axis=0, keepdims=True)
    payload_ref[...] = jnp.broadcast_to(row[None], payload_ref.shape)


def finish_kernel(cells, got_ref, merged_ref, inner_ref, *refs):
    *outer_refs, bary_ref, updated_ref, staged_ref, sem = refs
    members, lat = inner_ref.shape[1:]
    groups = members // SUB
    odd = odd_core()
    total = jnp.sum(got_ref[...], axis=0)
    table = jnp.broadcast_to(total, (128, 128)).T
    level = table[members : members + SUB, :]
    low = low_half((SUB, lat))
    wide = lambda v: jnp.concatenate([v] * (lat // 128), axis=1)
    inverse = wide(cells / level)
    outer, inner = [], []
    for c in range(REACH):
        both = merged_ref[c] * inverse
        swapped = pltpu.roll(both, SUB // 2, 0)
        outer.append(jnp.where(low, both, swapped))
        inner.append(jnp.where(low, swapped, both))
    bary = from_outside(outer + inner, odd)
    bary_ref[...] = jnp.swapaxes(jnp.stack(bary), 0, 1)[: SUB // 2]
    for group in range(groups):
        rows = slice(group * SUB, (group + 1) * SUB)
        factor = wide(table[rows, :] / cells)
        quotients = Chunked(outer_refs).stack(group) + stack_of(inner_ref, group)
        out = [b * factor * quotient for b, quotient in zip(bary, from_outside(quotients, odd))]
        span = pl.ds(group * SUB * SUB, SUB * SUB)
        staged_ref[span, :] = jnp.swapaxes(jnp.stack(out), 0, 1).reshape(SUB * SUB, lat)
        pltpu.make_async_copy(staged_ref.at[span, :], updated_ref.at[span, :], sem.at[group]).start()
    for group in range(groups):
        span = pl.ds(group * SUB * SUB, SUB * SUB)
        pltpu.make_async_copy(staged_ref.at[span, :], updated_ref.at[span, :], sem.at[group]).wait()


def shape(*dims):
    return jax.ShapeDtypeStruct(dims, jnp.float32)


def call(kernel, outs, *args, scratch=(), out_specs=None):
    return pl.pallas_call(
        kernel,
        out_shape=outs,
        in_specs=[SMEM if arg.ndim == 1 else VMEM for arg in args],
        out_specs=out_specs or (VMEM,) * len(outs),
        scratch_shapes=scratch,
        compiler_params=params(),
    )(*args)


def body(fields, scaling, counts, land_mask):
    members, levels, lon, lat = fields.shape
    tiles = lax.axis_size("tile")
    rows = members * levels
    cells = lon * tiles * lat
    half = shape(REACH, rows, lat)
    edge = shape(2 * REACH - 2, rows, lat)
    packed = shape(REACH, SUB, lat)
    chunks = chunk_groups(rows // SUB)
    bases = [sum(map(sum, chunks[:n])) for n in range(len(chunks))]
    parts = [shape(REACH, sum(own) * SUB, lat) for own in chunks]
    coef = jnp.asarray(coefficients(lat))
    with_mate = [(i, i ^ 1) for i in range(tiles)]
    with_neighbour = [(i, (i + (1 if i % 2 else -1)) % tiles) for i in range(tiles)]
    scaling = scaling.reshape(rows * lon, lat)
    fields = fields.reshape(rows * lon, lat)

    inner, *outer = call(spread_kernel, (half, *parts), scaling, coef)
    outer_halo = [lax.ppermute(part, "tile", with_neighbour) for part in outer]
    inner_halo = lax.ppermute(inner, "tile", with_mate)
    fields, inner = lax.optimization_barrier((fields, inner))
    v_inner, edges, filled, mass, weights = call(
        smooth_inner_kernel,
        (half, edge, half, shape(rows, 128), shape(rows + SUB, 128)),
        inner_halo,
        inner,
        fields,
        land_mask,
        counts,
        coef,
        *outer,
    )
    v_inner_halo = lax.ppermute(v_inner, "tile", with_mate)
    v_outer, v_outer_halo, places = [], [], []
    for base, sizes, halo, own in zip(bases, chunks, outer_halo, outer):
        outs = tuple(shape(REACH, size * SUB, lat) for size in sizes)
        values = call(partial(smooth_outer_kernel, base), outs, halo, own, edges, filled, coef)
        v_outer += values
        v_outer_halo += [lax.ppermute(value, "tile", with_neighbour) for value in values]
        places += [(base, base + sum(sizes[:n]), own) for n in range(len(sizes))]
    inverse_inner, edges, inner_logs = call(
        return_inner_kernel, (half, edge, packed), v_inner_halo, v_inner, inner, weights, coef, *v_outer
    )
    inverses, earlier = [inverse_inner], []
    for n, (base, first, own) in enumerate(places):
        if earlier:
            v_outer_halo[n], earlier[-1] = lax.optimization_barrier((v_outer_halo[n], earlier[-1]))
        operands = v_outer_halo[n], v_outer[n], edges, own, weights, coef
        part = shape(*v_outer[n].shape)
        if n < len(places) - 1:
            inverse, logs = call(partial(return_outer_kernel, base, first), (part, packed), *operands)
            earlier.append(logs)
        else:
            inverse, logs = call(
                partial(last_return_kernel, base, first),
                (part, shape((REACH * lat // 128 + 1) * SUB, 128)),
                *operands,
                inner_logs,
                *earlier,
                scratch=[pltpu.VMEM((REACH, SUB, lat), jnp.float32)],
            )
        inverses.append(inverse)
    other = lax.ppermute(logs, "mem", [(0, 1), (1, 0)])
    merged, payload = call(merge_kernel, (packed, shape(tiles, 1, 128)), logs, other, mass, coef)
    got = lax.all_to_all(payload, "tile", split_axis=0, concat_axis=0)
    barycenter, updated = call(
        partial(finish_kernel, float(cells)),
        (shape(levels, lon, lat), shape(rows * lon, lat)),
        got,
        merged,
        *inverses,
        scratch=[pltpu.VMEM((rows * lon, lat), jnp.float32), pltpu.SemaphoreType.DMA((rows // SUB,))],
        out_specs=(VMEM, HBM),
    )
    return barycenter, updated.reshape(members, levels, lon, lat)


def solution(mesh):
    return jax.shard_map(
        body,
        mesh=mesh,
        in_specs=(
            P("mem", None, "tile", None),
            P("mem", None, "tile", None),
            P("mem"),
            P("tile", None),
        ),
        out_specs=(P(None, "tile", None), P("mem", None, "tile", None)),
        check_vma=False,
    )
```

```python
import math
from functools import partial

import jax
import jax.numpy as jnp
import numpy as np
from jax import lax
from jax.experimental import pallas as pl
from jax.experimental.pallas import tpu as pltpu
from jax.sharding import PartitionSpec as P

BACKGROUND = 0.01
REACH = 4
SUB = 8
VMEM = pl.BlockSpec(memory_space=pltpu.VMEM)
SMEM = pl.BlockSpec(memory_space=pltpu.SMEM)
HBM = pl.BlockSpec(memory_space=pl.ANY)
AREA, ZONAL, NORTH, SOUTH, CENTER = range(5)


def coefficients(lat_cells):
    spacing = math.pi / lat_cells
    index = np.arange(lat_cells)
    latitude = -0.5 * math.pi + (index + 0.5) * spacing
    cell_area = np.cos(latitude)
    zonal = 0.2 * np.minimum(2.2, 1.0 / cell_area**2)
    north = np.where(index == lat_cells - 1, 0.0, 0.05 * np.cos(latitude + 0.5 * spacing) / cell_area)
    south = np.where(index == 0, 0.0, 0.05 * np.cos(latitude - 0.5 * spacing) / cell_area)
    center = 1.0 - 2.0 * zonal - north - south
    rows = np.stack([cell_area, zonal, north, south, center]).astype(np.float32)
    return np.ascontiguousarray(np.broadcast_to(rows[:, None, :], (5, SUB, lat_cells)))


def params(mib=12):
    return pltpu.CompilerParams(vmem_limit_bytes=mib * 2**20)


def rows_of(group):
    return pl.ds(group * SUB, SUB)


def block_of(group):
    return pl.ds(group * SUB * SUB, SUB * SUB)


def batches(last, first=0, size=4):
    return [range(start, min(start + size, last)) for start in range(first, last, size)]


def chunk_groups(groups):
    half = (groups + 1) // 2
    last = max(1, (groups - half) // 3)
    return [[half], [groups - half - last, last]]


class Chunked:
    def __init__(self, refs):
        self.refs = refs

    def stack(self, group, order=range(REACH)):
        for ref in self.refs:
            held = ref.shape[1] // SUB
            if group < held:
                return stack_of(ref, group, order)
            group -= held

    def put(self, group, values):
        for ref in self.refs:
            held = ref.shape[1] // SUB
            if 0 <= group < held:
                for c, value in enumerate(values):
                    ref[c, rows_of(group), :] = value
            group -= held


def by_longitude(block, lat):
    return jnp.swapaxes(block.reshape(SUB, SUB, lat), 0, 1)


def stack_of(ref, group, order=range(REACH)):
    return [ref[c, rows_of(group), :] for c in order]


def odd_core():
    return lax.rem(lax.axis_index("tile"), 2) == 1


def from_outside(columns, odd):
    last = len(columns) - 1
    return [jnp.where(odd, columns[last - c], columns[c]) for c in range(len(columns))]


def low_half(shape):
    return lax.broadcasted_iota(jnp.int32, shape, 0) < SUB // 2


def spread_kernel(scaling_ref, inner_ref, *outer_refs):
    groups, lat = inner_ref.shape[1] // SUB, inner_ref.shape[2]
    odd = odd_core()
    outer = Chunked(outer_refs)
    for group in range(groups):
        columns = from_outside(by_longitude(scaling_ref[block_of(group), :], lat), odd)
        outer.put(group, columns[:REACH])
        for c in range(REACH):
            inner_ref[c, rows_of(group), :] = columns[c + REACH]


def lane_fold(value):
    lat = value.shape[-1]
    total = value[:, :128]
    for t in range(1, lat // 128):
        total = total + value[:, t * 128 : (t + 1) * 128]
    return total


def diffuse(columns, coef_ref):
    lat = columns[0].shape[-1]
    return [
        coef_ref[CENTER] * here
        + coef_ref[ZONAL] * (west + east)
        + coef_ref[NORTH] * pltpu.roll(here, lat - 1, 1)
        + coef_ref[SOUTH] * pltpu.roll(here, 1, 1)
        for west, here, east in zip(columns[:-2], columns[1:-1], columns[2:])
    ]


def unit(values, coef_ref):
    return values


def by_area(values, coef_ref):
    return [value * coef_ref[AREA] for value in values]


def inner_half(batch, halo_ref, inner_ref, outer_refs, coef_ref, edge_ref, weigh=unit):
    outer = Chunked(outer_refs)
    columns = [outer.stack(g) + stack_of(inner_ref, g) + stack_of(halo_ref, g, (3, 2, 1, 0)) for g in batch]
    columns = [weigh(own, coef_ref) for own in columns]
    for s in range(REACH):
        columns = [diffuse(own, coef_ref) for own in columns]
        if s < REACH - 1:
            for own, group in zip(columns, batch):
                edge_ref[2 * s, rows_of(group), :] = own[0]
                edge_ref[2 * s + 1, rows_of(group), :] = own[1]
    return zip(batch, columns)


def outer_half(batch, first, halo_ref, outer_ref, edge_ref, coef_ref, weigh=unit):
    columns = [stack_of(halo_ref, g - first, (3, 2, 1, 0)) + stack_of(outer_ref, g - first, (0, 1)) for g in batch]
    columns = [weigh(own, coef_ref) for own in columns]
    for s in range(REACH):
        columns = [diffuse(own, coef_ref) for own in columns]
        if s < REACH - 1:
            columns = [own + stack_of(edge_ref, g, (2 * s, 2 * s + 1)) for own, g in zip(columns, batch)]
    return zip(batch, columns)


def smooth_inner_kernel(
    halo_ref, inner_ref, fields_ref, mask_ref, count_ref, coef_ref, *refs
):
    *outer_refs, out_ref, edge_ref, filled_ref, mass_ref, weight_ref = refs
    groups, lat = inner_ref.shape[1] // SUB, inner_ref.shape[2]
    odd = odd_core()
    low = low_half((SUB, 128))
    for group in range(groups):
        first, second = (count_ref[2 * group + n].astype(jnp.float32) for n in range(2))
        weight_ref[rows_of(group), :] = jnp.where(low, first, second)
    count = sum(count_ref[m] for m in range(2 * groups)).astype(jnp.float32)
    weight_ref[rows_of(groups), :] = jnp.full((SUB, 128), count)
    for batch in batches(groups):
        for group, smoothed in inner_half(
            batch, halo_ref, inner_ref, outer_refs, coef_ref, edge_ref, by_area
        ):
            fields = by_longitude(fields_ref[block_of(group), :], lat)
            filled = []
            for c in range(2 * REACH):
                valid = jnp.broadcast_to(mask_ref[c : c + 1, :], (SUB, lat)) == 1
                filled.append((jnp.where(valid, fields[c], 0.0) + BACKGROUND) * coef_ref[AREA])
            mass_ref[rows_of(group), :] = lane_fold(sum(filled))
            filled = from_outside(filled, odd)
            for c in range(REACH):
                filled_ref[c, rows_of(group), :] = filled[c]
                out_ref[c, rows_of(group), :] = filled[c + REACH] / smoothed[c]


def smooth_outer_kernel(first, halo_ref, outer_ref, edge_ref, filled_ref, coef_ref, *out_refs):
    last = first + outer_ref.shape[1] // SUB
    out = Chunked(out_refs)
    for batch in batches(last, first):
        for group, smoothed in outer_half(batch, first, halo_ref, outer_ref, edge_ref, coef_ref, by_area):
            filled = stack_of(filled_ref, group)
            out.put(group - first, [top / bottom for top, bottom in zip(filled, smoothed)])


def add_logs(group, held, result, scaled, weight_ref, inverse_ref, total_ref):
    lat = total_ref.shape[2]
    weight = jnp.concatenate([weight_ref[rows_of(group), :]] * (lat // 128), axis=1)
    for c in range(REACH):
        inverse_ref[c, rows_of(held), :] = 1.0 / result[c]
        total_ref[c] = total_ref[c] + weight * jnp.log(scaled[c] * result[c])


def return_inner_kernel(halo_ref, inner_ref, scaled_ref, weight_ref, coef_ref, *refs):
    *outer_refs, inverse_ref, edge_ref, total_ref = refs
    groups = inner_ref.shape[1] // SUB
    total_ref[...] = jnp.zeros_like(total_ref)
    for batch in batches(groups):
        for group, result in inner_half(batch, halo_ref, inner_ref, outer_refs, coef_ref, edge_ref):
            add_logs(group, group, result, stack_of(scaled_ref, group), weight_ref, inverse_ref, total_ref)


def return_outer_kernel(
    base, first, halo_ref, outer_ref, edge_ref, scaled_ref, weight_ref, coef_ref, inverse_ref, total_ref
):
    last = first + outer_ref.shape[1] // SUB
    total_ref[...] = jnp.zeros_like(total_ref)
    for batch in batches(last, first):
        for group, result in outer_half(batch, first, halo_ref, outer_ref, edge_ref, coef_ref):
            scaled = stack_of(scaled_ref, group - base)
            add_logs(group, group - first, result, scaled, weight_ref, inverse_ref, total_ref)


def last_return_kernel(
    base,
    first,
    halo_ref,
    outer_ref,
    edge_ref,
    scaled_ref,
    weight_ref,
    coef_ref,
    inner_ref,
    *refs,
):
    *earlier_refs, inverse_ref, logs_ref, total_ref = refs
    return_outer_kernel(
        base, first, halo_ref, outer_ref, edge_ref, scaled_ref, weight_ref, coef_ref, inverse_ref, total_ref
    )
    low = low_half(total_ref.shape[1:])
    tiles = total_ref.shape[2] // 128
    for c in range(REACH):
        outer, inner = sum((ref[c] for ref in earlier_refs), total_ref[c]), inner_ref[c]
        outer = outer + pltpu.roll(outer, SUB // 2, 0)
        inner = inner + pltpu.roll(inner, SUB // 2, 0)
        both = jnp.where(low, outer, inner)
        for t in range(tiles):
            logs_ref[rows_of(c * tiles + t), :] = both[:, t * 128 : (t + 1) * 128]
    logs_ref[rows_of(REACH * tiles), :] = weight_ref[rows_of(weight_ref.shape[0] // SUB - 1), :]


def merge_kernel(own_ref, other_ref, mass_ref, coef_ref, merged_ref, payload_ref):
    members, tiles = mass_ref.shape[0], merged_ref.shape[2] // 128
    both = lambda n: own_ref[rows_of(n), :] + other_ref[rows_of(n), :]
    scale = 1.0 / both(REACH * tiles)
    level = jnp.zeros((SUB, 128), jnp.float32)
    for c in range(REACH):
        for t in range(tiles):
            span = slice(t * 128, (t + 1) * 128)
            merged = jnp.exp(both(c * tiles + t) * scale)
            merged_ref[c, :, span] = merged
            level = level + merged * coef_ref[AREA, :, span]
    level = level + pltpu.roll(level, SUB // 2, 0)
    spare = jnp.zeros((128 - members - SUB, 128), jnp.float32)
    table = jnp.concatenate([mass_ref[...], level, spare], axis=0)
    row = jnp.sum(table.T, axis=0, keepdims=True)
    payload_ref[...] = jnp.broadcast_to(row[None], payload_ref.shape)


def ratio_kernel(merged_ref, inner_ref, *refs):
    *outer_refs, ratio_ref, field_ref = refs
    members, lat = inner_ref.shape[1:]
    odd = odd_core()
    low = low_half((SUB, lat))
    outer, inner = [], []
    for c in range(REACH):
        both = merged_ref[c]
        swapped = pltpu.roll(both, SUB // 2, 0)
        outer.append(jnp.where(low, both, swapped))
        inner.append(jnp.where(low, swapped, both))
    merged = from_outside(outer + inner, odd)
    field_ref[...] = jnp.swapaxes(jnp.stack(merged), 0, 1)[: SUB // 2]
    for group in range(members // SUB):
        quotients = Chunked(outer_refs).stack(group) + stack_of(inner_ref, group)
        out = [m * quotient for m, quotient in zip(merged, from_outside(quotients, odd))]
        ratio_ref[block_of(group), :] = jnp.swapaxes(jnp.stack(out), 0, 1).reshape(SUB * SUB, lat)


def finish_kernel(cells, got_ref, ratio_ref, field_ref, bary_ref, updated_ref, factor_ref, staged_ref, sem):
    lat = ratio_ref.shape[1]
    groups = ratio_ref.shape[0] // (SUB * SUB)
    members = groups * SUB
    total = jnp.sum(got_ref[...], axis=0)
    factor_ref[...] = jnp.broadcast_to(total, (128, 128)).T
    level = 1.0 / factor_ref[members : members + SUB, :]
    for group in range(groups):
        factor_ref[rows_of(group), :] = factor_ref[rows_of(group), :] * level
    factor_ref[members : members + SUB, :] = level * cells
    wide = lambda n: jnp.concatenate([jnp.broadcast_to(factor_ref[n : n + 1, :], (SUB, 128))] * (lat // 128), axis=1)
    copies = []
    for group in range(groups):
        for n in range(group * SUB, (group + 1) * SUB):
            staged_ref[rows_of(n), :] = ratio_ref[rows_of(n), :] * wide(n)
        span = block_of(group)
        copies.append(pltpu.make_async_copy(staged_ref.at[span, :], updated_ref.at[span, :], sem.at[group]))
        copies[-1].start()
    for n in range(SUB // 2):
        bary_ref[n] = field_ref[n] * wide(members + n)
    for copy in copies:
        copy.wait()


def shape(*dims):
    return jax.ShapeDtypeStruct(dims, jnp.float32)


def call(kernel, outs, *args, scratch=(), out_specs=None):
    return pl.pallas_call(
        kernel,
        out_shape=outs,
        in_specs=[SMEM if arg.ndim == 1 else VMEM for arg in args],
        out_specs=out_specs or (VMEM,) * len(outs),
        scratch_shapes=scratch,
        compiler_params=params(),
    )(*args)


def body(fields, scaling, counts, land_mask):
    members, levels, lon, lat = fields.shape
    tiles = lax.axis_size("tile")
    rows = members * levels
    cells = lon * tiles * lat
    half = shape(REACH, rows, lat)
    edge = shape(2 * REACH - 2, rows, lat)
    packed = shape(REACH, SUB, lat)
    chunks = chunk_groups(rows // SUB)
    bases = [sum(map(sum, chunks[:n])) for n in range(len(chunks))]
    parts = [shape(REACH, sum(own) * SUB, lat) for own in chunks]
    coef = jnp.asarray(coefficients(lat))
    with_mate = [(i, i ^ 1) for i in range(tiles)]
    with_neighbour = [(i, (i + (1 if i % 2 else -1)) % tiles) for i in range(tiles)]
    scaling = scaling.reshape(rows * lon, lat)
    fields = fields.reshape(rows * lon, lat)

    inner, *outer = call(spread_kernel, (half, *parts), scaling)
    outer_halo = [lax.ppermute(part, "tile", with_neighbour) for part in outer]
    inner_halo = lax.ppermute(inner, "tile", with_mate)
    fields, inner = lax.optimization_barrier((fields, inner))
    v_inner, edges, filled, mass, weights = call(
        smooth_inner_kernel,
        (half, edge, half, shape(rows, 128), shape(rows + SUB, 128)),
        inner_halo,
        inner,
        fields,
        land_mask,
        counts,
        coef,
        *outer,
    )
    v_inner_halo = lax.ppermute(v_inner, "tile", with_mate)
    v_outer, v_outer_halo, places = [], [], []
    for base, sizes, halo, own in zip(bases, chunks, outer_halo, outer):
        outs = tuple(shape(REACH, size * SUB, lat) for size in sizes)
        values = call(partial(smooth_outer_kernel, base), outs, halo, own, edges, filled, coef)
        v_outer += values
        v_outer_halo += [lax.ppermute(value, "tile", with_neighbour) for value in values]
        places += [(base, base + sum(sizes[:n]), own) for n in range(len(sizes))]
    inverse_inner, edges, inner_logs = call(
        return_inner_kernel, (half, edge, packed), v_inner_halo, v_inner, inner, weights, coef, *v_outer
    )
    inverses, earlier = [inverse_inner], []
    for n, (base, first, own) in enumerate(places):
        if earlier:
            v_outer_halo[n], earlier[-1] = lax.optimization_barrier((v_outer_halo[n], earlier[-1]))
        operands = v_outer_halo[n], v_outer[n], edges, own, weights, coef
        part = shape(*v_outer[n].shape)
        if n < len(places) - 1:
            inverse, logs = call(partial(return_outer_kernel, base, first), (part, packed), *operands)
            earlier.append(logs)
        else:
            inverse, logs = call(
                partial(last_return_kernel, base, first),
                (part, shape((REACH * lat // 128 + 1) * SUB, 128)),
                *operands,
                inner_logs,
                *earlier,
                scratch=[pltpu.VMEM((REACH, SUB, lat), jnp.float32)],
            )
        inverses.append(inverse)
    other = lax.ppermute(logs, "mem", [(0, 1), (1, 0)])
    merged, payload = call(merge_kernel, (packed, shape(tiles, 1, 128)), logs, other, mass, coef)
    ratio, field = call(ratio_kernel, (shape(rows * lon, lat), shape(levels, lon, lat)), merged, *inverses)
    got = lax.all_to_all(payload, "tile", split_axis=0, concat_axis=0)
    barycenter, updated = call(
        partial(finish_kernel, float(cells)),
        (shape(levels, lon, lat), shape(rows * lon, lat)),
        got,
        ratio,
        field,
        scratch=[
            pltpu.VMEM((128, 128), jnp.float32),
            pltpu.VMEM((rows * lon, lat), jnp.float32),
            pltpu.SemaphoreType.DMA((rows // SUB,)),
        ],
        out_specs=(VMEM, HBM),
    )
    return barycenter, updated.reshape(members, levels, lon, lat)


def solution(mesh):
    return jax.shard_map(
        body,
        mesh=mesh,
        in_specs=(
            P("mem", None, "tile", None),
            P("mem", None, "tile", None),
            P("mem"),
            P("tile", None),
        ),
        out_specs=(P(None, "tile", None), P("mem", None, "tile", None)),
        check_vma=False,
    )
```

```python
import math
from functools import partial

import jax
import jax.numpy as jnp
import numpy as np
from jax import lax
from jax.experimental import pallas as pl
from jax.experimental.pallas import tpu as pltpu
from jax.sharding import PartitionSpec as P

BACKGROUND = 0.01
REACH = 4
SUB = 8
VMEM = pl.BlockSpec(memory_space=pltpu.VMEM)
SMEM = pl.BlockSpec(memory_space=pltpu.SMEM)
HBM = pl.BlockSpec(memory_space=pl.ANY)
AREA, ZONAL, NORTH, SOUTH, CENTER = range(5)


def coefficients(lat_cells):
    spacing = math.pi / lat_cells
    index = np.arange(lat_cells)
    latitude = -0.5 * math.pi + (index + 0.5) * spacing
    cell_area = np.cos(latitude)
    zonal = 0.2 * np.minimum(2.2, 1.0 / cell_area**2)
    north = np.where(index == lat_cells - 1, 0.0, 0.05 * np.cos(latitude + 0.5 * spacing) / cell_area)
    south = np.where(index == 0, 0.0, 0.05 * np.cos(latitude - 0.5 * spacing) / cell_area)
    center = 1.0 - 2.0 * zonal - north - south
    rows = np.stack([cell_area, zonal, north, south, center]).astype(np.float32)
    return np.ascontiguousarray(np.broadcast_to(rows[:, None, :], (5, SUB, lat_cells)))


def params(mib=12):
    return pltpu.CompilerParams(vmem_limit_bytes=mib * 2**20)


def rows_of(group):
    return pl.ds(group * SUB, SUB)


def block_of(group):
    return pl.ds(group * SUB * SUB, SUB * SUB)


def batches(last, first=0, size=4):
    return [range(start, min(start + size, last)) for start in range(first, last, size)]


def chunk_groups(groups):
    half = (groups + 1) // 2
    last = max(1, (groups - half) // 3)
    return [[half], [groups - half - last, last]]


class Chunked:
    def __init__(self, refs):
        self.refs = refs

    def stack(self, group, order=range(REACH)):
        for ref in self.refs:
            held = ref.shape[1] // SUB
            if group < held:
                return stack_of(ref, group, order)
            group -= held

    def put(self, group, values):
        for ref in self.refs:
            held = ref.shape[1] // SUB
            if 0 <= group < held:
                for c, value in enumerate(values):
                    ref[c, rows_of(group), :] = value
            group -= held


def by_longitude(block, lat):
    return jnp.swapaxes(block.reshape(SUB, SUB, lat), 0, 1)


def stack_of(ref, group, order=range(REACH)):
    return [ref[c, rows_of(group), :] for c in order]


def odd_core():
    return lax.rem(lax.axis_index("tile"), 2) == 1


def from_outside(columns, odd):
    last = len(columns) - 1
    return [jnp.where(odd, columns[last - c], columns[c]) for c in range(len(columns))]


def low_half(shape):
    return lax.broadcasted_iota(jnp.int32, shape, 0) < SUB // 2


def spread_kernel(scaling_ref, inner_ref, *outer_refs):
    groups, lat = inner_ref.shape[1] // SUB, inner_ref.shape[2]
    odd = odd_core()
    outer = Chunked(outer_refs)
    for group in range(groups):
        columns = from_outside(by_longitude(scaling_ref[block_of(group), :], lat), odd)
        outer.put(group, columns[:REACH])
        for c in range(REACH):
            inner_ref[c, rows_of(group), :] = columns[c + REACH]


def lane_fold(value):
    lat = value.shape[-1]
    total = value[:, :128]
    for t in range(1, lat // 128):
        total = total + value[:, t * 128 : (t + 1) * 128]
    return total


def diffuse(columns, coef_ref):
    lat = columns[0].shape[-1]
    return [
        coef_ref[CENTER] * here
        + coef_ref[ZONAL] * (west + east)
        + coef_ref[NORTH] * pltpu.roll(here, lat - 1, 1)
        + coef_ref[SOUTH] * pltpu.roll(here, 1, 1)
        for west, here, east in zip(columns[:-2], columns[1:-1], columns[2:])
    ]


def unit(values, coef_ref):
    return values


def by_area(values, coef_ref):
    return [value * coef_ref[AREA] for value in values]


def inner_half(batch, halo_ref, inner_ref, outer_refs, coef_ref, edge_ref, weigh=unit):
    outer = Chunked(outer_refs)
    columns = [outer.stack(g) + stack_of(inner_ref, g) + stack_of(halo_ref, g, (3, 2, 1, 0)) for g in batch]
    columns = [weigh(own, coef_ref) for own in columns]
    for s in range(REACH):
        columns = [diffuse(own, coef_ref) for own in columns]
        if s < REACH - 1:
            for own, group in zip(columns, batch):
                edge_ref[2 * s, rows_of(group), :] = own[0]
                edge_ref[2 * s + 1, rows_of(group), :] = own[1]
    return zip(batch, columns)


def outer_half(batch, first, halo_ref, outer_ref, edge_ref, coef_ref, weigh=unit):
    columns = [stack_of(halo_ref, g - first, (3, 2, 1, 0)) + stack_of(outer_ref, g - first, (0, 1)) for g in batch]
    columns = [weigh(own, coef_ref) for own in columns]
    for s in range(REACH):
        columns = [diffuse(own, coef_ref) for own in columns]
        if s < REACH - 1:
            columns = [own + stack_of(edge_ref, g, (2 * s, 2 * s + 1)) for own, g in zip(columns, batch)]
    return zip(batch, columns)


def smooth_inner_kernel(
    halo_ref, inner_ref, fields_ref, mask_ref, count_ref, coef_ref, *refs
):
    *outer_refs, out_ref, edge_ref, filled_ref, mass_ref, weight_ref = refs
    groups, lat = inner_ref.shape[1] // SUB, inner_ref.shape[2]
    odd = odd_core()
    low = low_half((SUB, 128))
    for group in range(groups):
        first, second = (count_ref[2 * group + n].astype(jnp.float32) for n in range(2))
        weight_ref[rows_of(group), :] = jnp.where(low, first, second)
    count = sum(count_ref[m] for m in range(2 * groups)).astype(jnp.float32)
    weight_ref[rows_of(groups), :] = jnp.full((SUB, 128), count)
    for batch in batches(groups):
        for group, smoothed in inner_half(
            batch, halo_ref, inner_ref, outer_refs, coef_ref, edge_ref, by_area
        ):
            fields = by_longitude(fields_ref[block_of(group), :], lat)
            filled = []
            for c in range(2 * REACH):
                valid = jnp.broadcast_to(mask_ref[c : c + 1, :], (SUB, lat)) == 1
                filled.append((jnp.where(valid, fields[c], 0.0) + BACKGROUND) * coef_ref[AREA])
            mass_ref[rows_of(group), :] = lane_fold(sum(filled))
            filled = from_outside(filled, odd)
            for c in range(REACH):
                filled_ref[c, rows_of(group), :] = filled[c]
                out_ref[c, rows_of(group), :] = filled[c + REACH] / smoothed[c]


def smooth_outer_kernel(first, halo_ref, outer_ref, edge_ref, filled_ref, coef_ref, *out_refs):
    last = first + outer_ref.shape[1] // SUB
    out = Chunked(out_refs)
    for batch in batches(last, first):
        for group, smoothed in outer_half(batch, first, halo_ref, outer_ref, edge_ref, coef_ref, by_area):
            filled = stack_of(filled_ref, group)
            out.put(group - first, [top / bottom for top, bottom in zip(filled, smoothed)])


def add_logs(group, held, result, scaled, weight_ref, inverse_ref, total_ref):
    lat = total_ref.shape[2]
    weight = jnp.concatenate([weight_ref[rows_of(group), :]] * (lat // 128), axis=1)
    for c in range(REACH):
        inverse_ref[c, rows_of(held), :] = 1.0 / result[c]
        total_ref[c] = total_ref[c] + weight * jnp.log(scaled[c] * result[c])


def return_inner_kernel(halo_ref, inner_ref, scaled_ref, weight_ref, coef_ref, *refs):
    *outer_refs, inverse_ref, edge_ref, total_ref = refs
    groups = inner_ref.shape[1] // SUB
    total_ref[...] = jnp.zeros_like(total_ref)
    for batch in batches(groups):
        for group, result in inner_half(batch, halo_ref, inner_ref, outer_refs, coef_ref, edge_ref):
            add_logs(group, group, result, stack_of(scaled_ref, group), weight_ref, inverse_ref, total_ref)


def return_outer_kernel(
    base, first, halo_ref, outer_ref, edge_ref, scaled_ref, weight_ref, coef_ref, inverse_ref, total_ref
):
    last = first + outer_ref.shape[1] // SUB
    total_ref[...] = jnp.zeros_like(total_ref)
    for batch in batches(last, first):
        for group, result in outer_half(batch, first, halo_ref, outer_ref, edge_ref, coef_ref):
            scaled = stack_of(scaled_ref, group - base)
            add_logs(group, group - first, result, scaled, weight_ref, inverse_ref, total_ref)


def last_return_kernel(
    base,
    first,
    halo_ref,
    outer_ref,
    edge_ref,
    scaled_ref,
    weight_ref,
    coef_ref,
    inner_ref,
    *refs,
):
    *earlier_refs, inverse_ref, logs_ref, total_ref = refs
    return_outer_kernel(
        base, first, halo_ref, outer_ref, edge_ref, scaled_ref, weight_ref, coef_ref, inverse_ref, total_ref
    )
    low = low_half(total_ref.shape[1:])
    tiles = total_ref.shape[2] // 128
    for c in range(REACH):
        outer, inner = sum((ref[c] for ref in earlier_refs), total_ref[c]), inner_ref[c]
        outer = outer + pltpu.roll(outer, SUB // 2, 0)
        inner = inner + pltpu.roll(inner, SUB // 2, 0)
        both = jnp.where(low, outer, inner)
        for t in range(tiles):
            logs_ref[rows_of(c * tiles + t), :] = both[:, t * 128 : (t + 1) * 128]
    logs_ref[rows_of(REACH * tiles), :] = weight_ref[rows_of(weight_ref.shape[0] // SUB - 1), :]


def merge_kernel(own_ref, other_ref, mass_ref, coef_ref, merged_ref, payload_ref):
    members, tiles = mass_ref.shape[0], merged_ref.shape[2] // 128
    both = lambda n: own_ref[rows_of(n), :] + other_ref[rows_of(n), :]
    scale = 1.0 / both(REACH * tiles)
    level = jnp.zeros((SUB, 128), jnp.float32)
    for c in range(REACH):
        for t in range(tiles):
            span = slice(t * 128, (t + 1) * 128)
            merged = jnp.exp(both(c * tiles + t) * scale)
            merged_ref[c, :, span] = merged
            level = level + merged * coef_ref[AREA, :, span]
    level = level + pltpu.roll(level, SUB // 2, 0)
    spare = jnp.zeros((128 - members - SUB, 128), jnp.float32)
    table = jnp.concatenate([mass_ref[...], level, spare], axis=0)
    row = jnp.sum(table.T, axis=0, keepdims=True)
    payload_ref[...] = jnp.broadcast_to(row[None], payload_ref.shape)


def finish_kernel(cells, got_ref, merged_ref, inner_ref, *refs):
    *outer_refs, bary_ref, updated_ref, staged_ref, sem = refs
    members, lat = inner_ref.shape[1:]
    groups = members // SUB
    odd = odd_core()
    total = jnp.sum(got_ref[...], axis=0)
    table = jnp.broadcast_to(total, (128, 128)).T
    level = table[members : members + SUB, :]
    low = low_half((SUB, lat))
    wide = lambda v: jnp.concatenate([v] * (lat // 128), axis=1)
    inverse = wide(cells / level)
    outer, inner = [], []
    for c in range(REACH):
        both = merged_ref[c] * inverse
        swapped = pltpu.roll(both, SUB // 2, 0)
        outer.append(jnp.where(low, both, swapped))
        inner.append(jnp.where(low, swapped, both))
    bary = from_outside(outer + inner, odd)
    bary_ref[...] = jnp.swapaxes(jnp.stack(bary), 0, 1)[: SUB // 2]
    for group in range(groups):
        rows = slice(group * SUB, (group + 1) * SUB)
        factor = wide(table[rows, :] / cells)
        quotients = Chunked(outer_refs).stack(group) + stack_of(inner_ref, group)
        out = [b * factor * quotient for b, quotient in zip(bary, from_outside(quotients, odd))]
        span = pl.ds(group * SUB * SUB, SUB * SUB)
        staged_ref[span, :] = jnp.swapaxes(jnp.stack(out), 0, 1).reshape(SUB * SUB, lat)
        pltpu.make_async_copy(staged_ref.at[span, :], updated_ref.at[span, :], sem.at[group]).start()
    for group in range(groups):
        span = pl.ds(group * SUB * SUB, SUB * SUB)
        pltpu.make_async_copy(staged_ref.at[span, :], updated_ref.at[span, :], sem.at[group]).wait()


def shape(*dims):
    return jax.ShapeDtypeStruct(dims, jnp.float32)


def call(kernel, outs, *args, scratch=(), out_specs=None):
    return pl.pallas_call(
        kernel,
        out_shape=outs,
        in_specs=[SMEM if arg.ndim == 1 else VMEM for arg in args],
        out_specs=out_specs or (VMEM,) * len(outs),
        scratch_shapes=scratch,
        compiler_params=params(),
    )(*args)


def body(fields, scaling, counts, land_mask):
    members, levels, lon, lat = fields.shape
    tiles = lax.axis_size("tile")
    rows = members * levels
    cells = lon * tiles * lat
    half = shape(REACH, rows, lat)
    edge = shape(2 * REACH - 2, rows, lat)
    packed = shape(REACH, SUB, lat)
    chunks = chunk_groups(rows // SUB)
    bases = [sum(map(sum, chunks[:n])) for n in range(len(chunks))]
    parts = [shape(REACH, sum(own) * SUB, lat) for own in chunks]
    coef = jnp.asarray(coefficients(lat))
    with_mate = [(i, i ^ 1) for i in range(tiles)]
    with_neighbour = [(i, (i + (1 if i % 2 else -1)) % tiles) for i in range(tiles)]
    scaling = scaling.reshape(rows * lon, lat)
    fields = fields.reshape(rows * lon, lat)

    inner, *outer = call(spread_kernel, (half, *parts), scaling)
    outer_halo = [lax.ppermute(part, "tile", with_neighbour) for part in outer]
    inner_halo = lax.ppermute(inner, "tile", with_mate)
    fields, inner = lax.optimization_barrier((fields, inner))
    v_inner, edges, filled, mass, weights = call(
        smooth_inner_kernel,
        (half, edge, half, shape(rows, 128), shape(rows + SUB, 128)),
        inner_halo,
        inner,
        fields,
        land_mask,
        counts,
        coef,
        *outer,
    )
    v_inner_halo = lax.ppermute(v_inner, "tile", with_mate)
    v_outer, v_outer_halo, places = [], [], []
    for base, sizes, halo, own in zip(bases, chunks, outer_halo, outer):
        outs = tuple(shape(REACH, size * SUB, lat) for size in sizes)
        values = call(partial(smooth_outer_kernel, base), outs, halo, own, edges, filled, coef)
        v_outer += values
        v_outer_halo += [lax.ppermute(value, "tile", with_neighbour) for value in values]
        places += [(base, base + sum(sizes[:n]), own) for n in range(len(sizes))]
    inverse_inner, edges, inner_logs = call(
        return_inner_kernel, (half, edge, packed), v_inner_halo, v_inner, inner, weights, coef, *v_outer
    )
    inverses, earlier = [inverse_inner], []
    for n, (base, first, own) in enumerate(places):
        if earlier:
            v_outer_halo[n], earlier[-1] = lax.optimization_barrier((v_outer_halo[n], earlier[-1]))
        operands = v_outer_halo[n], v_outer[n], edges, own, weights, coef
        part = shape(*v_outer[n].shape)
        if n < len(places) - 1:
            inverse, logs = call(partial(return_outer_kernel, base, first), (part, packed), *operands)
            earlier.append(logs)
        else:
            inverse, logs = call(
                partial(last_return_kernel, base, first),
                (part, shape((REACH * lat // 128 + 1) * SUB, 128)),
                *operands,
                inner_logs,
                *earlier,
                scratch=[pltpu.VMEM((REACH, SUB, lat), jnp.float32)],
            )
        inverses.append(inverse)
    other = lax.ppermute(logs, "mem", [(0, 1), (1, 0)])
    merged, payload = call(merge_kernel, (packed, shape(tiles, 1, 128)), logs, other, mass, coef)
    got = lax.all_to_all(payload, "tile", split_axis=0, concat_axis=0)
    barycenter, updated = call(
        partial(finish_kernel, float(cells)),
        (shape(levels, lon, lat), shape(rows * lon, lat)),
        got,
        merged,
        *inverses,
        scratch=[pltpu.VMEM((rows * lon, lat), jnp.float32), pltpu.SemaphoreType.DMA((rows // SUB,))],
        out_specs=(VMEM, HBM),
    )
    return barycenter, updated.reshape(members, levels, lon, lat)


def solution(mesh):
    return jax.shard_map(
        body,
        mesh=mesh,
        in_specs=(
            P("mem", None, "tile", None),
            P("mem", None, "tile", None),
            P("mem"),
            P("tile", None),
        ),
        out_specs=(P(None, "tile", None), P("mem", None, "tile", None)),
        check_vma=False,
    )
```

```python
import math
from functools import partial

import jax
import jax.numpy as jnp
import numpy as np
from jax import lax
from jax.experimental import pallas as pl
from jax.experimental.pallas import tpu as pltpu
from jax.sharding import PartitionSpec as P

BACKGROUND = 0.01
REACH = 4
SUB = 8
VMEM = pl.BlockSpec(memory_space=pltpu.VMEM)
SMEM = pl.BlockSpec(memory_space=pltpu.SMEM)
HBM = pl.BlockSpec(memory_space=pl.ANY)
AREA, ZONAL, NORTH, SOUTH, CENTER = range(5)


def coefficients(lat_cells):
    spacing = math.pi / lat_cells
    index = np.arange(lat_cells)
    latitude = -0.5 * math.pi + (index + 0.5) * spacing
    cell_area = np.cos(latitude)
    zonal = 0.2 * np.minimum(2.2, 1.0 / cell_area**2)
    north = np.where(index == lat_cells - 1, 0.0, 0.05 * np.cos(latitude + 0.5 * spacing) / cell_area)
    south = np.where(index == 0, 0.0, 0.05 * np.cos(latitude - 0.5 * spacing) / cell_area)
    center = 1.0 - 2.0 * zonal - north - south
    rows = np.stack([cell_area, zonal, north, south, center]).astype(np.float32)
    return np.ascontiguousarray(np.broadcast_to(rows[:, None, :], (5, SUB, lat_cells)))


def params(mib=12):
    return pltpu.CompilerParams(vmem_limit_bytes=mib * 2**20)


def rows_of(group):
    return pl.ds(group * SUB, SUB)


def block_of(group):
    return pl.ds(group * SUB * SUB, SUB * SUB)


def batches(last, first=0, size=4):
    return [range(start, min(start + size, last)) for start in range(first, last, size)]


def chunk_groups(groups):
    half = (groups + 1) // 2
    last = max(1, (groups - half) // 3)
    return [[half], [groups - half - last, last]]


class Chunked:
    def __init__(self, refs):
        self.refs = refs

    def stack(self, group, order=range(REACH)):
        for ref in self.refs:
            held = ref.shape[1] // SUB
            if group < held:
                return stack_of(ref, group, order)
            group -= held

    def put(self, group, values):
        for ref in self.refs:
            held = ref.shape[1] // SUB
            if 0 <= group < held:
                for c, value in enumerate(values):
                    ref[c, rows_of(group), :] = value
            group -= held


def by_longitude(block, lat):
    return jnp.swapaxes(block.reshape(SUB, SUB, lat), 0, 1)


def stack_of(ref, group, order=range(REACH)):
    return [ref[c, rows_of(group), :] for c in order]


def odd_core():
    return lax.rem(lax.axis_index("tile"), 2) == 1


def from_outside(columns, odd):
    last = len(columns) - 1
    return [jnp.where(odd, columns[last - c], columns[c]) for c in range(len(columns))]


def low_half(shape):
    return lax.broadcasted_iota(jnp.int32, shape, 0) < SUB // 2


def spread_kernel(scaling_ref, inner_ref, *outer_refs):
    groups, lat = inner_ref.shape[1] // SUB, inner_ref.shape[2]
    odd = odd_core()
    outer = Chunked(outer_refs)
    for group in range(groups):
        columns = from_outside(by_longitude(scaling_ref[block_of(group), :], lat), odd)
        outer.put(group, columns[:REACH])
        for c in range(REACH):
            inner_ref[c, rows_of(group), :] = columns[c + REACH]


def lane_fold(value):
    lat = value.shape[-1]
    total = value[:, :128]
    for t in range(1, lat // 128):
        total = total + value[:, t * 128 : (t + 1) * 128]
    return total


def diffuse(columns, coef_ref):
    lat = columns[0].shape[-1]
    return [
        coef_ref[CENTER] * here
        + coef_ref[ZONAL] * (west + east)
        + coef_ref[NORTH] * pltpu.roll(here, lat - 1, 1)
        + coef_ref[SOUTH] * pltpu.roll(here, 1, 1)
        for west, here, east in zip(columns[:-2], columns[1:-1], columns[2:])
    ]


def unit(values, coef_ref):
    return values


def by_area(values, coef_ref):
    return [value * coef_ref[AREA] for value in values]


def inner_half(batch, halo_ref, inner_ref, outer_refs, coef_ref, edge_ref, weigh=unit):
    outer = Chunked(outer_refs)
    columns = [outer.stack(g) + stack_of(inner_ref, g) + stack_of(halo_ref, g, (3, 2, 1, 0)) for g in batch]
    columns = [weigh(own, coef_ref) for own in columns]
    for s in range(REACH):
        columns = [diffuse(own, coef_ref) for own in columns]
        if s < REACH - 1:
            for own, group in zip(columns, batch):
                edge_ref[2 * s, rows_of(group), :] = own[0]
                edge_ref[2 * s + 1, rows_of(group), :] = own[1]
    return zip(batch, columns)


def outer_half(batch, first, halo_ref, outer_ref, edge_ref, coef_ref, weigh=unit):
    columns = [stack_of(halo_ref, g - first, (3, 2, 1, 0)) + stack_of(outer_ref, g - first, (0, 1)) for g in batch]
    columns = [weigh(own, coef_ref) for own in columns]
    for s in range(REACH):
        columns = [diffuse(own, coef_ref) for own in columns]
        if s < REACH - 1:
            columns = [own + stack_of(edge_ref, g, (2 * s, 2 * s + 1)) for own, g in zip(columns, batch)]
    return zip(batch, columns)


def smooth_inner_kernel(
    halo_ref, inner_ref, fields_ref, mask_ref, count_ref, coef_ref, *refs
):
    *outer_refs, out_ref, edge_ref, filled_ref, mass_ref, weight_ref = refs
    groups, lat = inner_ref.shape[1] // SUB, inner_ref.shape[2]
    odd = odd_core()
    low = low_half((SUB, 128))
    for group in range(groups):
        first, second = (count_ref[2 * group + n].astype(jnp.float32) for n in range(2))
        weight_ref[rows_of(group), :] = jnp.where(low, first, second)
    count = sum(count_ref[m] for m in range(2 * groups)).astype(jnp.float32)
    weight_ref[rows_of(groups), :] = jnp.full((SUB, 128), count)
    for batch in batches(groups):
        for group, smoothed in inner_half(
            batch, halo_ref, inner_ref, outer_refs, coef_ref, edge_ref, by_area
        ):
            fields = by_longitude(fields_ref[block_of(group), :], lat)
            filled = []
            for c in range(2 * REACH):
                valid = jnp.broadcast_to(mask_ref[c : c + 1, :], (SUB, lat)) == 1
                filled.append((jnp.where(valid, fields[c], 0.0) + BACKGROUND) * coef_ref[AREA])
            mass_ref[rows_of(group), :] = lane_fold(sum(filled))
            filled = from_outside(filled, odd)
            for c in range(REACH):
                filled_ref[c, rows_of(group), :] = filled[c]
                out_ref[c, rows_of(group), :] = filled[c + REACH] / smoothed[c]


def smooth_outer_kernel(first, halo_ref, outer_ref, edge_ref, filled_ref, coef_ref, *out_refs):
    last = first + outer_ref.shape[1] // SUB
    out = Chunked(out_refs)
    for batch in batches(last, first):
        for group, smoothed in outer_half(batch, first, halo_ref, outer_ref, edge_ref, coef_ref, by_area):
            filled = stack_of(filled_ref, group)
            out.put(group - first, [top / bottom for top, bottom in zip(filled, smoothed)])


def add_logs(group, held, result, scaled, weight_ref, inverse_ref, total_ref):
    lat = total_ref.shape[2]
    weight = jnp.concatenate([weight_ref[rows_of(group), :]] * (lat // 128), axis=1)
    for c in range(REACH):
        inverse_ref[c, rows_of(held), :] = 1.0 / result[c]
        total_ref[c] = total_ref[c] + weight * jnp.log(scaled[c] * result[c])


def return_inner_kernel(halo_ref, inner_ref, scaled_ref, weight_ref, coef_ref, *refs):
    *outer_refs, inverse_ref, edge_ref, total_ref = refs
    groups = inner_ref.shape[1] // SUB
    total_ref[...] = jnp.zeros_like(total_ref)
    for batch in batches(groups):
        for group, result in inner_half(batch, halo_ref, inner_ref, outer_refs, coef_ref, edge_ref):
            add_logs(group, group, result, stack_of(scaled_ref, group), weight_ref, inverse_ref, total_ref)


def return_outer_kernel(
    base, first, halo_ref, outer_ref, edge_ref, scaled_ref, weight_ref, coef_ref, inverse_ref, total_ref
):
    last = first + outer_ref.shape[1] // SUB
    total_ref[...] = jnp.zeros_like(total_ref)
    for batch in batches(last, first):
        for group, result in outer_half(batch, first, halo_ref, outer_ref, edge_ref, coef_ref):
            scaled = stack_of(scaled_ref, group - base)
            add_logs(group, group - first, result, scaled, weight_ref, inverse_ref, total_ref)


def last_return_kernel(
    base,
    first,
    halo_ref,
    outer_ref,
    edge_ref,
    scaled_ref,
    weight_ref,
    coef_ref,
    inner_ref,
    *refs,
):
    *earlier_refs, inverse_ref, logs_ref, total_ref = refs
    return_outer_kernel(
        base, first, halo_ref, outer_ref, edge_ref, scaled_ref, weight_ref, coef_ref, inverse_ref, total_ref
    )
    low = low_half(total_ref.shape[1:])
    tiles = total_ref.shape[2] // 128
    for c in range(REACH):
        outer, inner = sum((ref[c] for ref in earlier_refs), total_ref[c]), inner_ref[c]
        outer = outer + pltpu.roll(outer, SUB // 2, 0)
        inner = inner + pltpu.roll(inner, SUB // 2, 0)
        both = jnp.where(low, outer, inner)
        for t in range(tiles):
            logs_ref[rows_of(c * tiles + t), :] = both[:, t * 128 : (t + 1) * 128]
    logs_ref[rows_of(REACH * tiles), :] = weight_ref[rows_of(weight_ref.shape[0] // SUB - 1), :]


def merge_kernel(own_ref, other_ref, mass_ref, coef_ref, merged_ref, payload_ref):
    members, tiles = mass_ref.shape[0], merged_ref.shape[2] // 128
    both = lambda n: own_ref[rows_of(n), :] + other_ref[rows_of(n), :]
    scale = 1.0 / both(REACH * tiles)
    level = jnp.zeros((SUB, 128), jnp.float32)
    for c in range(REACH):
        for t in range(tiles):
            span = slice(t * 128, (t + 1) * 128)
            merged = jnp.exp(both(c * tiles + t) * scale)
            merged_ref[c, :, span] = merged
            level = level + merged * coef_ref[AREA, :, span]
    level = level + pltpu.roll(level, SUB // 2, 0)
    spare = jnp.zeros((128 - members - SUB, 128), jnp.float32)
    table = jnp.concatenate([mass_ref[...], level, spare], axis=0)
    row = jnp.sum(table.T, axis=0, keepdims=True)
    payload_ref[...] = jnp.broadcast_to(row[None], payload_ref.shape)


def finish_kernel(cells, got_ref, merged_ref, inner_ref, *refs):
    *outer_refs, bary_ref, updated_ref, field_ref, staged_ref, field_sem, sem = refs
    members, lat = inner_ref.shape[1:]
    groups = members // SUB
    odd = odd_core()
    total = jnp.sum(got_ref[...], axis=0)
    table = jnp.broadcast_to(total, (128, 128)).T
    level = table[members : members + SUB, :]
    low = low_half((SUB, lat))
    wide = lambda v: jnp.concatenate([v] * (lat // 128), axis=1)
    inverse = wide(cells / level)
    outer, inner = [], []
    for c in range(REACH):
        both = merged_ref[c] * inverse
        swapped = pltpu.roll(both, SUB // 2, 0)
        outer.append(jnp.where(low, both, swapped))
        inner.append(jnp.where(low, swapped, both))
    bary = from_outside(outer + inner, odd)
    field_ref[...] = jnp.swapaxes(jnp.stack(bary), 0, 1)[: SUB // 2]
    copies = [pltpu.make_async_copy(field_ref, bary_ref, field_sem)]
    copies[0].start()
    for group in range(groups):
        rows = slice(group * SUB, (group + 1) * SUB)
        factor = wide(table[rows, :] / cells)
        quotients = Chunked(outer_refs).stack(group) + stack_of(inner_ref, group)
        out = [b * factor * quotient for b, quotient in zip(bary, from_outside(quotients, odd))]
        span = block_of(group)
        staged_ref[span, :] = jnp.swapaxes(jnp.stack(out), 0, 1).reshape(SUB * SUB, lat)
        copies.append(pltpu.make_async_copy(staged_ref.at[span, :], updated_ref.at[span, :], sem.at[group]))
        copies[-1].start()
    for copy in copies:
        copy.wait()


def shape(*dims):
    return jax.ShapeDtypeStruct(dims, jnp.float32)


def call(kernel, outs, *args, scratch=(), out_specs=None):
    return pl.pallas_call(
        kernel,
        out_shape=outs,
        in_specs=[SMEM if arg.ndim == 1 else VMEM for arg in args],
        out_specs=out_specs or (VMEM,) * len(outs),
        scratch_shapes=scratch,
        compiler_params=params(),
    )(*args)


def body(fields, scaling, counts, land_mask):
    members, levels, lon, lat = fields.shape
    tiles = lax.axis_size("tile")
    rows = members * levels
    cells = lon * tiles * lat
    half = shape(REACH, rows, lat)
    edge = shape(2 * REACH - 2, rows, lat)
    packed = shape(REACH, SUB, lat)
    chunks = chunk_groups(rows // SUB)
    bases = [sum(map(sum, chunks[:n])) for n in range(len(chunks))]
    parts = [shape(REACH, sum(own) * SUB, lat) for own in chunks]
    coef = jnp.asarray(coefficients(lat))
    with_mate = [(i, i ^ 1) for i in range(tiles)]
    with_neighbour = [(i, (i + (1 if i % 2 else -1)) % tiles) for i in range(tiles)]
    scaling = scaling.reshape(rows * lon, lat)
    fields = fields.reshape(rows * lon, lat)

    inner, *outer = call(spread_kernel, (half, *parts), scaling)
    outer_halo = [lax.ppermute(part, "tile", with_neighbour) for part in outer]
    inner_halo = lax.ppermute(inner, "tile", with_mate)
    fields, inner = lax.optimization_barrier((fields, inner))
    v_inner, edges, filled, mass, weights = call(
        smooth_inner_kernel,
        (half, edge, half, shape(rows, 128), shape(rows + SUB, 128)),
        inner_halo,
        inner,
        fields,
        land_mask,
        counts,
        coef,
        *outer,
    )
    v_inner_halo = lax.ppermute(v_inner, "tile", with_mate)
    v_outer, v_outer_halo, places = [], [], []
    for base, sizes, halo, own in zip(bases, chunks, outer_halo, outer):
        outs = tuple(shape(REACH, size * SUB, lat) for size in sizes)
        values = call(partial(smooth_outer_kernel, base), outs, halo, own, edges, filled, coef)
        v_outer += values
        v_outer_halo += [lax.ppermute(value, "tile", with_neighbour) for value in values]
        places += [(base, base + sum(sizes[:n]), own) for n in range(len(sizes))]
    inverse_inner, edges, inner_logs = call(
        return_inner_kernel, (half, edge, packed), v_inner_halo, v_inner, inner, weights, coef, *v_outer
    )
    inverses, earlier = [inverse_inner], []
    for n, (base, first, own) in enumerate(places):
        if earlier:
            v_outer_halo[n], earlier[-1] = lax.optimization_barrier((v_outer_halo[n], earlier[-1]))
        operands = v_outer_halo[n], v_outer[n], edges, own, weights, coef
        part = shape(*v_outer[n].shape)
        if n < len(places) - 1:
            inverse, logs = call(partial(return_outer_kernel, base, first), (part, packed), *operands)
            earlier.append(logs)
        else:
            inverse, logs = call(
                partial(last_return_kernel, base, first),
                (part, shape((REACH * lat // 128 + 1) * SUB, 128)),
                *operands,
                inner_logs,
                *earlier,
                scratch=[pltpu.VMEM((REACH, SUB, lat), jnp.float32)],
            )
        inverses.append(inverse)
    other = lax.ppermute(logs, "mem", [(0, 1), (1, 0)])
    merged, payload = call(merge_kernel, (packed, shape(tiles, 1, 128)), logs, other, mass, coef)
    got = lax.all_to_all(payload, "tile", split_axis=0, concat_axis=0)
    barycenter, updated = call(
        partial(finish_kernel, float(cells)),
        (shape(levels, lon, lat), shape(rows * lon, lat)),
        got,
        merged,
        *inverses,
        scratch=[
            pltpu.VMEM((levels, lon, lat), jnp.float32),
            pltpu.VMEM((rows * lon, lat), jnp.float32),
            pltpu.SemaphoreType.DMA,
            pltpu.SemaphoreType.DMA((rows // SUB,)),
        ],
        out_specs=(HBM, HBM),
    )
    return barycenter, updated.reshape(members, levels, lon, lat)


def solution(mesh):
    return jax.shard_map(
        body,
        mesh=mesh,
        in_specs=(
            P("mem", None, "tile", None),
            P("mem", None, "tile", None),
            P("mem"),
            P("tile", None),
        ),
        out_specs=(P(None, "tile", None), P("mem", None, "tile", None)),
        check_vma=False,
    )
```

```python
import math
from functools import partial

import jax
import jax.numpy as jnp
import numpy as np
from jax import lax
from jax.experimental import pallas as pl
from jax.experimental.pallas import tpu as pltpu
from jax.sharding import PartitionSpec as P

BACKGROUND = 0.01
REACH = 4
SUB = 8
VMEM = pl.BlockSpec(memory_space=pltpu.VMEM)
SMEM = pl.BlockSpec(memory_space=pltpu.SMEM)
HBM = pl.BlockSpec(memory_space=pl.ANY)
AREA, ZONAL, NORTH, SOUTH, CENTER = range(5)


def coefficients(lat_cells):
    spacing = math.pi / lat_cells
    index = np.arange(lat_cells)
    latitude = -0.5 * math.pi + (index + 0.5) * spacing
    cell_area = np.cos(latitude)
    zonal = 0.2 * np.minimum(2.2, 1.0 / cell_area**2)
    north = np.where(index == lat_cells - 1, 0.0, 0.05 * np.cos(latitude + 0.5 * spacing) / cell_area)
    south = np.where(index == 0, 0.0, 0.05 * np.cos(latitude - 0.5 * spacing) / cell_area)
    center = 1.0 - 2.0 * zonal - north - south
    rows = np.stack([cell_area, zonal, north, south, center]).astype(np.float32)
    return np.ascontiguousarray(np.broadcast_to(rows[:, None, :], (5, SUB, lat_cells)))


def params(mib):
    return pltpu.CompilerParams(vmem_limit_bytes=mib * 2**20)


def rows_of(group):
    return pl.ds(group * SUB, SUB)


def block_of(group):
    return pl.ds(group * SUB * SUB, SUB * SUB)


def batches(last, first=0, size=4):
    return [range(start, min(start + size, last)) for start in range(first, last, size)]


def chunk_groups(groups):
    half = (groups + 1) // 2
    last = max(1, (groups - half) // 3)
    return [[half], [groups - half - last, last]]


class Chunked:
    def __init__(self, refs):
        self.refs = refs

    def stack(self, group, order=range(REACH)):
        for ref in self.refs:
            held = ref.shape[1] // SUB
            if group < held:
                return stack_of(ref, group, order)
            group -= held

    def put(self, group, values):
        for ref in self.refs:
            held = ref.shape[1] // SUB
            if 0 <= group < held:
                for c, value in enumerate(values):
                    ref[c, rows_of(group), :] = value
            group -= held


def by_longitude(block, lat):
    return jnp.swapaxes(block.reshape(SUB, SUB, lat), 0, 1)


def stack_of(ref, group, order=range(REACH)):
    return [ref[c, rows_of(group), :] for c in order]


def odd_core():
    return lax.rem(lax.axis_index("tile"), 2) == 1


def from_outside(columns, odd):
    last = len(columns) - 1
    return [jnp.where(odd, columns[last - c], columns[c]) for c in range(len(columns))]


def low_half(shape):
    return lax.broadcasted_iota(jnp.int32, shape, 0) < SUB // 2


def spread_kernel(scaling_ref, inner_ref, *refs):
    *outer_refs, staged_ref, sem = refs
    groups, lat = inner_ref.shape[1] // SUB, inner_ref.shape[2]
    odd = odd_core()
    outer = Chunked(outer_refs)
    copies = [
        pltpu.make_async_copy(scaling_ref.at[block_of(g), :], staged_ref.at[block_of(g), :], sem.at[g])
        for g in range(groups)
    ]
    for copy in copies:
        copy.start()
    for group in range(groups):
        copies[group].wait()
        columns = from_outside(by_longitude(staged_ref[block_of(group), :], lat), odd)
        outer.put(group, columns[:REACH])
        for c in range(REACH):
            inner_ref[c, rows_of(group), :] = columns[c + REACH]


def lane_fold(value):
    lat = value.shape[-1]
    total = value[:, :128]
    for t in range(1, lat // 128):
        total = total + value[:, t * 128 : (t + 1) * 128]
    return total


def diffuse(columns, coef_ref):
    lat = columns[0].shape[-1]
    return [
        coef_ref[CENTER] * here
        + coef_ref[ZONAL] * (west + east)
        + coef_ref[NORTH] * pltpu.roll(here, lat - 1, 1)
        + coef_ref[SOUTH] * pltpu.roll(here, 1, 1)
        for west, here, east in zip(columns[:-2], columns[1:-1], columns[2:])
    ]


def unit(values, coef_ref):
    return values


def by_area(values, coef_ref):
    return [value * coef_ref[AREA] for value in values]


def inner_half(batch, halo_ref, inner_ref, outer_refs, coef_ref, edge_ref, weigh=unit):
    outer = Chunked(outer_refs)
    columns = [outer.stack(g) + stack_of(inner_ref, g) + stack_of(halo_ref, g, (3, 2, 1, 0)) for g in batch]
    columns = [weigh(own, coef_ref) for own in columns]
    for s in range(REACH):
        columns = [diffuse(own, coef_ref) for own in columns]
        if s < REACH - 1:
            for own, group in zip(columns, batch):
                edge_ref[2 * s, rows_of(group), :] = own[0]
                edge_ref[2 * s + 1, rows_of(group), :] = own[1]
    return zip(batch, columns)


def outer_half(batch, first, halo_ref, outer_ref, edge_ref, coef_ref, weigh=unit):
    columns = [stack_of(halo_ref, g - first, (3, 2, 1, 0)) + stack_of(outer_ref, g - first, (0, 1)) for g in batch]
    columns = [weigh(own, coef_ref) for own in columns]
    for s in range(REACH):
        columns = [diffuse(own, coef_ref) for own in columns]
        if s < REACH - 1:
            columns = [own + stack_of(edge_ref, g, (2 * s, 2 * s + 1)) for own, g in zip(columns, batch)]
    return zip(batch, columns)


def smooth_inner_kernel(
    halo_ref, inner_ref, fields_ref, mask_ref, count_ref, coef_ref, *refs
):
    *outer_refs, out_ref, edge_ref, filled_ref, mass_ref, weight_ref = refs
    groups, lat = inner_ref.shape[1] // SUB, inner_ref.shape[2]
    odd = odd_core()
    low = low_half((SUB, 128))
    for group in range(groups):
        first, second = (count_ref[2 * group + n].astype(jnp.float32) for n in range(2))
        weight_ref[rows_of(group), :] = jnp.where(low, first, second)
    count = sum(count_ref[m] for m in range(2 * groups)).astype(jnp.float32)
    weight_ref[rows_of(groups), :] = jnp.full((SUB, 128), count)
    for batch in batches(groups):
        for group, smoothed in inner_half(
            batch, halo_ref, inner_ref, outer_refs, coef_ref, edge_ref, by_area
        ):
            fields = by_longitude(fields_ref[block_of(group), :], lat)
            filled = []
            for c in range(2 * REACH):
                valid = jnp.broadcast_to(mask_ref[c : c + 1, :], (SUB, lat)) == 1
                filled.append((jnp.where(valid, fields[c], 0.0) + BACKGROUND) * coef_ref[AREA])
            mass_ref[rows_of(group), :] = lane_fold(sum(filled))
            filled = from_outside(filled, odd)
            for c in range(REACH):
                filled_ref[c, rows_of(group), :] = filled[c]
                out_ref[c, rows_of(group), :] = filled[c + REACH] / smoothed[c]


def smooth_outer_kernel(first, halo_ref, outer_ref, edge_ref, filled_ref, coef_ref, *out_refs):
    last = first + outer_ref.shape[1] // SUB
    out = Chunked(out_refs)
    for batch in batches(last, first):
        for group, smoothed in outer_half(batch, first, halo_ref, outer_ref, edge_ref, coef_ref, by_area):
            filled = stack_of(filled_ref, group)
            out.put(group - first, [top / bottom for top, bottom in zip(filled, smoothed)])


def add_logs(group, held, result, scaled, weight_ref, inverse_ref, total_ref):
    lat = total_ref.shape[2]
    weight = jnp.concatenate([weight_ref[rows_of(group), :]] * (lat // 128), axis=1)
    for c in range(REACH):
        inverse_ref[c, rows_of(held), :] = 1.0 / result[c]
        total_ref[c] = total_ref[c] + weight * jnp.log(scaled[c] * result[c])


def return_inner_kernel(halo_ref, inner_ref, scaled_ref, weight_ref, coef_ref, *refs):
    *outer_refs, inverse_ref, edge_ref, total_ref = refs
    groups = inner_ref.shape[1] // SUB
    total_ref[...] = jnp.zeros_like(total_ref)
    for batch in batches(groups):
        for group, result in inner_half(batch, halo_ref, inner_ref, outer_refs, coef_ref, edge_ref):
            add_logs(group, group, result, stack_of(scaled_ref, group), weight_ref, inverse_ref, total_ref)


def return_outer_kernel(
    base, first, halo_ref, outer_ref, edge_ref, scaled_ref, weight_ref, coef_ref, inverse_ref, total_ref
):
    last = first + outer_ref.shape[1] // SUB
    total_ref[...] = jnp.zeros_like(total_ref)
    for batch in batches(last, first):
        for group, result in outer_half(batch, first, halo_ref, outer_ref, edge_ref, coef_ref):
            scaled = stack_of(scaled_ref, group - base)
            add_logs(group, group - first, result, scaled, weight_ref, inverse_ref, total_ref)


def last_return_kernel(
    base,
    first,
    halo_ref,
    outer_ref,
    edge_ref,
    scaled_ref,
    weight_ref,
    coef_ref,
    inner_ref,
    *refs,
):
    *earlier_refs, inverse_ref, logs_ref, total_ref = refs
    return_outer_kernel(
        base, first, halo_ref, outer_ref, edge_ref, scaled_ref, weight_ref, coef_ref, inverse_ref, total_ref
    )
    low = low_half(total_ref.shape[1:])
    tiles = total_ref.shape[2] // 128
    for c in range(REACH):
        outer, inner = sum((ref[c] for ref in earlier_refs), total_ref[c]), inner_ref[c]
        outer = outer + pltpu.roll(outer, SUB // 2, 0)
        inner = inner + pltpu.roll(inner, SUB // 2, 0)
        both = jnp.where(low, outer, inner)
        for t in range(tiles):
            logs_ref[rows_of(c * tiles + t), :] = both[:, t * 128 : (t + 1) * 128]
    logs_ref[rows_of(REACH * tiles), :] = weight_ref[rows_of(weight_ref.shape[0] // SUB - 1), :]


def merge_kernel(own_ref, other_ref, mass_ref, coef_ref, merged_ref, payload_ref):
    members, tiles = mass_ref.shape[0], merged_ref.shape[2] // 128
    both = lambda n: own_ref[rows_of(n), :] + other_ref[rows_of(n), :]
    scale = 1.0 / both(REACH * tiles)
    level = jnp.zeros((SUB, 128), jnp.float32)
    for c in range(REACH):
        for t in range(tiles):
            span = slice(t * 128, (t + 1) * 128)
            merged = jnp.exp(both(c * tiles + t) * scale)
            merged_ref[c, :, span] = merged
            level = level + merged * coef_ref[AREA, :, span]
    level = level + pltpu.roll(level, SUB // 2, 0)
    spare = jnp.zeros((128 - members - SUB, 128), jnp.float32)
    table = jnp.concatenate([mass_ref[...], level, spare], axis=0)
    row = jnp.sum(table.T, axis=0, keepdims=True)
    payload_ref[...] = jnp.broadcast_to(row[None], payload_ref.shape)


def finish_kernel(cells, got_ref, merged_ref, inner_ref, *refs):
    *outer_refs, bary_ref, updated_ref, field_ref, staged_ref, field_sem, sem = refs
    members, lat = inner_ref.shape[1:]
    groups = members // SUB
    odd = odd_core()
    total = jnp.sum(got_ref[...], axis=0)
    table = jnp.broadcast_to(total, (128, 128)).T
    level = table[members : members + SUB, :]
    low = low_half((SUB, lat))
    wide = lambda v: jnp.concatenate([v] * (lat // 128), axis=1)
    inverse = wide(cells / level)
    outer, inner = [], []
    for c in range(REACH):
        both = merged_ref[c] * inverse
        swapped = pltpu.roll(both, SUB // 2, 0)
        outer.append(jnp.where(low, both, swapped))
        inner.append(jnp.where(low, swapped, both))
    bary = from_outside(outer + inner, odd)
    field_ref[...] = jnp.swapaxes(jnp.stack(bary), 0, 1)[: SUB // 2]
    copies = [pltpu.make_async_copy(field_ref, bary_ref, field_sem)]
    copies[0].start()
    for group in range(groups):
        rows = slice(group * SUB, (group + 1) * SUB)
        factor = wide(table[rows, :] / cells)
        quotients = Chunked(outer_refs).stack(group) + stack_of(inner_ref, group)
        out = [b * factor * quotient for b, quotient in zip(bary, from_outside(quotients, odd))]
        span = block_of(group)
        staged_ref[span, :] = jnp.swapaxes(jnp.stack(out), 0, 1).reshape(SUB * SUB, lat)
        copies.append(pltpu.make_async_copy(staged_ref.at[span, :], updated_ref.at[span, :], sem.at[group]))
        copies[-1].start()
    for copy in copies:
        copy.wait()


def shape(*dims):
    return jax.ShapeDtypeStruct(dims, jnp.float32)


def call(kernel, outs, *args, scratch=(), in_specs=None, out_specs=None, mib=12):
    return pl.pallas_call(
        kernel,
        out_shape=outs,
        in_specs=in_specs or [SMEM if arg.ndim == 1 else VMEM for arg in args],
        out_specs=out_specs or (VMEM,) * len(outs),
        scratch_shapes=scratch,
        compiler_params=params(mib),
    )(*args)


def body(fields, scaling, counts, land_mask):
    members, levels, lon, lat = fields.shape
    tiles = lax.axis_size("tile")
    rows = members * levels
    cells = lon * tiles * lat
    half = shape(REACH, rows, lat)
    edge = shape(2 * REACH - 2, rows, lat)
    packed = shape(REACH, SUB, lat)
    chunks = chunk_groups(rows // SUB)
    bases = [sum(map(sum, chunks[:n])) for n in range(len(chunks))]
    parts = [shape(REACH, sum(own) * SUB, lat) for own in chunks]
    coef = jnp.asarray(coefficients(lat))
    with_mate = [(i, i ^ 1) for i in range(tiles)]
    with_neighbour = [(i, (i + (1 if i % 2 else -1)) % tiles) for i in range(tiles)]
    scaling = scaling.reshape(rows * lon, lat)
    fields = fields.reshape(rows * lon, lat)

    inner, *outer = call(
        spread_kernel,
        (half, *parts),
        scaling,
        in_specs=[HBM],
        scratch=[pltpu.VMEM((rows * lon, lat), jnp.float32), pltpu.SemaphoreType.DMA((rows // SUB,))],
        mib=51,
    )
    outer_halo = [lax.ppermute(part, "tile", with_neighbour) for part in outer]
    inner_halo = lax.ppermute(inner, "tile", with_mate)
    fields, inner = lax.optimization_barrier((fields, inner))
    v_inner, edges, filled, mass, weights = call(
        smooth_inner_kernel,
        (half, edge, half, shape(rows, 128), shape(rows + SUB, 128)),
        inner_halo,
        inner,
        fields,
        land_mask,
        counts,
        coef,
        *outer,
    )
    v_inner_halo = lax.ppermute(v_inner, "tile", with_mate)
    v_outer, v_outer_halo, places = [], [], []
    for base, sizes, halo, own in zip(bases, chunks, outer_halo, outer):
        outs = tuple(shape(REACH, size * SUB, lat) for size in sizes)
        values = call(partial(smooth_outer_kernel, base), outs, halo, own, edges, filled, coef)
        v_outer += values
        v_outer_halo += [lax.ppermute(value, "tile", with_neighbour) for value in values]
        places += [(base, base + sum(sizes[:n]), own) for n in range(len(sizes))]
    inverse_inner, edges, inner_logs = call(
        return_inner_kernel, (half, edge, packed), v_inner_halo, v_inner, inner, weights, coef, *v_outer
    )
    inverses, earlier = [inverse_inner], []
    for n, (base, first, own) in enumerate(places):
        if earlier:
            v_outer_halo[n], earlier[-1] = lax.optimization_barrier((v_outer_halo[n], earlier[-1]))
        operands = v_outer_halo[n], v_outer[n], edges, own, weights, coef
        part = shape(*v_outer[n].shape)
        if n < len(places) - 1:
            inverse, logs = call(partial(return_outer_kernel, base, first), (part, packed), *operands)
            earlier.append(logs)
        else:
            inverse, logs = call(
                partial(last_return_kernel, base, first),
                (part, shape((REACH * lat // 128 + 1) * SUB, 128)),
                *operands,
                inner_logs,
                *earlier,
                scratch=[pltpu.VMEM((REACH, SUB, lat), jnp.float32)],
            )
        inverses.append(inverse)
    other = lax.ppermute(logs, "mem", [(0, 1), (1, 0)])
    merged, payload = call(merge_kernel, (packed, shape(tiles, 1, 128)), logs, other, mass, coef)
    got = lax.all_to_all(payload, "tile", split_axis=0, concat_axis=0)
    barycenter, updated = call(
        partial(finish_kernel, float(cells)),
        (shape(levels, lon, lat), shape(rows * lon, lat)),
        got,
        merged,
        *inverses,
        scratch=[
            pltpu.VMEM((levels, lon, lat), jnp.float32),
            pltpu.VMEM((rows * lon, lat), jnp.float32),
            pltpu.SemaphoreType.DMA,
            pltpu.SemaphoreType.DMA((rows // SUB,)),
        ],
        out_specs=(HBM, HBM),
    )
    return barycenter, updated.reshape(members, levels, lon, lat)


def solution(mesh):
    return jax.shard_map(
        body,
        mesh=mesh,
        in_specs=(
            P("mem", None, "tile", None),
            P("mem", None, "tile", None),
            P("mem"),
            P("tile", None),
        ),
        out_specs=(P(None, "tile", None), P("mem", None, "tile", None)),
        check_vma=False,
    )
```

```python
import math
from functools import partial

import jax
import jax.numpy as jnp
import numpy as np
from jax import lax
from jax.experimental import pallas as pl
from jax.experimental.pallas import tpu as pltpu
from jax.sharding import PartitionSpec as P

BACKGROUND = 0.01
REACH = 4
SUB = 8
VMEM = pl.BlockSpec(memory_space=pltpu.VMEM)
SMEM = pl.BlockSpec(memory_space=pltpu.SMEM)
HBM = pl.BlockSpec(memory_space=pl.ANY)
AREA, ZONAL, NORTH, SOUTH, CENTER = range(5)


def coefficients(lat_cells):
    spacing = math.pi / lat_cells
    index = np.arange(lat_cells)
    latitude = -0.5 * math.pi + (index + 0.5) * spacing
    cell_area = np.cos(latitude)
    zonal = 0.2 * np.minimum(2.2, 1.0 / cell_area**2)
    north = np.where(index == lat_cells - 1, 0.0, 0.05 * np.cos(latitude + 0.5 * spacing) / cell_area)
    south = np.where(index == 0, 0.0, 0.05 * np.cos(latitude - 0.5 * spacing) / cell_area)
    center = 1.0 - 2.0 * zonal - north - south
    rows = np.stack([cell_area, zonal, north, south, center]).astype(np.float32)
    return np.ascontiguousarray(np.broadcast_to(rows[:, None, :], (5, SUB, lat_cells)))


def params(mib=12):
    return pltpu.CompilerParams(vmem_limit_bytes=mib * 2**20)


def rows_of(group):
    return pl.ds(group * SUB, SUB)


def block_of(group):
    return pl.ds(group * SUB * SUB, SUB * SUB)


def batches(last, first=0, size=4):
    return [range(start, min(start + size, last)) for start in range(first, last, size)]


def chunk_groups(groups):
    first = (groups * 3 + 2) // 5
    return [[first], [groups - first - 1, 1]]


class Chunked:
    def __init__(self, refs):
        self.refs = refs

    def stack(self, group, order=range(REACH)):
        for ref in self.refs:
            held = ref.shape[1] // SUB
            if group < held:
                return stack_of(ref, group, order)
            group -= held

    def put(self, group, values):
        for ref in self.refs:
            held = ref.shape[1] // SUB
            if 0 <= group < held:
                for c, value in enumerate(values):
                    ref[c, rows_of(group), :] = value
            group -= held


def by_longitude(block, lat):
    return jnp.swapaxes(block.reshape(SUB, SUB, lat), 0, 1)


def stack_of(ref, group, order=range(REACH)):
    return [ref[c, rows_of(group), :] for c in order]


def odd_core():
    return lax.rem(lax.axis_index("tile"), 2) == 1


def from_outside(columns, odd):
    last = len(columns) - 1
    return [jnp.where(odd, columns[last - c], columns[c]) for c in range(len(columns))]


def low_half(shape):
    return lax.broadcasted_iota(jnp.int32, shape, 0) < SUB // 2


def spread_kernel(scaling_ref, inner_ref, *outer_refs):
    groups, lat = inner_ref.shape[1] // SUB, inner_ref.shape[2]
    odd = odd_core()
    outer = Chunked(outer_refs)
    for group in range(groups):
        columns = from_outside(by_longitude(scaling_ref[block_of(group), :], lat), odd)
        outer.put(group, columns[:REACH])
        for c in range(REACH):
            inner_ref[c, rows_of(group), :] = columns[c + REACH]


def lane_fold(value):
    lat = value.shape[-1]
    total = value[:, :128]
    for t in range(1, lat // 128):
        total = total + value[:, t * 128 : (t + 1) * 128]
    return total


def diffuse(columns, coef_ref):
    lat = columns[0].shape[-1]
    return [
        coef_ref[CENTER] * here
        + coef_ref[ZONAL] * (west + east)
        + coef_ref[NORTH] * pltpu.roll(here, lat - 1, 1)
        + coef_ref[SOUTH] * pltpu.roll(here, 1, 1)
        for west, here, east in zip(columns[:-2], columns[1:-1], columns[2:])
    ]


def unit(values, coef_ref):
    return values


def by_area(values, coef_ref):
    return [value * coef_ref[AREA] for value in values]


def inner_half(batch, halo_ref, inner_ref, outer_refs, coef_ref, edge_ref, weigh=unit):
    outer = Chunked(outer_refs)
    columns = [outer.stack(g) + stack_of(inner_ref, g) + stack_of(halo_ref, g, (3, 2, 1, 0)) for g in batch]
    columns = [weigh(own, coef_ref) for own in columns]
    for s in range(REACH):
        columns = [diffuse(own, coef_ref) for own in columns]
        if s < REACH - 1:
            for own, group in zip(columns, batch):
                edge_ref[2 * s, rows_of(group), :] = own[0]
                edge_ref[2 * s + 1, rows_of(group), :] = own[1]
    return zip(batch, columns)


def outer_half(batch, first, halo_ref, outer_ref, edge_ref, coef_ref, weigh=unit):
    columns = [stack_of(halo_ref, g - first, (3, 2, 1, 0)) + stack_of(outer_ref, g - first, (0, 1)) for g in batch]
    columns = [weigh(own, coef_ref) for own in columns]
    for s in range(REACH):
        columns = [diffuse(own, coef_ref) for own in columns]
        if s < REACH - 1:
            columns = [own + stack_of(edge_ref, g, (2 * s, 2 * s + 1)) for own, g in zip(columns, batch)]
    return zip(batch, columns)


def smooth_inner_kernel(
    halo_ref, inner_ref, fields_ref, mask_ref, count_ref, coef_ref, *refs
):
    *outer_refs, out_ref, edge_ref, filled_ref, mass_ref, weight_ref = refs
    groups, lat = inner_ref.shape[1] // SUB, inner_ref.shape[2]
    odd = odd_core()
    low = low_half((SUB, 128))
    for group in range(groups):
        first, second = (count_ref[2 * group + n].astype(jnp.float32) for n in range(2))
        weight_ref[rows_of(group), :] = jnp.where(low, first, second)
    count = sum(count_ref[m] for m in range(2 * groups)).astype(jnp.float32)
    weight_ref[rows_of(groups), :] = jnp.full((SUB, 128), count)
    for batch in batches(groups):
        for group, smoothed in inner_half(
            batch, halo_ref, inner_ref, outer_refs, coef_ref, edge_ref, by_area
        ):
            fields = by_longitude(fields_ref[block_of(group), :], lat)
            filled = []
            for c in range(2 * REACH):
                valid = jnp.broadcast_to(mask_ref[c : c + 1, :], (SUB, lat)) == 1
                filled.append((jnp.where(valid, fields[c], 0.0) + BACKGROUND) * coef_ref[AREA])
            mass_ref[rows_of(group), :] = lane_fold(sum(filled))
            filled = from_outside(filled, odd)
            for c in range(REACH):
                filled_ref[c, rows_of(group), :] = filled[c]
                out_ref[c, rows_of(group), :] = filled[c + REACH] / smoothed[c]


def smooth_outer_kernel(first, halo_ref, outer_ref, edge_ref, filled_ref, coef_ref, *out_refs):
    last = first + outer_ref.shape[1] // SUB
    out = Chunked(out_refs)
    for batch in batches(last, first):
        for group, smoothed in outer_half(batch, first, halo_ref, outer_ref, edge_ref, coef_ref, by_area):
            filled = stack_of(filled_ref, group)
            out.put(group - first, [top / bottom for top, bottom in zip(filled, smoothed)])


def add_logs(group, held, result, scaled, weight_ref, inverse_ref, total_ref):
    lat = total_ref.shape[2]
    weight = jnp.concatenate([weight_ref[rows_of(group), :]] * (lat // 128), axis=1)
    for c in range(REACH):
        inverse_ref[c, rows_of(held), :] = 1.0 / result[c]
        total_ref[c] = total_ref[c] + weight * jnp.log(scaled[c] * result[c])


def return_inner_kernel(halo_ref, inner_ref, scaled_ref, weight_ref, coef_ref, *refs):
    *outer_refs, inverse_ref, edge_ref, total_ref = refs
    groups = inner_ref.shape[1] // SUB
    total_ref[...] = jnp.zeros_like(total_ref)
    for batch in batches(groups):
        for group, result in inner_half(batch, halo_ref, inner_ref, outer_refs, coef_ref, edge_ref):
            add_logs(group, group, result, stack_of(scaled_ref, group), weight_ref, inverse_ref, total_ref)


def return_outer_kernel(
    base, first, halo_ref, outer_ref, edge_ref, scaled_ref, weight_ref, coef_ref, inverse_ref, total_ref
):
    last = first + outer_ref.shape[1] // SUB
    total_ref[...] = jnp.zeros_like(total_ref)
    for batch in batches(last, first):
        for group, result in outer_half(batch, first, halo_ref, outer_ref, edge_ref, coef_ref):
            scaled = stack_of(scaled_ref, group - base)
            add_logs(group, group - first, result, scaled, weight_ref, inverse_ref, total_ref)


def last_return_kernel(
    base,
    first,
    halo_ref,
    outer_ref,
    edge_ref,
    scaled_ref,
    weight_ref,
    coef_ref,
    inner_ref,
    *refs,
):
    *earlier_refs, inverse_ref, logs_ref, total_ref = refs
    return_outer_kernel(
        base, first, halo_ref, outer_ref, edge_ref, scaled_ref, weight_ref, coef_ref, inverse_ref, total_ref
    )
    low = low_half(total_ref.shape[1:])
    tiles = total_ref.shape[2] // 128
    for c in range(REACH):
        outer, inner = sum((ref[c] for ref in earlier_refs), total_ref[c]), inner_ref[c]
        outer = outer + pltpu.roll(outer, SUB // 2, 0)
        inner = inner + pltpu.roll(inner, SUB // 2, 0)
        both = jnp.where(low, outer, inner)
        for t in range(tiles):
            logs_ref[rows_of(c * tiles + t), :] = both[:, t * 128 : (t + 1) * 128]
    logs_ref[rows_of(REACH * tiles), :] = weight_ref[rows_of(weight_ref.shape[0] // SUB - 1), :]


def merge_kernel(own_ref, other_ref, mass_ref, coef_ref, merged_ref, payload_ref):
    members, tiles = mass_ref.shape[0], merged_ref.shape[2] // 128
    both = lambda n: own_ref[rows_of(n), :] + other_ref[rows_of(n), :]
    scale = 1.0 / both(REACH * tiles)
    level = jnp.zeros((SUB, 128), jnp.float32)
    for c in range(REACH):
        for t in range(tiles):
            span = slice(t * 128, (t + 1) * 128)
            merged = jnp.exp(both(c * tiles + t) * scale)
            merged_ref[c, :, span] = merged
            level = level + merged * coef_ref[AREA, :, span]
    level = level + pltpu.roll(level, SUB // 2, 0)
    spare = jnp.zeros((128 - members - SUB, 128), jnp.float32)
    table = jnp.concatenate([mass_ref[...], level, spare], axis=0)
    row = jnp.sum(table.T, axis=0, keepdims=True)
    payload_ref[...] = jnp.broadcast_to(row[None], payload_ref.shape)


def finish_kernel(cells, got_ref, merged_ref, inner_ref, *refs):
    *outer_refs, bary_ref, updated_ref, field_ref, staged_ref, field_sem, sem = refs
    members, lat = inner_ref.shape[1:]
    groups = members // SUB
    odd = odd_core()
    total = jnp.sum(got_ref[...], axis=0)
    table = jnp.broadcast_to(total, (128, 128)).T
    level = table[members : members + SUB, :]
    low = low_half((SUB, lat))
    wide = lambda v: jnp.concatenate([v] * (lat // 128), axis=1)
    inverse = wide(cells / level)
    outer, inner = [], []
    for c in range(REACH):
        both = merged_ref[c] * inverse
        swapped = pltpu.roll(both, SUB // 2, 0)
        outer.append(jnp.where(low, both, swapped))
        inner.append(jnp.where(low, swapped, both))
    bary = from_outside(outer + inner, odd)
    field_ref[...] = jnp.swapaxes(jnp.stack(bary), 0, 1)[: SUB // 2]
    copies = [pltpu.make_async_copy(field_ref, bary_ref, field_sem)]
    copies[0].start()
    for group in range(groups):
        rows = slice(group * SUB, (group + 1) * SUB)
        factor = wide(table[rows, :] / cells)
        quotients = Chunked(outer_refs).stack(group) + stack_of(inner_ref, group)
        out = [b * factor * quotient for b, quotient in zip(bary, from_outside(quotients, odd))]
        span = block_of(group)
        staged_ref[span, :] = jnp.swapaxes(jnp.stack(out), 0, 1).reshape(SUB * SUB, lat)
        copies.append(pltpu.make_async_copy(staged_ref.at[span, :], updated_ref.at[span, :], sem.at[group]))
        copies[-1].start()
    for copy in copies:
        copy.wait()


def shape(*dims):
    return jax.ShapeDtypeStruct(dims, jnp.float32)


def call(kernel, outs, *args, scratch=(), out_specs=None):
    return pl.pallas_call(
        kernel,
        out_shape=outs,
        in_specs=[SMEM if arg.ndim == 1 else VMEM for arg in args],
        out_specs=out_specs or (VMEM,) * len(outs),
        scratch_shapes=scratch,
        compiler_params=params(),
    )(*args)


def body(fields, scaling, counts, land_mask):
    members, levels, lon, lat = fields.shape
    tiles = lax.axis_size("tile")
    rows = members * levels
    cells = lon * tiles * lat
    half = shape(REACH, rows, lat)
    edge = shape(2 * REACH - 2, rows, lat)
    packed = shape(REACH, SUB, lat)
    chunks = chunk_groups(rows // SUB)
    bases = [sum(map(sum, chunks[:n])) for n in range(len(chunks))]
    parts = [shape(REACH, sum(own) * SUB, lat) for own in chunks]
    coef = jnp.asarray(coefficients(lat))
    with_mate = [(i, i ^ 1) for i in range(tiles)]
    with_neighbour = [(i, (i + (1 if i % 2 else -1)) % tiles) for i in range(tiles)]
    scaling = scaling.reshape(rows * lon, lat)
    fields = fields.reshape(rows * lon, lat)

    inner, *outer = call(spread_kernel, (half, *parts), scaling)
    outer_halo = [lax.ppermute(part, "tile", with_neighbour) for part in outer]
    inner_halo = lax.ppermute(inner, "tile", with_mate)
    fields, inner = lax.optimization_barrier((fields, inner))
    v_inner, edges, filled, mass, weights = call(
        smooth_inner_kernel,
        (half, edge, half, shape(rows, 128), shape(rows + SUB, 128)),
        inner_halo,
        inner,
        fields,
        land_mask,
        counts,
        coef,
        *outer,
    )
    v_inner_halo = lax.ppermute(v_inner, "tile", with_mate)
    v_outer, v_outer_halo, places = [], [], []
    for base, sizes, halo, own in zip(bases, chunks, outer_halo, outer):
        outs = tuple(shape(REACH, size * SUB, lat) for size in sizes)
        values = call(partial(smooth_outer_kernel, base), outs, halo, own, edges, filled, coef)
        v_outer += values
        v_outer_halo += [lax.ppermute(value, "tile", with_neighbour) for value in values]
        places += [(base, base + sum(sizes[:n]), own) for n in range(len(sizes))]
    inverse_inner, edges, inner_logs = call(
        return_inner_kernel, (half, edge, packed), v_inner_halo, v_inner, inner, weights, coef, *v_outer
    )
    inverses, earlier = [inverse_inner], []
    for n, (base, first, own) in enumerate(places):
        if earlier:
            v_outer_halo[n], earlier[-1] = lax.optimization_barrier((v_outer_halo[n], earlier[-1]))
        operands = v_outer_halo[n], v_outer[n], edges, own, weights, coef
        part = shape(*v_outer[n].shape)
        if n < len(places) - 1:
            inverse, logs = call(partial(return_outer_kernel, base, first), (part, packed), *operands)
            earlier.append(logs)
        else:
            inverse, logs = call(
                partial(last_return_kernel, base, first),
                (part, shape((REACH * lat // 128 + 1) * SUB, 128)),
                *operands,
                inner_logs,
                *earlier,
                scratch=[pltpu.VMEM((REACH, SUB, lat), jnp.float32)],
            )
        inverses.append(inverse)
    other = lax.ppermute(logs, "mem", [(0, 1), (1, 0)])
    merged, payload = call(merge_kernel, (packed, shape(tiles, 1, 128)), logs, other, mass, coef)
    got = lax.all_to_all(payload, "tile", split_axis=0, concat_axis=0)
    barycenter, updated = call(
        partial(finish_kernel, float(cells)),
        (shape(levels, lon, lat), shape(rows * lon, lat)),
        got,
        merged,
        *inverses,
        scratch=[
            pltpu.VMEM((levels, lon, lat), jnp.float32),
            pltpu.VMEM((rows * lon, lat), jnp.float32),
            pltpu.SemaphoreType.DMA,
            pltpu.SemaphoreType.DMA((rows // SUB,)),
        ],
        out_specs=(HBM, HBM),
    )
    return barycenter, updated.reshape(members, levels, lon, lat)


def solution(mesh):
    return jax.shard_map(
        body,
        mesh=mesh,
        in_specs=(
            P("mem", None, "tile", None),
            P("mem", None, "tile", None),
            P("mem"),
            P("tile", None),
        ),
        out_specs=(P(None, "tile", None), P("mem", None, "tile", None)),
        check_vma=False,
    )
```

```python
import math
from functools import partial

import jax
import jax.numpy as jnp
import numpy as np
from jax import lax
from jax.experimental import pallas as pl
from jax.experimental.pallas import tpu as pltpu
from jax.sharding import PartitionSpec as P

BACKGROUND = 0.01
REACH = 4
SUB = 8
VMEM = pl.BlockSpec(memory_space=pltpu.VMEM)
SMEM = pl.BlockSpec(memory_space=pltpu.SMEM)
HBM = pl.BlockSpec(memory_space=pl.ANY)
AREA, ZONAL, NORTH, SOUTH, CENTER = range(5)


def coefficients(lat_cells):
    spacing = math.pi / lat_cells
    index = np.arange(lat_cells)
    latitude = -0.5 * math.pi + (index + 0.5) * spacing
    cell_area = np.cos(latitude)
    zonal = 0.2 * np.minimum(2.2, 1.0 / cell_area**2)
    north = np.where(index == lat_cells - 1, 0.0, 0.05 * np.cos(latitude + 0.5 * spacing) / cell_area)
    south = np.where(index == 0, 0.0, 0.05 * np.cos(latitude - 0.5 * spacing) / cell_area)
    center = 1.0 - 2.0 * zonal - north - south
    rows = np.stack([cell_area, zonal, north, south, center]).astype(np.float32)
    return np.ascontiguousarray(np.broadcast_to(rows[:, None, :], (5, SUB, lat_cells)))


def params(mib=12):
    return pltpu.CompilerParams(vmem_limit_bytes=mib * 2**20)


def rows_of(group):
    return pl.ds(group * SUB, SUB)


def block_of(group):
    return pl.ds(group * SUB * SUB, SUB * SUB)


def batches(last, first=0, size=4):
    return [range(start, min(start + size, last)) for start in range(first, last, size)]


def chunk_groups(groups):
    first = (groups * 3 + 2) // 5
    return [[first], [groups - first - 1, 1]]


class Chunked:
    def __init__(self, refs):
        self.refs = refs

    def stack(self, group, order=range(REACH)):
        for ref in self.refs:
            held = ref.shape[1] // SUB
            if group < held:
                return stack_of(ref, group, order)
            group -= held

    def put(self, group, values):
        for ref in self.refs:
            held = ref.shape[1] // SUB
            if 0 <= group < held:
                for c, value in enumerate(values):
                    ref[c, rows_of(group), :] = value
            group -= held


def by_longitude(block, lat):
    return jnp.swapaxes(block.reshape(SUB, SUB, lat), 0, 1)


def stack_of(ref, group, order=range(REACH)):
    return [ref[c, rows_of(group), :] for c in order]


def odd_core():
    return lax.rem(lax.axis_index("tile"), 2) == 1


def from_outside(columns, odd):
    last = len(columns) - 1
    return [jnp.where(odd, columns[last - c], columns[c]) for c in range(len(columns))]


def low_half(shape):
    return lax.broadcasted_iota(jnp.int32, shape, 0) < SUB // 2


def spread_kernel(scaling_ref, inner_ref, *outer_refs):
    groups, lat = inner_ref.shape[1] // SUB, inner_ref.shape[2]
    odd = odd_core()
    outer = Chunked(outer_refs)
    for group in range(groups):
        columns = from_outside(by_longitude(scaling_ref[block_of(group), :], lat), odd)
        outer.put(group, columns[:REACH])
        for c in range(REACH):
            inner_ref[c, rows_of(group), :] = columns[c + REACH]


def lane_fold(value):
    lat = value.shape[-1]
    total = value[:, :128]
    for t in range(1, lat // 128):
        total = total + value[:, t * 128 : (t + 1) * 128]
    return total


def diffuse(columns, coef_ref):
    lat = columns[0].shape[-1]
    return [
        coef_ref[CENTER] * here
        + coef_ref[ZONAL] * (west + east)
        + coef_ref[NORTH] * pltpu.roll(here, lat - 1, 1)
        + coef_ref[SOUTH] * pltpu.roll(here, 1, 1)
        for west, here, east in zip(columns[:-2], columns[1:-1], columns[2:])
    ]


def unit(values, coef_ref):
    return values


def by_area(values, coef_ref):
    return [value * coef_ref[AREA] for value in values]


def inner_half(batch, halo_ref, inner_ref, outer_refs, coef_ref, edge_ref, weigh=unit):
    outer = Chunked(outer_refs)
    columns = [outer.stack(g) + stack_of(inner_ref, g) + stack_of(halo_ref, g, (3, 2, 1, 0)) for g in batch]
    columns = [weigh(own, coef_ref) for own in columns]
    for s in range(REACH):
        columns = [diffuse(own, coef_ref) for own in columns]
        if s < REACH - 1:
            for own, group in zip(columns, batch):
                edge_ref[2 * s, rows_of(group), :] = own[0]
                edge_ref[2 * s + 1, rows_of(group), :] = own[1]
    return zip(batch, columns)


def outer_half(batch, first, halo_ref, outer_ref, edge_ref, coef_ref, weigh=unit):
    columns = [stack_of(halo_ref, g - first, (3, 2, 1, 0)) + stack_of(outer_ref, g - first, (0, 1)) for g in batch]
    columns = [weigh(own, coef_ref) for own in columns]
    for s in range(REACH):
        columns = [diffuse(own, coef_ref) for own in columns]
        if s < REACH - 1:
            columns = [own + stack_of(edge_ref, g, (2 * s, 2 * s + 1)) for own, g in zip(columns, batch)]
    return zip(batch, columns)


def smooth_inner_kernel(
    halo_ref, inner_ref, fields_ref, mask_ref, count_ref, coef_ref, *refs
):
    *outer_refs, out_ref, edge_ref, filled_ref, mass_ref, weight_ref = refs
    groups, lat = inner_ref.shape[1] // SUB, inner_ref.shape[2]
    odd = odd_core()
    low = low_half((SUB, 128))
    for group in range(groups):
        first, second = (count_ref[2 * group + n].astype(jnp.float32) for n in range(2))
        weight_ref[rows_of(group), :] = jnp.where(low, first, second)
    count = sum(count_ref[m] for m in range(2 * groups)).astype(jnp.float32)
    weight_ref[rows_of(groups), :] = jnp.full((SUB, 128), count)
    for batch in batches(groups):
        for group, smoothed in inner_half(
            batch, halo_ref, inner_ref, outer_refs, coef_ref, edge_ref, by_area
        ):
            fields = by_longitude(fields_ref[block_of(group), :], lat)
            filled = []
            for c in range(2 * REACH):
                valid = jnp.broadcast_to(mask_ref[c : c + 1, :], (SUB, lat)) == 1
                filled.append((jnp.where(valid, fields[c], 0.0) + BACKGROUND) * coef_ref[AREA])
            mass_ref[rows_of(group), :] = lane_fold(sum(filled))
            filled = from_outside(filled, odd)
            for c in range(REACH):
                filled_ref[c, rows_of(group), :] = filled[c]
                out_ref[c, rows_of(group), :] = filled[c + REACH] / smoothed[c]


def smooth_outer_kernel(first, halo_ref, outer_ref, edge_ref, filled_ref, coef_ref, *out_refs):
    last = first + outer_ref.shape[1] // SUB
    out = Chunked(out_refs)
    for batch in batches(last, first):
        for group, smoothed in outer_half(batch, first, halo_ref, outer_ref, edge_ref, coef_ref, by_area):
            filled = stack_of(filled_ref, group)
            out.put(group - first, [top / bottom for top, bottom in zip(filled, smoothed)])


def add_logs(group, held, result, scaled, weight_ref, inverse_ref, total_ref):
    lat = total_ref.shape[2]
    weight = jnp.concatenate([weight_ref[rows_of(group), :]] * (lat // 128), axis=1)
    for c in range(REACH):
        inverse_ref[c, rows_of(held), :] = 1.0 / result[c]
        total_ref[c] = total_ref[c] + weight * jnp.log(scaled[c] * result[c])


def return_inner_kernel(halo_ref, inner_ref, scaled_ref, weight_ref, coef_ref, *refs):
    *outer_refs, inverse_ref, edge_ref, total_ref = refs
    groups = inner_ref.shape[1] // SUB
    total_ref[...] = jnp.zeros_like(total_ref)
    for batch in batches(groups):
        for group, result in inner_half(batch, halo_ref, inner_ref, outer_refs, coef_ref, edge_ref):
            add_logs(group, group, result, stack_of(scaled_ref, group), weight_ref, inverse_ref, total_ref)


def return_outer_kernel(
    base, first, halo_ref, outer_ref, edge_ref, scaled_ref, weight_ref, coef_ref, inverse_ref, total_ref
):
    last = first + outer_ref.shape[1] // SUB
    total_ref[...] = jnp.zeros_like(total_ref)
    for batch in batches(last, first):
        for group, result in outer_half(batch, first, halo_ref, outer_ref, edge_ref, coef_ref):
            scaled = stack_of(scaled_ref, group - base)
            add_logs(group, group - first, result, scaled, weight_ref, inverse_ref, total_ref)


def last_return_kernel(
    base,
    first,
    halo_ref,
    outer_ref,
    edge_ref,
    scaled_ref,
    weight_ref,
    coef_ref,
    inner_ref,
    *refs,
):
    *earlier_refs, inverse_ref, logs_ref, total_ref = refs
    return_outer_kernel(
        base, first, halo_ref, outer_ref, edge_ref, scaled_ref, weight_ref, coef_ref, inverse_ref, total_ref
    )
    low = low_half(total_ref.shape[1:])
    tiles = total_ref.shape[2] // 128
    for c in range(REACH):
        outer, inner = sum((ref[c] for ref in earlier_refs), total_ref[c]), inner_ref[c]
        outer = outer + pltpu.roll(outer, SUB // 2, 0)
        inner = inner + pltpu.roll(inner, SUB // 2, 0)
        both = jnp.where(low, outer, inner)
        for t in range(tiles):
            logs_ref[:, rows_of(c * tiles + t), :] = jnp.stack([both[:, t * 128 : (t + 1) * 128]] * 2)
    count = weight_ref[rows_of(weight_ref.shape[0] // SUB - 1), :]
    logs_ref[:, rows_of(REACH * tiles), :] = jnp.stack([count] * 2)


def merge_kernel(logs_ref, mass_ref, coef_ref, merged_ref, payload_ref):
    members, tiles = mass_ref.shape[0], merged_ref.shape[2] // 128
    both = lambda n: logs_ref[0, rows_of(n), :] + logs_ref[1, rows_of(n), :]
    scale = 1.0 / both(REACH * tiles)
    level = jnp.zeros((SUB, 128), jnp.float32)
    for c in range(REACH):
        for t in range(tiles):
            span = slice(t * 128, (t + 1) * 128)
            merged = jnp.exp(both(c * tiles + t) * scale)
            merged_ref[c, :, span] = merged
            level = level + merged * coef_ref[AREA, :, span]
    level = level + pltpu.roll(level, SUB // 2, 0)
    spare = jnp.zeros((128 - members - SUB, 128), jnp.float32)
    table = jnp.concatenate([mass_ref[...], level, spare], axis=0)
    row = jnp.sum(table.T, axis=0, keepdims=True)
    payload_ref[...] = jnp.broadcast_to(row[None], payload_ref.shape)


def finish_kernel(cells, got_ref, merged_ref, inner_ref, *refs):
    *outer_refs, bary_ref, updated_ref, field_ref, staged_ref, field_sem, sem = refs
    members, lat = inner_ref.shape[1:]
    groups = members // SUB
    odd = odd_core()
    total = jnp.sum(got_ref[...], axis=0)
    table = jnp.broadcast_to(total, (128, 128)).T
    level = table[members : members + SUB, :]
    low = low_half((SUB, lat))
    wide = lambda v: jnp.concatenate([v] * (lat // 128), axis=1)
    inverse = wide(cells / level)
    outer, inner = [], []
    for c in range(REACH):
        both = merged_ref[c] * inverse
        swapped = pltpu.roll(both, SUB // 2, 0)
        outer.append(jnp.where(low, both, swapped))
        inner.append(jnp.where(low, swapped, both))
    bary = from_outside(outer + inner, odd)
    field_ref[...] = jnp.swapaxes(jnp.stack(bary), 0, 1)[: SUB // 2]
    copies = [pltpu.make_async_copy(field_ref, bary_ref, field_sem)]
    copies[0].start()
    for group in range(groups):
        rows = slice(group * SUB, (group + 1) * SUB)
        factor = wide(table[rows, :] / cells)
        quotients = Chunked(outer_refs).stack(group) + stack_of(inner_ref, group)
        out = [b * factor * quotient for b, quotient in zip(bary, from_outside(quotients, odd))]
        span = block_of(group)
        staged_ref[span, :] = jnp.swapaxes(jnp.stack(out), 0, 1).reshape(SUB * SUB, lat)
        copies.append(pltpu.make_async_copy(staged_ref.at[span, :], updated_ref.at[span, :], sem.at[group]))
        copies[-1].start()
    for copy in copies:
        copy.wait()


def shape(*dims):
    return jax.ShapeDtypeStruct(dims, jnp.float32)


def call(kernel, outs, *args, scratch=(), out_specs=None):
    return pl.pallas_call(
        kernel,
        out_shape=outs,
        in_specs=[SMEM if arg.ndim == 1 else VMEM for arg in args],
        out_specs=out_specs or (VMEM,) * len(outs),
        scratch_shapes=scratch,
        compiler_params=params(),
    )(*args)


def body(fields, scaling, counts, land_mask):
    members, levels, lon, lat = fields.shape
    tiles = lax.axis_size("tile")
    rows = members * levels
    cells = lon * tiles * lat
    half = shape(REACH, rows, lat)
    edge = shape(2 * REACH - 2, rows, lat)
    packed = shape(REACH, SUB, lat)
    chunks = chunk_groups(rows // SUB)
    bases = [sum(map(sum, chunks[:n])) for n in range(len(chunks))]
    parts = [shape(REACH, sum(own) * SUB, lat) for own in chunks]
    coef = jnp.asarray(coefficients(lat))
    with_mate = [(i, i ^ 1) for i in range(tiles)]
    with_neighbour = [(i, (i + (1 if i % 2 else -1)) % tiles) for i in range(tiles)]
    scaling = scaling.reshape(rows * lon, lat)
    fields = fields.reshape(rows * lon, lat)

    inner, *outer = call(spread_kernel, (half, *parts), scaling)
    outer_halo = [lax.ppermute(part, "tile", with_neighbour) for part in outer]
    inner_halo = lax.ppermute(inner, "tile", with_mate)
    fields, inner = lax.optimization_barrier((fields, inner))
    v_inner, edges, filled, mass, weights = call(
        smooth_inner_kernel,
        (half, edge, half, shape(rows, 128), shape(rows + SUB, 128)),
        inner_halo,
        inner,
        fields,
        land_mask,
        counts,
        coef,
        *outer,
    )
    v_inner_halo = lax.ppermute(v_inner, "tile", with_mate)
    v_outer, v_outer_halo, places = [], [], []
    for base, sizes, halo, own in zip(bases, chunks, outer_halo, outer):
        outs = tuple(shape(REACH, size * SUB, lat) for size in sizes)
        values = call(partial(smooth_outer_kernel, base), outs, halo, own, edges, filled, coef)
        v_outer += values
        v_outer_halo += [lax.ppermute(value, "tile", with_neighbour) for value in values]
        places += [(base, base + sum(sizes[:n]), own) for n in range(len(sizes))]
    inverse_inner, edges, inner_logs = call(
        return_inner_kernel, (half, edge, packed), v_inner_halo, v_inner, inner, weights, coef, *v_outer
    )
    inverses, earlier = [inverse_inner], []
    for n, (base, first, own) in enumerate(places):
        if earlier:
            v_outer_halo[n], earlier[-1] = lax.optimization_barrier((v_outer_halo[n], earlier[-1]))
        operands = v_outer_halo[n], v_outer[n], edges, own, weights, coef
        part = shape(*v_outer[n].shape)
        if n < len(places) - 1:
            inverse, logs = call(partial(return_outer_kernel, base, first), (part, packed), *operands)
            earlier.append(logs)
        else:
            inverse, logs = call(
                partial(last_return_kernel, base, first),
                (part, shape(2, (REACH * lat // 128 + 1) * SUB, 128)),
                *operands,
                inner_logs,
                *earlier,
                scratch=[pltpu.VMEM((REACH, SUB, lat), jnp.float32)],
            )
        inverses.append(inverse)
    logs = lax.all_to_all(logs, "mem", split_axis=0, concat_axis=0)
    merged, payload = call(merge_kernel, (packed, shape(tiles, 1, 128)), logs, mass, coef)
    got = lax.all_to_all(payload, "tile", split_axis=0, concat_axis=0)
    barycenter, updated = call(
        partial(finish_kernel, float(cells)),
        (shape(levels, lon, lat), shape(rows * lon, lat)),
        got,
        merged,
        *inverses,
        scratch=[
            pltpu.VMEM((levels, lon, lat), jnp.float32),
            pltpu.VMEM((rows * lon, lat), jnp.float32),
            pltpu.SemaphoreType.DMA,
            pltpu.SemaphoreType.DMA((rows // SUB,)),
        ],
        out_specs=(HBM, HBM),
    )
    return barycenter, updated.reshape(members, levels, lon, lat)


def solution(mesh):
    return jax.shard_map(
        body,
        mesh=mesh,
        in_specs=(
            P("mem", None, "tile", None),
            P("mem", None, "tile", None),
            P("mem"),
            P("tile", None),
        ),
        out_specs=(P(None, "tile", None), P("mem", None, "tile", None)),
        check_vma=False,
    )
```

```python
import math
from functools import partial

import jax
import jax.numpy as jnp
import numpy as np
from jax import lax
from jax.experimental import pallas as pl
from jax.experimental.pallas import tpu as pltpu
from jax.sharding import PartitionSpec as P

BACKGROUND = 0.01
REACH = 4
SUB = 8
VMEM = pl.BlockSpec(memory_space=pltpu.VMEM)
SMEM = pl.BlockSpec(memory_space=pltpu.SMEM)
HBM = pl.BlockSpec(memory_space=pl.ANY)
AREA, ZONAL, NORTH, SOUTH, CENTER = range(5)


def coefficients(lat_cells):
    spacing = math.pi / lat_cells
    index = np.arange(lat_cells)
    latitude = -0.5 * math.pi + (index + 0.5) * spacing
    cell_area = np.cos(latitude)
    zonal = 0.2 * np.minimum(2.2, 1.0 / cell_area**2)
    north = np.where(index == lat_cells - 1, 0.0, 0.05 * np.cos(latitude + 0.5 * spacing) / cell_area)
    south = np.where(index == 0, 0.0, 0.05 * np.cos(latitude - 0.5 * spacing) / cell_area)
    center = 1.0 - 2.0 * zonal - north - south
    rows = np.stack([cell_area, zonal, north, south, center]).astype(np.float32)
    return np.ascontiguousarray(np.broadcast_to(rows[:, None, :], (5, SUB, lat_cells)))


def params(mib=12):
    return pltpu.CompilerParams(vmem_limit_bytes=mib * 2**20)


def rows_of(group):
    return pl.ds(group * SUB, SUB)


def block_of(group):
    return pl.ds(group * SUB * SUB, SUB * SUB)


def batches(last, first=0, size=4):
    return [range(start, min(start + size, last)) for start in range(first, last, size)]


def chunk_groups(groups):
    first = (groups + 1) // 2
    return [[first], [groups - first - 1, 1]]


class Chunked:
    def __init__(self, refs):
        self.refs = refs

    def stack(self, group, order=range(REACH)):
        for ref in self.refs:
            held = ref.shape[1] // SUB
            if group < held:
                return stack_of(ref, group, order)
            group -= held

    def put(self, group, values):
        for ref in self.refs:
            held = ref.shape[1] // SUB
            if 0 <= group < held:
                for c, value in enumerate(values):
                    ref[c, rows_of(group), :] = value
            group -= held


def by_longitude(block, lat):
    return jnp.swapaxes(block.reshape(SUB, SUB, lat), 0, 1)


def stack_of(ref, group, order=range(REACH)):
    return [ref[c, rows_of(group), :] for c in order]


def odd_core():
    return lax.rem(lax.axis_index("tile"), 2) == 1


def from_outside(columns, odd):
    last = len(columns) - 1
    return [jnp.where(odd, columns[last - c], columns[c]) for c in range(len(columns))]


def low_half(shape):
    return lax.broadcasted_iota(jnp.int32, shape, 0) < SUB // 2


def spread_kernel(scaling_ref, inner_ref, *outer_refs):
    groups, lat = inner_ref.shape[1] // SUB, inner_ref.shape[2]
    odd = odd_core()
    outer = Chunked(outer_refs)
    for group in range(groups):
        columns = from_outside(by_longitude(scaling_ref[block_of(group), :], lat), odd)
        outer.put(group, columns[:REACH])
        for c in range(REACH):
            inner_ref[c, rows_of(group), :] = columns[c + REACH]


def lane_fold(value):
    lat = value.shape[-1]
    total = value[:, :128]
    for t in range(1, lat // 128):
        total = total + value[:, t * 128 : (t + 1) * 128]
    return total


def diffuse(columns, coef_ref):
    lat = columns[0].shape[-1]
    return [
        coef_ref[CENTER] * here
        + coef_ref[ZONAL] * (west + east)
        + coef_ref[NORTH] * pltpu.roll(here, lat - 1, 1)
        + coef_ref[SOUTH] * pltpu.roll(here, 1, 1)
        for west, here, east in zip(columns[:-2], columns[1:-1], columns[2:])
    ]


def unit(values, coef_ref):
    return values


def by_area(values, coef_ref):
    return [value * coef_ref[AREA] for value in values]


def inner_half(batch, halo_ref, inner_ref, outer_refs, coef_ref, edge_ref, weigh=unit):
    outer = Chunked(outer_refs)
    columns = [outer.stack(g) + stack_of(inner_ref, g) + stack_of(halo_ref, g, (3, 2, 1, 0)) for g in batch]
    columns = [weigh(own, coef_ref) for own in columns]
    for s in range(REACH):
        columns = [diffuse(own, coef_ref) for own in columns]
        if s < REACH - 1:
            for own, group in zip(columns, batch):
                edge_ref[2 * s, rows_of(group), :] = own[0]
                edge_ref[2 * s + 1, rows_of(group), :] = own[1]
    return zip(batch, columns)


def outer_half(batch, first, halo_ref, outer_ref, edge_ref, coef_ref, weigh=unit):
    columns = [stack_of(halo_ref, g - first, (3, 2, 1, 0)) + stack_of(outer_ref, g - first, (0, 1)) for g in batch]
    columns = [weigh(own, coef_ref) for own in columns]
    for s in range(REACH):
        columns = [diffuse(own, coef_ref) for own in columns]
        if s < REACH - 1:
            columns = [own + stack_of(edge_ref, g, (2 * s, 2 * s + 1)) for own, g in zip(columns, batch)]
    return zip(batch, columns)


def smooth_inner_kernel(
    halo_ref, inner_ref, fields_ref, mask_ref, count_ref, coef_ref, *refs
):
    *outer_refs, out_ref, edge_ref, filled_ref, mass_ref, weight_ref = refs
    groups, lat = inner_ref.shape[1] // SUB, inner_ref.shape[2]
    odd = odd_core()
    low = low_half((SUB, 128))
    for group in range(groups):
        first, second = (count_ref[2 * group + n].astype(jnp.float32) for n in range(2))
        weight_ref[rows_of(group), :] = jnp.where(low, first, second)
    count = sum(count_ref[m] for m in range(2 * groups)).astype(jnp.float32)
    weight_ref[rows_of(groups), :] = jnp.full((SUB, 128), count)
    for batch in batches(groups):
        for group, smoothed in inner_half(
            batch, halo_ref, inner_ref, outer_refs, coef_ref, edge_ref, by_area
        ):
            fields = by_longitude(fields_ref[block_of(group), :], lat)
            filled = []
            for c in range(2 * REACH):
                valid = jnp.broadcast_to(mask_ref[c : c + 1, :], (SUB, lat)) == 1
                filled.append((jnp.where(valid, fields[c], 0.0) + BACKGROUND) * coef_ref[AREA])
            mass_ref[rows_of(group), :] = lane_fold(sum(filled))
            filled = from_outside(filled, odd)
            for c in range(REACH):
                filled_ref[c, rows_of(group), :] = filled[c]
                out_ref[c, rows_of(group), :] = filled[c + REACH] / smoothed[c]


def smooth_outer_kernel(first, halo_ref, outer_ref, edge_ref, filled_ref, coef_ref, *out_refs):
    last = first + outer_ref.shape[1] // SUB
    out = Chunked(out_refs)
    for batch in batches(last, first):
        for group, smoothed in outer_half(batch, first, halo_ref, outer_ref, edge_ref, coef_ref, by_area):
            filled = stack_of(filled_ref, group)
            out.put(group - first, [top / bottom for top, bottom in zip(filled, smoothed)])


def add_logs(group, held, result, scaled, weight_ref, inverse_ref, total_ref):
    lat = total_ref.shape[2]
    weight = jnp.concatenate([weight_ref[rows_of(group), :]] * (lat // 128), axis=1)
    for c in range(REACH):
        inverse_ref[c, rows_of(held), :] = 1.0 / result[c]
        total_ref[c] = total_ref[c] + weight * jnp.log(scaled[c] * result[c])


def return_inner_kernel(halo_ref, inner_ref, scaled_ref, weight_ref, coef_ref, *refs):
    *outer_refs, inverse_ref, edge_ref, total_ref = refs
    groups = inner_ref.shape[1] // SUB
    total_ref[...] = jnp.zeros_like(total_ref)
    for batch in batches(groups):
        for group, result in inner_half(batch, halo_ref, inner_ref, outer_refs, coef_ref, edge_ref):
            add_logs(group, group, result, stack_of(scaled_ref, group), weight_ref, inverse_ref, total_ref)


def return_outer_kernel(
    base, first, halo_ref, outer_ref, edge_ref, scaled_ref, weight_ref, coef_ref, inverse_ref, total_ref
):
    last = first + outer_ref.shape[1] // SUB
    total_ref[...] = jnp.zeros_like(total_ref)
    for batch in batches(last, first):
        for group, result in outer_half(batch, first, halo_ref, outer_ref, edge_ref, coef_ref):
            scaled = stack_of(scaled_ref, group - base)
            add_logs(group, group - first, result, scaled, weight_ref, inverse_ref, total_ref)


def last_return_kernel(
    base,
    first,
    halo_ref,
    outer_ref,
    edge_ref,
    scaled_ref,
    weight_ref,
    coef_ref,
    inner_ref,
    *refs,
):
    *earlier_refs, inverse_ref, logs_ref, total_ref = refs
    return_outer_kernel(
        base, first, halo_ref, outer_ref, edge_ref, scaled_ref, weight_ref, coef_ref, inverse_ref, total_ref
    )
    low = low_half(total_ref.shape[1:])
    tiles = total_ref.shape[2] // 128
    for c in range(REACH):
        outer, inner = sum((ref[c] for ref in earlier_refs), total_ref[c]), inner_ref[c]
        outer = outer + pltpu.roll(outer, SUB // 2, 0)
        inner = inner + pltpu.roll(inner, SUB // 2, 0)
        both = jnp.where(low, outer, inner)
        for t in range(tiles):
            logs_ref[rows_of(c * tiles + t), :] = both[:, t * 128 : (t + 1) * 128]
    logs_ref[rows_of(REACH * tiles), :] = weight_ref[rows_of(weight_ref.shape[0] // SUB - 1), :]


def merge_kernel(own_ref, other_ref, mass_ref, coef_ref, merged_ref, payload_ref):
    members, tiles = mass_ref.shape[0], merged_ref.shape[2] // 128
    both = lambda n: own_ref[rows_of(n), :] + other_ref[rows_of(n), :]
    scale = 1.0 / both(REACH * tiles)
    level = jnp.zeros((SUB, 128), jnp.float32)
    for c in range(REACH):
        for t in range(tiles):
            span = slice(t * 128, (t + 1) * 128)
            merged = jnp.exp(both(c * tiles + t) * scale)
            merged_ref[c, :, span] = merged
            level = level + merged * coef_ref[AREA, :, span]
    level = level + pltpu.roll(level, SUB // 2, 0)
    spare = jnp.zeros((128 - members - SUB, 128), jnp.float32)
    table = jnp.concatenate([mass_ref[...], level, spare], axis=0)
    row = jnp.sum(table.T, axis=0, keepdims=True)
    payload_ref[...] = jnp.broadcast_to(row[None], payload_ref.shape)


def finish_kernel(cells, got_ref, merged_ref, inner_ref, *refs):
    *outer_refs, bary_ref, updated_ref, field_ref, staged_ref, field_sem, sem = refs
    members, lat = inner_ref.shape[1:]
    groups = members // SUB
    odd = odd_core()
    total = jnp.sum(got_ref[...], axis=0)
    table = jnp.broadcast_to(total, (128, 128)).T
    level = table[members : members + SUB, :]
    low = low_half((SUB, lat))
    wide = lambda v: jnp.concatenate([v] * (lat // 128), axis=1)
    inverse = wide(cells / level)
    outer, inner = [], []
    for c in range(REACH):
        both = merged_ref[c] * inverse
        swapped = pltpu.roll(both, SUB // 2, 0)
        outer.append(jnp.where(low, both, swapped))
        inner.append(jnp.where(low, swapped, both))
    bary = from_outside(outer + inner, odd)
    field_ref[...] = jnp.swapaxes(jnp.stack(bary), 0, 1)[: SUB // 2]
    copies = [pltpu.make_async_copy(field_ref, bary_ref, field_sem)]
    copies[0].start()
    for group in range(groups):
        rows = slice(group * SUB, (group + 1) * SUB)
        factor = wide(table[rows, :] / cells)
        quotients = Chunked(outer_refs).stack(group) + stack_of(inner_ref, group)
        out = [b * factor * quotient for b, quotient in zip(bary, from_outside(quotients, odd))]
        span = block_of(group)
        staged_ref[span, :] = jnp.swapaxes(jnp.stack(out), 0, 1).reshape(SUB * SUB, lat)
        copies.append(pltpu.make_async_copy(staged_ref.at[span, :], updated_ref.at[span, :], sem.at[group]))
        copies[-1].start()
    for copy in copies:
        copy.wait()


def shape(*dims):
    return jax.ShapeDtypeStruct(dims, jnp.float32)


def call(kernel, outs, *args, scratch=(), out_specs=None):
    return pl.pallas_call(
        kernel,
        out_shape=outs,
        in_specs=[SMEM if arg.ndim == 1 else VMEM for arg in args],
        out_specs=out_specs or (VMEM,) * len(outs),
        scratch_shapes=scratch,
        compiler_params=params(),
    )(*args)


def body(fields, scaling, counts, land_mask):
    members, levels, lon, lat = fields.shape
    tiles = lax.axis_size("tile")
    rows = members * levels
    cells = lon * tiles * lat
    half = shape(REACH, rows, lat)
    edge = shape(2 * REACH - 2, rows, lat)
    packed = shape(REACH, SUB, lat)
    chunks = chunk_groups(rows // SUB)
    bases = [sum(map(sum, chunks[:n])) for n in range(len(chunks))]
    parts = [shape(REACH, sum(own) * SUB, lat) for own in chunks]
    coef = jnp.asarray(coefficients(lat))
    with_mate = [(i, i ^ 1) for i in range(tiles)]
    with_neighbour = [(i, (i + (1 if i % 2 else -1)) % tiles) for i in range(tiles)]
    scaling = scaling.reshape(rows * lon, lat)
    fields = fields.reshape(rows * lon, lat)

    inner, *outer = call(spread_kernel, (half, *parts), scaling)
    outer_halo = [lax.ppermute(part, "tile", with_neighbour) for part in outer]
    inner_halo = lax.ppermute(inner, "tile", with_mate)
    fields, inner = lax.optimization_barrier((fields, inner))
    v_inner, edges, filled, mass, weights = call(
        smooth_inner_kernel,
        (half, edge, half, shape(rows, 128), shape(rows + SUB, 128)),
        inner_halo,
        inner,
        fields,
        land_mask,
        counts,
        coef,
        *outer,
    )
    v_inner_halo = lax.ppermute(v_inner, "tile", with_mate)
    v_outer, v_outer_halo, places = [], [], []
    for base, sizes, halo, own in zip(bases, chunks, outer_halo, outer):
        outs = tuple(shape(REACH, size * SUB, lat) for size in sizes)
        values = call(partial(smooth_outer_kernel, base), outs, halo, own, edges, filled, coef)
        v_outer += values
        v_outer_halo += [lax.ppermute(value, "tile", with_neighbour) for value in values]
        places += [(base, base + sum(sizes[:n]), own) for n in range(len(sizes))]
    inverse_inner, edges, inner_logs = call(
        return_inner_kernel, (half, edge, packed), v_inner_halo, v_inner, inner, weights, coef, *v_outer
    )
    inverses, earlier = [inverse_inner], []
    for n, (base, first, own) in enumerate(places):
        if earlier:
            v_outer_halo[n], earlier[-1] = lax.optimization_barrier((v_outer_halo[n], earlier[-1]))
        operands = v_outer_halo[n], v_outer[n], edges, own, weights, coef
        part = shape(*v_outer[n].shape)
        if n < len(places) - 1:
            inverse, logs = call(partial(return_outer_kernel, base, first), (part, packed), *operands)
            earlier.append(logs)
        else:
            inverse, logs = call(
                partial(last_return_kernel, base, first),
                (part, shape((REACH * lat // 128 + 1) * SUB, 128)),
                *operands,
                inner_logs,
                *earlier,
                scratch=[pltpu.VMEM((REACH, SUB, lat), jnp.float32)],
            )
        inverses.append(inverse)
    other = lax.ppermute(logs, "mem", [(0, 1), (1, 0)])
    merged, payload = call(merge_kernel, (packed, shape(tiles, 1, 128)), logs, other, mass, coef)
    got = lax.all_to_all(payload, "tile", split_axis=0, concat_axis=0)
    barycenter, updated = call(
        partial(finish_kernel, float(cells)),
        (shape(levels, lon, lat), shape(rows * lon, lat)),
        got,
        merged,
        *inverses,
        scratch=[
            pltpu.VMEM((levels, lon, lat), jnp.float32),
            pltpu.VMEM((rows * lon, lat), jnp.float32),
            pltpu.SemaphoreType.DMA,
            pltpu.SemaphoreType.DMA((rows // SUB,)),
        ],
        out_specs=(HBM, HBM),
    )
    return barycenter, updated.reshape(members, levels, lon, lat)


def solution(mesh):
    return jax.shard_map(
        body,
        mesh=mesh,
        in_specs=(
            P("mem", None, "tile", None),
            P("mem", None, "tile", None),
            P("mem"),
            P("tile", None),
        ),
        out_specs=(P(None, "tile", None), P("mem", None, "tile", None)),
        check_vma=False,
    )
```
